32 devices in a mesh: dp: 16 (over z, y, core), shard: 2 (over x).
Axes of the slice: x: 2, y: 2, z: 4, core: 2. Of those that a mesh axis runs over, the one named last changes fastest.
Arguments:
- tokens: bfloat16 [64, 2, 502, 768], P(('dp', 'shard')), may hold values from -6 to 6
- segment_count: int32 [64], P(('dp', 'shard')), may hold values from 1 to 2, as said below
- memory_init: bfloat16 [768, 10], P(('dp', 'shard')), may hold values from -6 to 6
- query_weight: bfloat16 [768, 768], P(('dp', 'shard')), may hold values from -0.21875 to 0.21875
- key_weight: bfloat16 [768, 768], P(('dp', 'shard')), may hold values from -0.21875 to 0.21875
- value_weight: bfloat16 [768, 768], P(('dp', 'shard')), may hold values from -0.21875 to 0.21875
- output_weight: bfloat16 [768, 768], P(('dp', 'shard')), may hold values from -1.75 to 1.75
- up_weight: bfloat16 [768, 3072], P(('dp', 'shard')), may hold values from -0.21875 to 0.21875
- down_weight: bfloat16 [3072, 768], P(('dp', 'shard')), may hold values from -0.109375 to 0.109375
- query_bias: bfloat16 [768], P(('dp', 'shard')), may hold values from -2 to 2
- value_bias: bfloat16 [768], P(('dp', 'shard')), may hold values from -2 to 2
- output_bias: bfloat16 [768], P(('dp', 'shard')), may hold values from -2 to 2
- up_bias: bfloat16 [3072], P(('dp', 'shard')), may hold values from -2 to 2
- down_bias: bfloat16 [768], P(('dp', 'shard')), may hold values from -2 to 2
- first_gain: bfloat16 [768], P(('dp', 'shard')), may hold values from 0.5 to 1.5
- first_shift: bfloat16 [768], P(('dp', 'shard')), may hold values from -2 to 2
- second_gain: bfloat16 [768], P(('dp', 'shard')), may hold values from 0.5 to 1.5
- second_shift: bfloat16 [768], P(('dp', 'shard')), may hold values from -2 to 2
- output_cotangent: bfloat16 [64, 2, 502, 768], P(('dp', 'shard')), may hold values from -6 to 6
- memory_cotangent: bfloat16 [64, 10, 768], P(('dp', 'shard')), may hold values from -6 to 6
Outputs:
- layer_output: bfloat16 [64, 2, 502, 768], P(('dp', 'shard'))
- memory_final: bfloat16 [64, 10, 768], P(('dp', 'shard'))
- token_gradient: bfloat16 [64, 2, 502, 768], P(('dp', 'shard'))
- memory_init_gradient: float32 [768, 10], P(('dp', 'shard'))
- query_weight_gradient: float32 [768, 768], P(('dp', 'shard'))
- key_weight_gradient: float32 [768, 768], P(('dp', 'shard'))
- value_weight_gradient: float32 [768, 768], P(('dp', 'shard'))
- output_weight_gradient: float32 [768, 768], P(('dp', 'shard'))
- up_weight_gradient: float32 [768, 3072], P(('dp', 'shard'))
- down_weight_gradient: float32 [3072, 768], P(('dp', 'shard'))
- query_bias_gradient: float32 [768], P(('dp', 'shard'))
- value_bias_gradient: float32 [768], P(('dp', 'shard'))
- output_bias_gradient: float32 [768], P(('dp', 'shard'))
- up_bias_gradient: float32 [3072], P(('dp', 'shard'))
- down_bias_gradient: float32 [768], P(('dp', 'shard'))
- first_gain_gradient: float32 [768], P(('dp', 'shard'))
- first_shift_gradient: float32 [768], P(('dp', 'shard'))
- second_gain_gradient: float32 [768], P(('dp', 'shard'))
- second_shift_gradient: float32 [768], P(('dp', 'shard'))
The draws below stay inside these ranges and needn't reach their ends.
Inputs may be any that keep to these rules, and one draw needn't show every extreme that they name: `segment_count`: segments of each item; item 0 has 2 and item 1 has one.
All inputs are finite; a program needn't handle non-finite values.
Results may differ from the reference program's by a relative error of at most 0.019.
Values may be sent and summed in bfloat16 or wider, within the bound.
No kernel may reach another device: no remote copies, remote signals or barrier semaphores. Data moves between devices by JAX's collectives and lax.ppermute only.
A program may use at most 320 MiB of HBM per device.

```python
import jax
import jax.numpy as jnp
from jax import lax

D = 768
FF = 3072
HEADS = 12
HEAD_DIM = 64
MEM = 10
SEG_TOK = 502
SEGS = 2
ITEMS = 64


def draw_segment_count(key, part):
    counts = jax.random.randint(key, (ITEMS,), 1, SEGS + 1)
    return counts.at[0].set(SEGS).at[1].set(1).astype(jnp.int32)


def steps_of(own_key, extent, shards, least, top_value):
    level = 1.0
    for position, shards_of in shards:
        heights = jax.random.uniform(jax.random.fold_in(jax.random.fold_in(own_key, 6), position), (shards_of,), jnp.float32, least / len(shards), top_value / len(shards))
        level = level * jnp.repeat(jnp.exp(heights), extent[position] // shards_of).reshape((-1,) + (1,) * (len(extent) - 1 - position))
    return level


def normal_values(key, dims, deviation, reach, shards=(), held_as=jnp.bfloat16):
    level = steps_of(key, dims, shards, -0.22, 0.18) if shards else 1.0
    array = jax.random.normal(key, dims, jnp.float32) * deviation * level
    return jnp.minimum(jnp.maximum(array, -reach), reach).astype(held_as)


def setup_inputs(seed: int = 0) -> dict:
    seeds = jax.random.split(jax.random.key(seed), 21)
    return {
        "tokens": normal_values(seeds[0], (ITEMS, SEGS, SEG_TOK, D), 1.0, 6.0, ((0, 32),)),
        "segment_count": draw_segment_count(jax.random.fold_in(seeds[20], 71), 0),
        "memory_init": normal_values(seeds[2], (D, MEM), 1.0, 6.0, ((0, 32),)),
        "query_weight": normal_values(seeds[3], (D, D), D ** -0.5, 0.21875, ((0, 32),)),
        "key_weight": normal_values(seeds[4], (D, D), D ** -0.5, 0.21875, ((0, 32),)),
        "value_weight": normal_values(seeds[5], (D, D), D ** -0.5, 0.21875, ((0, 32),)),
        "output_weight": normal_values(seeds[6], (D, D), (D // 64) ** -0.5, 1.75, ((0, 32),)),
        "up_weight": normal_values(seeds[7], (D, FF), D ** -0.5, 0.21875, ((0, 32),)),
        "down_weight": normal_values(seeds[8], (FF, D), FF ** -0.5, 0.109375, ((0, 32),)),
        "query_bias": normal_values(seeds[9], (D,), 0.3, 2.0, ((0, 32),)),
        "value_bias": normal_values(seeds[10], (D,), 0.3, 2.0, ((0, 32),)),
        "output_bias": normal_values(seeds[11], (D,), 0.3, 2.0, ((0, 32),)),
        "up_bias": normal_values(seeds[12], (FF,), 0.3, 2.0, ((0, 32),)),
        "down_bias": normal_values(seeds[13], (D,), 0.3, 2.0, ((0, 32),)),
        "first_gain": jnp.clip(1.0 + 0.1 * jax.random.normal(seeds[14], (D,), jnp.float32), 0.5, 1.5).astype(jnp.bfloat16),
        "first_shift": normal_values(seeds[15], (D,), 0.3, 2.0, ((0, 32),)),
        "second_gain": jnp.clip(1.0 + 0.1 * jax.random.normal(seeds[16], (D,), jnp.float32), 0.5, 1.5).astype(jnp.bfloat16),
        "second_shift": normal_values(seeds[17], (D,), 0.3, 2.0, ((0, 32),)),
        "output_cotangent": normal_values(seeds[18], (ITEMS, SEGS, SEG_TOK, D), 1.0, 6.0, ((0, 32),)),
        "memory_cotangent": normal_values(seeds[19], (ITEMS, MEM, D), 1.0, 6.0, ((0, 32),)),
    }


@jax.custom_vjp
def low(v):
    return lax.optimization_barrier(v.astype(jnp.bfloat16)).astype(jnp.float32)

@jax.custom_vjp
def low_back(v):
    return v

def low_keep(v):
    return (low(v), None)

def low_pass(kept, grad):
    return (grad,)

def back_keep(v):
    return (v, None)

def back_low(kept, grad):
    return (low(grad),)
low.defvjp(low_keep, low_pass)
low_back.defvjp(back_keep, back_low)
norm_eps = 1e-06
root_half = 0.7071067811865476

def layer_norm(resid, gain, shift):
    center = resid - lax.optimization_barrier(jnp.mean(resid, axis=-1, keepdims=True))
    spread = lax.optimization_barrier(jnp.mean(center * center, axis=-1, keepdims=True))
    return center * lax.rsqrt(spread + norm_eps) * gain + shift

def matmul(left, right):
    return jnp.dot(left, right, precision=lax.Precision.HIGHEST, preferred_element_type=jnp.float32)

def segment_forward(inputs, params):
    query_weight, key_weight, value_weight, output_weight, up_weight, down_weight, query_bias, value_bias, output_bias, up_bias, down_bias, first_gain, first_shift, second_gain, second_shift = params
    length = inputs.shape[0]
    inputs_low = low(inputs)
    queries = low(low_back(matmul(inputs_low, query_weight) + query_bias)).reshape(length, HEADS, HEAD_DIM)
    key_rows = low(low_back(matmul(inputs_low, key_weight))).reshape(length, HEADS, HEAD_DIM)
    value_rows = low(low_back(matmul(inputs_low, value_weight) + value_bias)).reshape(length, HEADS, HEAD_DIM)
    scores = low_back(jnp.einsum('qhd,khd->hqk', queries, key_rows, precision=lax.Precision.HIGHEST) * 0.125)
    highest = lax.optimization_barrier(jnp.max(scores, axis=-1, keepdims=True))
    exponent = jnp.exp(scores - highest)
    attention = low(exponent / lax.optimization_barrier(jnp.sum(exponent, axis=-1, keepdims=True)))
    mixed_rows = jnp.einsum('hqk,khd->qhd', attention, value_rows, precision=lax.Precision.HIGHEST).reshape(length, D)
    mixed_rows = low(low_back(mixed_rows))
    branch = low_back(matmul(mixed_rows, output_weight) + output_bias)
    hidden = layer_norm(inputs + branch, first_gain, first_shift)
    up_value = low_back(matmul(low(hidden), up_weight) + up_bias)
    activated = low(0.5 * up_value * (1.0 + jax.scipy.special.erf(up_value * root_half)))
    feed = low_back(matmul(activated, down_weight) + down_bias)
    return layer_norm(hidden + feed, second_gain, second_shift)

def item_forward(token_rows, memory_cols, params, limit):
    memory = memory_cols.T
    produced = []
    for segment in range(SEGS):
        inputs = jnp.concatenate([memory, token_rows[segment], memory], axis=0)
        result = segment_forward(inputs, params)
        active = limit > segment
        produced.append(jnp.where(active, result[MEM:MEM + SEG_TOK], 0.0))
        memory = jnp.where(active, result[MEM + SEG_TOK:], memory)
    return (jnp.stack(produced), memory)

def reference(tokens, segment_count, memory_init, query_weight, key_weight, value_weight, output_weight, up_weight, down_weight, query_bias, value_bias, output_bias, up_bias, down_bias, first_gain, first_shift, second_gain, second_shift, output_cotangent, memory_cotangent):
    params = tuple((piece.astype(jnp.float32) for piece in (query_weight, key_weight, value_weight, output_weight, up_weight, down_weight, query_bias, value_bias, output_bias, up_bias, down_bias, first_gain, first_shift, second_gain, second_shift)))
    memory_cols = memory_init.astype(jnp.float32)
    initial = jax.tree.map(jnp.zeros_like, (memory_cols, params))

    def step(carry, member):
        token_rows, limit, token_cot, memory_cot = member

        def forward(rows_in, cols_in, params_in):
            return item_forward(rows_in, cols_in, params_in, limit)
        (produced, memory), backward = jax.vjp(forward, token_rows.astype(jnp.float32), memory_cols, params)
        token_grad, memory_grad, params_grad = backward((token_cot.astype(jnp.float32), memory_cot.astype(jnp.float32)))
        carry = jax.tree.map(jnp.add, carry, (memory_grad, params_grad))
        return (carry, (produced.astype(jnp.bfloat16), memory.astype(jnp.bfloat16), token_grad.astype(jnp.bfloat16)))
    (memory_total, param_total), (outputs, memories, token_grads) = lax.scan(step, initial, (tokens, segment_count, output_cotangent, memory_cotangent))
    return (outputs, memories, token_grads, memory_total, param_total[0], param_total[1], param_total[2], param_total[3], param_total[4], param_total[5], param_total[6], param_total[7], param_total[8], param_total[9], param_total[10], param_total[11], param_total[12], param_total[13], param_total[14])
```

```python
import functools

import jax
import jax.numpy as jnp
from jax import lax
from jax.experimental import pallas as pl
from jax.experimental.pallas import tpu as pltpu
from jax.sharding import PartitionSpec as P

F32 = jnp.float32
BF16 = jnp.bfloat16
HEADS = 12
HEAD_DIM = 64
NORM_EPS = 1e-06
ROOT_HALF = 0.7071067811865476
ROOT_TWO_PI = 0.3989422804014327
VMEM_BYTES = 60 << 20


def dot_nn(left, right):
    return jnp.dot(left, right, preferred_element_type=F32)


def dot_nt(left, right):
    return lax.dot_general(left, right, (((1,), (1,)), ((), ())), preferred_element_type=F32)


def dot_tn(left, right):
    return lax.dot_general(left, right, (((0,), (0,)), ((), ())), preferred_element_type=F32)


def lane_masks(rows):
    lane = lax.broadcasted_iota(jnp.int32, (rows, 128), 1)
    first = jnp.where(lane < HEAD_DIM, 1.0, 0.0)
    return first, 1.0 - first


def key_counts(rows, tokens):
    row = lax.broadcasted_iota(jnp.int32, (rows, 128), 0)
    return jnp.where(row < tokens, 1.0, 2.0)


def gelu_parts(u):
    bell = jnp.exp(u * u * -0.5)
    t = pl.reciprocal(1.0 + (0.3275911 * ROOT_HALF) * jnp.abs(u))
    poly = t * (
        0.5 * 0.254829592
        + t * (0.5 * -0.284496736 + t * (0.5 * 1.421413741 + t * (0.5 * -1.453152027 + t * (0.5 * 1.061405429))))
    )
    tail = poly * bell
    cdf = jnp.where(u < 0.0, tail, 1.0 - tail)
    return u * cdf, cdf + u * bell * ROOT_TWO_PI


def attend_forward(tok, mem, wq, wk, wv, bq, bv, x_o, q_o, k_o, v_o, e_o, o_o, li_o):
    seg = tok.shape[2]
    rows = x_o.shape[1]
    x_o[0, rows - 16 :, :] = mem[0].astype(BF16)
    x_o[0, :seg, :] = tok[0, 0]
    x = x_o[0]
    q_o[0] = ((dot_nn(x, wq[...]) + bq[...]).astype(BF16).astype(F32) * 0.125).astype(BF16)
    k_o[0] = dot_nn(x, wk[...]).astype(BF16)
    v_o[0] = (dot_nn(x, wv[...]) + bv[...]).astype(BF16)
    masks = lane_masks(rows)
    count = key_counts(rows, seg)
    low_masks = tuple(m.astype(BF16) for m in masks)

    def pair(p, carry):
        at = pl.ds(pl.multiple_of(p * 128, 128), 128)
        q2 = q_o[0, :, at]
        k2 = k_o[0, :, at]
        v2 = v_o[0, :, at].astype(F32) * count
        total = None
        for h in range(2):
            s = dot_nt(q2 * low_masks[h], k2)
            e = jnp.exp(s - jnp.max(s, axis=-1, keepdims=True)).astype(BF16)
            e_o[0, 2 * p + h] = e
            right = jnp.concatenate(
                [(v2 * masks[h]).astype(BF16), (count * masks[h]).astype(BF16)], axis=1
            )
            part = dot_nn(e, right)
            total = part if total is None else total + part
        inv = 1.0 / total[:, 128:]
        li_o[0, :, at] = inv
        o_o[0, :, at] = (total[:, :128] * inv).astype(BF16)
        return carry

    lax.fori_loop(0, HEADS // 2, pair, 0)


def norm_rows(r):
    mean = jnp.mean(r, axis=-1, keepdims=True)
    center = r - mean
    var = jnp.mean(center * center, axis=-1, keepdims=True)
    scale = lax.rsqrt(var + NORM_EPS)
    return center * scale, scale


def feed_forward(
    segment, step,
    count, tok, mem, o, wo, wup, wdown, bo, g1, s1, bup, bdown, g2, s2,
    y_o, mem_o, xh1_o, sc1_o, h_o, a_o, gp_o, xh2_o, sc2_o, x_s,
):
    seg = tok.shape[2]
    rows = o.shape[1]
    ff = wup.shape[1]
    x_s[rows - 16 :, :] = mem[0]
    x_s[:seg, :] = tok[0, 0].astype(F32)
    xh, sc = norm_rows(x_s[...] + dot_nn(o[0], wo[...]) + bo[...])
    xh1_o[0] = xh.astype(BF16)
    sc1_o[0] = jnp.broadcast_to(sc, (rows, 128))
    h1 = xh * g1[...] + s1[...]
    h_o[0] = h1.astype(BF16)
    x_s[...] = h1 + bdown[...]

    def chunk(j, carry):
        at = pl.ds(pl.multiple_of(j * step, step), step)
        act, slope = gelu_parts(dot_nn(h_o[0], wup[:, at]) + bup[:, at])
        a_o[0, :, at] = act.astype(BF16)
        gp_o[0, :, at] = slope.astype(BF16)
        x_s[...] += dot_nn(a_o[0, :, at], wdown[at, :])
        return carry

    lax.fori_loop(0, ff // step, chunk, 0)
    xh, sc = norm_rows(x_s[...])
    xh2_o[0] = xh.astype(BF16)
    sc2_o[0] = jnp.broadcast_to(sc, (rows, 128))
    x_s[...] = xh * g2[...] + s2[...]
    active = count[pl.program_id(0)] > segment
    y_o[0] = jnp.where(active, x_s[:seg, :], 0.0).astype(BF16)
    mem_o[0] = jnp.where(active, x_s[rows - 16 :, :], mem[0])


def norm_back(dy, xh, sc, gain):
    dxh = dy * gain
    m1 = jnp.mean(dxh, axis=-1, keepdims=True)
    m2 = jnp.mean(dxh * xh, axis=-1, keepdims=True)
    return sc * (dxh - m1 - xh * m2)


def col_sum(x):
    return jnp.sum(x, axis=0, keepdims=True)


def feed_backward(
    segment, step,
    count, cot, dmem, xh2, sc2, gp, xh1, sc1, wup, wdown, g1, g2,
    df_o, du_o, dr_o, db_o, vec_o, vup_o, x_s,
):
    seg = cot.shape[2]
    rows = xh2.shape[1]
    ff = wup.shape[1]
    active = jnp.where(count[pl.program_id(0)] > segment, 1.0, 0.0)
    x_s[rows - 16 :, :] = dmem[0] * active
    x_s[:seg, :] = cot[0, 0].astype(F32) * active
    dy = x_s[...]
    xh = xh2[0].astype(F32)
    vec_o[0, 2:3, :] = col_sum(dy * xh)
    vec_o[0, 3:4, :] = col_sum(dy)
    dr = norm_back(dy, xh, sc2[0, :, :1], g2[...])
    df = dr.astype(BF16)
    df_o[0] = df
    vec_o[0, 4:5, :] = col_sum(df.astype(F32))
    x_s[...] = dr

    def chunk(j, carry):
        at = pl.ds(pl.multiple_of(j * step, step), step)
        du = dot_nt(df_o[0], wdown[at, :]) * gp[0, :, at].astype(F32)
        vup_o[0, :, at] = col_sum(du)
        du_o[0, :, at] = du.astype(BF16)
        x_s[...] += dot_nt(du_o[0, :, at], wup[:, at])
        return carry

    lax.fori_loop(0, ff // step, chunk, 0)
    dh = x_s[...]
    xh = xh1[0].astype(F32)
    vec_o[0, 0:1, :] = col_sum(dh * xh)
    vec_o[0, 1:2, :] = col_sum(dh)
    dr = norm_back(dh, xh, sc1[0, :, :1], g1[...])
    dr_o[0] = dr
    db_o[0] = dr.astype(BF16)
    vec_o[0, 5:6, :] = col_sum(dr)


def attend_backward(
    segment,
    count, dmem, dr, db, q, k, v, e, o, li, wo, wq, wk, wv,
    tg_o, dmem_o, dq_o, dk_o, dv_o, vec_o, do_s, x_s,
):
    seg = tg_o.shape[1]
    rows = q.shape[1]
    do_s[...] = dot_nt(db[0], wo[...]).astype(BF16)
    masks = lane_masks(rows)
    count2 = key_counts(rows, seg)
    low_masks = tuple(m.astype(BF16) for m in masks)
    ones = jnp.ones((rows, 128), BF16)

    def pair(p, carry):
        at = pl.ds(pl.multiple_of(p * 128, 128), 128)
        dop = do_s[:, at].astype(F32) * li[0, :, at]
        pr = (dop * o[0, :, at].astype(F32) * -1.0).astype(BF16)
        dop = dop.astype(BF16)
        q2 = q[0, :, at]
        k2 = (k[0, :, at].astype(F32) * (count2 * 0.125)).astype(BF16)
        right = jnp.concatenate([v[0, :, at], ones], axis=1)
        dq = dk = dv = None
        for h in range(2):
            e_h = e[0, 2 * p + h]
            d_h = dop * low_masks[h]
            left = jnp.concatenate([d_h, pr * low_masks[h]], axis=1)
            ds = (e_h.astype(F32) * dot_nt(left, right)).astype(BF16)
            q_t = dot_nn(ds, k2 * low_masks[h])
            k_t = dot_tn(ds, q2 * low_masks[h])
            v_t = dot_tn(e_h, d_h)
            dq = q_t if dq is None else dq + q_t
            dk = k_t if dk is None else dk + k_t
            dv = v_t if dv is None else dv + v_t
        dq_o[0, :, at] = dq.astype(BF16)
        dk_o[0, :, at] = (dk * count2).astype(BF16)
        dv_o[0, :, at] = (dv * count2).astype(BF16)
        return carry

    lax.fori_loop(0, HEADS // 2, pair, 0)
    vec_o[0, 0:1, :] = col_sum(dq_o[0].astype(F32))
    vec_o[0, 1:2, :] = col_sum(dv_o[0].astype(F32))
    x_s[...] = (
        dr[0]
        + dot_nt(dq_o[0], wq[...])
        + dot_nt(dk_o[0], wk[...])
        + dot_nt(dv_o[0], wv[...])
    )
    tg_o[0] = x_s[:seg, :].astype(BF16)
    kept = jnp.where(count[pl.program_id(0)] > segment, 0.0, 1.0)
    dmem_o[0] = dmem[0] * kept + x_s[rows - 16 :, :]


def weight_product(parts, *refs):
    lefts = refs[:parts]
    rights = refs[parts : 2 * parts]
    out = refs[2 * parts]
    total = None
    for left, right in zip(lefts, rights):
        for i in range(left.shape[0]):
            term = dot_tn(left[i], right[i])
            total = term if total is None else total + term
    out[...] = total.astype(out.dtype)


def whole(array):
    dims = array.shape
    return pl.BlockSpec(dims, lambda *g: (0,) * len(dims), pipeline_mode=pl.Buffered(1))


def per_item(dims):
    return pl.BlockSpec((1,) + dims, lambda i: (i,) + (0,) * len(dims))


def out_of(items, dims, dtype):
    return jax.ShapeDtypeStruct((items,) + dims, dtype)


SCALARS = pl.BlockSpec(memory_space=pltpu.SMEM)


def params(**more):
    return pltpu.CompilerParams(vmem_limit_bytes=VMEM_BYTES, **more)


def call_attend_forward(segment, tokens, mem, wq, wk, wv, bq, bv):
    items, _, seg, width = tokens.shape
    rows = seg + 10
    tok = pl.BlockSpec((1, 1, seg, width), lambda i: (i, segment, 0, 0))
    outs = [((rows, width), BF16)] * 4 + [((HEADS, rows, rows), BF16), ((rows, width), BF16), ((rows, width), F32)]
    return pl.pallas_call(
        attend_forward,
        grid=(items,),
        in_specs=[tok, per_item((16, width)), whole(wq), whole(wk), whole(wv), whole(bq), whole(bv)],
        out_specs=[per_item(d) for d, t in outs],
        out_shape=[out_of(items, d, t) for d, t in outs],
        compiler_params=params(),
        cost_estimate=pl.CostEstimate(flops=items * 2 * rows * (3 * width * width + 8 * rows * width), bytes_accessed=items * rows * (width * 14 + HEADS * rows * 2), transcendentals=0),
        name="attend_forward",
    )(tokens, mem, wq, wk, wv, bq, bv)


def call_feed_forward(segment, count, tokens, mem, o, wo, wup, wdown, bo, g1, s1, bup, bdown, g2, s2):
    items, _, seg, width = tokens.shape
    rows = o.shape[1]
    ff = wup.shape[1]
    tok = pl.BlockSpec((1, 1, seg, width), lambda i: (i, segment, 0, 0))
    outs = [
        ((seg, width), BF16), ((16, width), F32), ((rows, width), BF16), ((rows, 128), F32), ((rows, width), BF16),
        ((rows, ff), BF16), ((rows, ff), BF16), ((rows, width), BF16), ((rows, 128), F32),
    ]
    fixed = (wo, wup, wdown, bo, g1, s1, bup, bdown, g2, s2)
    return pl.pallas_call(
        functools.partial(feed_forward, segment, 768),
        grid=(items,),
        in_specs=[SCALARS, tok, per_item((16, width)), per_item((rows, width))] + [whole(w) for w in fixed],
        out_specs=[per_item(d) for d, t in outs],
        out_shape=[out_of(items, d, t) for d, t in outs],
        scratch_shapes=[pltpu.VMEM((rows, width), F32)],
        compiler_params=params(),
        cost_estimate=pl.CostEstimate(flops=items * 2 * rows * width * (width + 2 * ff), bytes_accessed=items * rows * (width * 14 + ff * 4), transcendentals=0),
        name="feed_forward",
    )(count, tokens, mem, o, *fixed)


def call_feed_backward(segment, count, cot, dmem, xh2, sc2, gp, xh1, sc1, wup, wdown, g1, g2):
    items, _, seg, width = cot.shape
    rows = xh2.shape[1]
    ff = wup.shape[1]
    tok = pl.BlockSpec((1, 1, seg, width), lambda i: (i, segment, 0, 0))
    outs = [((rows, width), BF16), ((rows, ff), BF16), ((rows, width), F32), ((rows, width), BF16), ((8, width), F32), ((1, ff), F32)]
    fixed = (wup, wdown, g1, g2)
    return pl.pallas_call(
        functools.partial(feed_backward, segment, 768),
        grid=(items,),
        in_specs=[SCALARS, tok] + [per_item(a.shape[1:]) for a in (dmem, xh2, sc2, gp, xh1, sc1)] + [whole(w) for w in fixed],
        out_specs=[per_item(d) for d, t in outs],
        out_shape=[out_of(items, d, t) for d, t in outs],
        scratch_shapes=[pltpu.VMEM((rows, width), F32)],
        compiler_params=params(),
        cost_estimate=pl.CostEstimate(flops=items * 4 * rows * width * ff, bytes_accessed=items * rows * (width * 14 + ff * 4), transcendentals=0),
        name="feed_backward",
    )(count, cot, dmem, xh2, sc2, gp, xh1, sc1, *fixed)


def call_attend_backward(segment, seg, count, dmem, dr, db, q, k, v, e, o, li, wo, wq, wk, wv):
    items, rows, width = q.shape
    outs = [((seg, width), BF16), ((16, width), F32)] + [((rows, width), BF16)] * 3 + [((8, width), F32)]
    fixed = (wo, wq, wk, wv)
    return pl.pallas_call(
        functools.partial(attend_backward, segment),
        grid=(items,),
        in_specs=[SCALARS] + [per_item(a.shape[1:]) for a in (dmem, dr, db, q, k, v, e, o, li)] + [whole(w) for w in fixed],
        out_specs=[per_item(d) for d, t in outs],
        out_shape=[out_of(items, d, t) for d, t in outs],
        scratch_shapes=[pltpu.VMEM((rows, width), BF16), pltpu.VMEM((rows, width), F32)],
        compiler_params=params(),
        cost_estimate=pl.CostEstimate(flops=items * 2 * rows * width * (4 * width + 16 * rows), bytes_accessed=items * rows * (width * 24 + HEADS * rows * 2), transcendentals=0),
        name="attend_backward",
    )(count, dmem, dr, db, q, k, v, e, o, li, *fixed)


def call_weight_product(lefts, rights, step_left, step_right, dtype):
    parts = len(lefts)
    items, rows, n_left = lefts[0].shape
    n_right = rights[0].shape[2]
    left_spec = pl.BlockSpec((items, rows, step_left), lambda i, j: (0, 0, i))
    right_spec = pl.BlockSpec((items, rows, step_right), lambda i, j: (0, 0, j))
    return pl.pallas_call(
        functools.partial(weight_product, parts),
        grid=(n_left // step_left, n_right // step_right),
        in_specs=[left_spec] * parts + [right_spec] * parts,
        out_specs=pl.BlockSpec((step_left, step_right), lambda i, j: (i, j)),
        out_shape=jax.ShapeDtypeStruct((n_left, n_right), dtype),
        compiler_params=params(),
        cost_estimate=pl.CostEstimate(flops=2 * parts * items * rows * n_left * n_right, bytes_accessed=2 * parts * items * rows * (n_left + n_right), transcendentals=0),
        name="weight_product",
    )(*lefts, *rights)


def local(*args):
    tokens, segment_count = args[:2]
    shards = args[2:18]
    cotangent, memory_cotangent = args[18:]
    axes = ("dp", "shard")
    items, segments, seg, width = tokens.shape

    def gather(a):
        return lax.all_gather(a, axes, axis=0, tiled=True)

    full = [gather(a) for a in shards]
    mem0 = full[0].astype(F32).T
    wq, wk, wv, wo, wup, wdown = full[1:7]
    bq, bv, bo, bup, bdown, g1, s1, g2, s2 = [a.astype(F32)[None, :] for a in full[7:]]
    mem_rows = mem0.shape[0]
    pad = 16 - mem_rows
    mem = jnp.broadcast_to(jnp.pad(mem0, ((pad, 0), (0, 0)))[None], (items, 16, width))
    saved = []
    outputs = []
    for s in range(segments):
        x, q, k, v, e, o, li = call_attend_forward(s, tokens, mem, wq, wk, wv, bq, bv)
        y, mem, xh1, sc1, h, a, gp, xh2, sc2 = call_feed_forward(
            s, segment_count, tokens, mem, o, wo, wup, wdown, bo, g1, s1, bup, bdown, g2, s2
        )
        outputs.append(y)
        saved.append((x, q, k, v, e, o, li, xh1, sc1, h, a, gp, xh2, sc2))
    memory_final = mem[:, pad:].astype(BF16)
    dmem = jnp.pad(memory_cotangent.astype(F32), ((0, 0), (pad, 0), (0, 0)))
    grads = [None] * segments
    pieces = [None] * segments
    vec = 0.0
    vup = 0.0
    vat = 0.0
    for s in reversed(range(segments)):
        x, q, k, v, e, o, li, xh1, sc1, h, a, gp, xh2, sc2 = saved[s]
        df, du, dr, db, vec_s, vup_s = call_feed_backward(
            s, segment_count, cotangent, dmem, xh2, sc2, gp, xh1, sc1, wup, wdown, g1, g2
        )
        tg, dmem, dq, dk, dv, vat_s = call_attend_backward(
            s, seg, segment_count, dmem, dr, db, q, k, v, e, o, li, wo, wq, wk, wv
        )
        grads[s] = tg
        pieces[s] = (x, dq, dk, dv, o, db, h, du, a, df)
        vec = vec + vec_s.sum(axis=0)
        vup = vup + vup_s.sum(axis=(0, 1))
        vat = vat + vat_s.sum(axis=0)
    x, dq, dk, dv, o, db, h, du, a, df = zip(*pieces)
    gq = call_weight_product(x, dq, 768, 256, F32)
    gk = call_weight_product(x, dk, 768, 256, F32)
    gv = call_weight_product(x, dv, 768, 256, F32)
    go = call_weight_product(o, db, 768, 256, F32)
    gup = call_weight_product(h, du, 768, 256, F32)
    gdown = call_weight_product(a, df, 256, 768, F32)
    gmem = dmem[:, pad:].sum(axis=0).T
    terms = (gmem, gq, gk, gv, go, gup, gdown, vat[0], vat[1], vec[5], vup, vec[4], vec[0], vec[1], vec[2], vec[3])
    owned = lax.psum_scatter(terms, axes, scatter_dimension=0, tiled=True)
    return (jnp.stack(outputs, 1), memory_final, jnp.stack(grads, 1)) + tuple(owned)


def solution(mesh):
    rows = P(("dp", "shard"))
    return jax.shard_map(local, mesh=mesh, in_specs=(rows,) * 20, out_specs=(rows,) * 19, check_vma=False)
```

```python
import functools

import jax
import jax.numpy as jnp
from jax import lax
from jax.experimental import pallas as pl
from jax.experimental.pallas import tpu as pltpu
from jax.sharding import PartitionSpec as P

F32 = jnp.float32
BF16 = jnp.bfloat16
HEADS = 12
HEAD_DIM = 64
NORM_EPS = 1e-06
ROOT_HALF = 0.7071067811865476
ROOT_TWO_PI = 0.3989422804014327
VMEM_BYTES = 60 << 20


def dot_nn(left, right):
    return jnp.dot(left, right, preferred_element_type=F32)


def dot_nt(left, right):
    return lax.dot_general(left, right, (((1,), (1,)), ((), ())), preferred_element_type=F32)


def dot_tn(left, right):
    return lax.dot_general(left, right, (((0,), (0,)), ((), ())), preferred_element_type=F32)


def lane_masks(rows):
    lane = lax.broadcasted_iota(jnp.int32, (rows, 128), 1)
    first = jnp.where(lane < HEAD_DIM, 1.0, 0.0)
    return first, 1.0 - first


def key_counts(rows, tokens):
    row = lax.broadcasted_iota(jnp.int32, (rows, 128), 0)
    return jnp.where(row < tokens, 1.0, 2.0)


def gelu_parts(u):
    bell = jnp.exp(u * u * -0.5)
    t = pl.reciprocal(1.0 + (0.3275911 * ROOT_HALF) * jnp.abs(u))
    poly = t * (
        0.5 * 0.254829592
        + t * (0.5 * -0.284496736 + t * (0.5 * 1.421413741 + t * (0.5 * -1.453152027 + t * (0.5 * 1.061405429))))
    )
    tail = poly * bell
    cdf = jnp.where(u < 0.0, tail, 1.0 - tail)
    return u * cdf, cdf + u * bell * ROOT_TWO_PI


def attend_forward(tok, mem, wq, wk, wv, bq, bv, x_o, q_o, k_o, v_o, e_o, o_o, li_o):
    seg = tok.shape[2]
    rows = x_o.shape[1]
    x_o[0, rows - 16 :, :] = mem[0].astype(BF16)
    x_o[0, :seg, :] = tok[0, 0]
    x = x_o[0]
    q_o[0] = ((dot_nn(x, wq[...]) + bq[...]).astype(BF16).astype(F32) * 0.125).astype(BF16)
    k_o[0] = dot_nn(x, wk[...]).astype(BF16)
    v_o[0] = (dot_nn(x, wv[...]) + bv[...]).astype(BF16)
    masks = lane_masks(rows)
    count = key_counts(rows, seg)
    low_masks = tuple(m.astype(BF16) for m in masks)

    def pair(p, carry):
        at = pl.ds(pl.multiple_of(p * 128, 128), 128)
        q2 = q_o[0, :, at]
        k2 = k_o[0, :, at]
        v2 = v_o[0, :, at].astype(F32) * count
        total = None
        for h in range(2):
            s = dot_nt(q2 * low_masks[h], k2)
            e = jnp.exp(s - jnp.max(s, axis=-1, keepdims=True)).astype(BF16)
            e_o[0, 2 * p + h] = e
            right = jnp.concatenate(
                [(v2 * masks[h]).astype(BF16), (count * masks[h]).astype(BF16)], axis=1
            )
            part = dot_nn(e, right)
            total = part if total is None else total + part
        inv = 1.0 / total[:, 128:]
        li_o[0, :, at] = inv
        o_o[0, :, at] = (total[:, :128] * inv).astype(BF16)
        return carry

    lax.fori_loop(0, HEADS // 2, pair, 0)


def norm_rows(r):
    mean = jnp.mean(r, axis=-1, keepdims=True)
    center = r - mean
    var = jnp.mean(center * center, axis=-1, keepdims=True)
    scale = lax.rsqrt(var + NORM_EPS)
    return center * scale, scale


def feed_forward(
    segment, step,
    count, tok, mem, o, wo, wup, wdown, bo, g1, s1, bup, bdown, g2, s2,
    y_o, mem_o, xh1_o, sc1_o, h_o, a_o, gp_o, xh2_o, sc2_o, x_s,
):
    seg = tok.shape[2]
    rows = o.shape[1]
    ff = wup.shape[1]
    x_s[rows - 16 :, :] = mem[0]
    x_s[:seg, :] = tok[0, 0].astype(F32)
    xh, sc = norm_rows(x_s[...] + dot_nn(o[0], wo[...]) + bo[...])
    xh1_o[0] = xh.astype(BF16)
    sc1_o[0] = jnp.broadcast_to(sc, (rows, 128))
    h1 = xh * g1[...] + s1[...]
    h_o[0] = h1.astype(BF16)
    x_s[...] = h1 + bdown[...]

    def chunk(j, carry):
        at = pl.ds(pl.multiple_of(j * step, step), step)
        act, slope = gelu_parts(dot_nn(h_o[0], wup[:, at]) + bup[:, at])
        a_o[0, :, at] = act.astype(BF16)
        gp_o[0, :, at] = slope.astype(BF16)
        x_s[...] += dot_nn(a_o[0, :, at], wdown[at, :])
        return carry

    lax.fori_loop(0, ff // step, chunk, 0)
    xh, sc = norm_rows(x_s[...])
    xh2_o[0] = xh.astype(BF16)
    sc2_o[0] = jnp.broadcast_to(sc, (rows, 128))
    x_s[...] = xh * g2[...] + s2[...]
    active = count[pl.program_id(0)] > segment
    y_o[0] = jnp.where(active, x_s[:seg, :], 0.0).astype(BF16)
    mem_o[0] = jnp.where(active, x_s[rows - 16 :, :], mem[0])


def norm_back(dy, xh, sc, gain):
    dxh = dy * gain
    m1 = jnp.mean(dxh, axis=-1, keepdims=True)
    m2 = jnp.mean(dxh * xh, axis=-1, keepdims=True)
    return sc * (dxh - m1 - xh * m2)


def col_sum(x):
    return jnp.sum(x, axis=0, keepdims=True)


def feed_backward(
    segment, step,
    count, cot, dmem, xh2, sc2, gp, xh1, sc1, wup, wdown, g1, g2,
    df_o, du_o, dr_o, db_o, vec_o, vup_o, x_s,
):
    seg = cot.shape[2]
    rows = xh2.shape[1]
    ff = wup.shape[1]
    active = jnp.where(count[pl.program_id(0)] > segment, 1.0, 0.0)
    x_s[rows - 16 :, :] = dmem[0] * active
    x_s[:seg, :] = cot[0, 0].astype(F32) * active
    dy = x_s[...]
    xh = xh2[0].astype(F32)
    vec_o[0, 2:3, :] = col_sum(dy * xh)
    vec_o[0, 3:4, :] = col_sum(dy)
    dr = norm_back(dy, xh, sc2[0, :, :1], g2[...])
    df = dr.astype(BF16)
    df_o[0] = df
    vec_o[0, 4:5, :] = col_sum(df.astype(F32))
    x_s[...] = dr

    def chunk(j, carry):
        at = pl.ds(pl.multiple_of(j * step, step), step)
        du = dot_nt(df_o[0], wdown[at, :]) * gp[0, :, at].astype(F32)
        vup_o[0, :, at] = col_sum(du)
        du_o[0, :, at] = du.astype(BF16)
        x_s[...] += dot_nt(du_o[0, :, at], wup[:, at])
        return carry

    lax.fori_loop(0, ff // step, chunk, 0)
    dh = x_s[...]
    xh = xh1[0].astype(F32)
    vec_o[0, 0:1, :] = col_sum(dh * xh)
    vec_o[0, 1:2, :] = col_sum(dh)
    dr = norm_back(dh, xh, sc1[0, :, :1], g1[...])
    dr_o[0] = dr
    db_o[0] = dr.astype(BF16)
    vec_o[0, 5:6, :] = col_sum(dr)


def attend_backward(
    segment,
    count, dmem, dr, db, q, k, v, e, o, li, wo, wq, wk, wv,
    tg_o, dmem_o, dq_o, dk_o, dv_o, vec_o, do_s, x_s,
):
    seg = tg_o.shape[1]
    rows = q.shape[1]
    do_s[...] = dot_nt(db[0], wo[...]).astype(BF16)
    masks = lane_masks(rows)
    count2 = key_counts(rows, seg)
    low_masks = tuple(m.astype(BF16) for m in masks)
    ones = jnp.ones((rows, 128), BF16)

    def pair(p, carry):
        at = pl.ds(pl.multiple_of(p * 128, 128), 128)
        dop = do_s[:, at].astype(F32) * li[0, :, at]
        pr = (dop * o[0, :, at].astype(F32) * -1.0).astype(BF16)
        dop = dop.astype(BF16)
        q2 = q[0, :, at]
        k2 = (k[0, :, at].astype(F32) * (count2 * 0.125)).astype(BF16)
        right = jnp.concatenate([v[0, :, at], ones], axis=1)
        dq = dk = dv = None
        for h in range(2):
            e_h = e[0, 2 * p + h]
            d_h = dop * low_masks[h]
            left = jnp.concatenate([d_h, pr * low_masks[h]], axis=1)
            ds = (e_h.astype(F32) * dot_nt(left, right)).astype(BF16)
            q_t = dot_nn(ds, k2 * low_masks[h])
            k_t = dot_tn(ds, q2 * low_masks[h])
            v_t = dot_tn(e_h, d_h)
            dq = q_t if dq is None else dq + q_t
            dk = k_t if dk is None else dk + k_t
            dv = v_t if dv is None else dv + v_t
        dq_o[0, :, at] = dq.astype(BF16)
        dk_o[0, :, at] = (dk * count2).astype(BF16)
        dv_o[0, :, at] = (dv * count2).astype(BF16)
        return carry

    lax.fori_loop(0, HEADS // 2, pair, 0)
    vec_o[0, 0:1, :] = col_sum(dq_o[0].astype(F32))
    vec_o[0, 1:2, :] = col_sum(dv_o[0].astype(F32))
    x_s[...] = (
        dr[0]
        + dot_nt(dq_o[0], wq[...])
        + dot_nt(dk_o[0], wk[...])
        + dot_nt(dv_o[0], wv[...])
    )
    tg_o[0] = x_s[:seg, :].astype(BF16)
    kept = jnp.where(count[pl.program_id(0)] > segment, 0.0, 1.0)
    dmem_o[0] = dmem[0] * kept + x_s[rows - 16 :, :]


def weight_product(parts, *refs):
    lefts = refs[:parts]
    rights = refs[parts : 2 * parts]
    out = refs[2 * parts]
    total = None
    for left, right in zip(lefts, rights):
        for i in range(left.shape[0]):
            term = dot_tn(left[i], right[i])
            total = term if total is None else total + term
    out[...] = total.astype(out.dtype)


def whole(array):
    dims = array.shape
    return pl.BlockSpec(dims, lambda *g: (0,) * len(dims), pipeline_mode=pl.Buffered(1))


def per_item(dims):
    return pl.BlockSpec((1,) + dims, lambda i: (i,) + (0,) * len(dims))


def out_of(items, dims, dtype):
    return jax.ShapeDtypeStruct((items,) + dims, dtype)


SCALARS = pl.BlockSpec(memory_space=pltpu.SMEM)


def params(**more):
    return pltpu.CompilerParams(vmem_limit_bytes=VMEM_BYTES, **more)


def call_attend_forward(segment, tokens, mem, wq, wk, wv, bq, bv):
    items, _, seg, width = tokens.shape
    rows = seg + 10
    tok = pl.BlockSpec((1, 1, seg, width), lambda i: (i, segment, 0, 0))
    outs = [((rows, width), BF16)] * 4 + [((HEADS, rows, rows), BF16), ((rows, width), BF16), ((rows, width), F32)]
    return pl.pallas_call(
        attend_forward,
        grid=(items,),
        in_specs=[tok, per_item((16, width)), whole(wq), whole(wk), whole(wv), whole(bq), whole(bv)],
        out_specs=[per_item(d) for d, t in outs],
        out_shape=[out_of(items, d, t) for d, t in outs],
        compiler_params=params(),
        cost_estimate=pl.CostEstimate(flops=items * 2 * rows * (3 * width * width + 8 * rows * width), bytes_accessed=items * rows * (width * 14 + HEADS * rows * 2), transcendentals=0),
        name="attend_forward",
    )(tokens, mem, wq, wk, wv, bq, bv)


def call_feed_forward(segment, count, tokens, mem, o, wo, wup, wdown, bo, g1, s1, bup, bdown, g2, s2):
    items, _, seg, width = tokens.shape
    rows = o.shape[1]
    ff = wup.shape[1]
    tok = pl.BlockSpec((1, 1, seg, width), lambda i: (i, segment, 0, 0))
    outs = [
        ((seg, width), BF16), ((16, width), F32), ((rows, width), BF16), ((rows, 128), F32), ((rows, width), BF16),
        ((rows, ff), BF16), ((rows, ff), BF16), ((rows, width), BF16), ((rows, 128), F32),
    ]
    fixed = (wo, wup, wdown, bo, g1, s1, bup, bdown, g2, s2)
    return pl.pallas_call(
        functools.partial(feed_forward, segment, 768),
        grid=(items,),
        in_specs=[SCALARS, tok, per_item((16, width)), per_item((rows, width))] + [whole(w) for w in fixed],
        out_specs=[per_item(d) for d, t in outs],
        out_shape=[out_of(items, d, t) for d, t in outs],
        scratch_shapes=[pltpu.VMEM((rows, width), F32)],
        compiler_params=params(),
        cost_estimate=pl.CostEstimate(flops=items * 2 * rows * width * (width + 2 * ff), bytes_accessed=items * rows * (width * 14 + ff * 4), transcendentals=0),
        name="feed_forward",
    )(count, tokens, mem, o, *fixed)


def call_feed_backward(segment, count, cot, dmem, xh2, sc2, gp, xh1, sc1, wup, wdown, g1, g2):
    items, _, seg, width = cot.shape
    rows = xh2.shape[1]
    ff = wup.shape[1]
    tok = pl.BlockSpec((1, 1, seg, width), lambda i: (i, segment, 0, 0))
    outs = [((rows, width), BF16), ((rows, ff), BF16), ((rows, width), F32), ((rows, width), BF16), ((8, width), F32), ((1, ff), F32)]
    fixed = (wup, wdown, g1, g2)
    return pl.pallas_call(
        functools.partial(feed_backward, segment, 768),
        grid=(items,),
        in_specs=[SCALARS, tok] + [per_item(a.shape[1:]) for a in (dmem, xh2, sc2, gp, xh1, sc1)] + [whole(w) for w in fixed],
        out_specs=[per_item(d) for d, t in outs],
        out_shape=[out_of(items, d, t) for d, t in outs],
        scratch_shapes=[pltpu.VMEM((rows, width), F32)],
        compiler_params=params(),
        cost_estimate=pl.CostEstimate(flops=items * 4 * rows * width * ff, bytes_accessed=items * rows * (width * 14 + ff * 4), transcendentals=0),
        name="feed_backward",
    )(count, cot, dmem, xh2, sc2, gp, xh1, sc1, *fixed)


def call_attend_backward(segment, seg, count, dmem, dr, db, q, k, v, e, o, li, wo, wq, wk, wv):
    items, rows, width = q.shape
    outs = [((seg, width), BF16), ((16, width), F32)] + [((rows, width), BF16)] * 3 + [((8, width), F32)]
    fixed = (wo, wq, wk, wv)
    return pl.pallas_call(
        functools.partial(attend_backward, segment),
        grid=(items,),
        in_specs=[SCALARS] + [per_item(a.shape[1:]) for a in (dmem, dr, db, q, k, v, e, o, li)] + [whole(w) for w in fixed],
        out_specs=[per_item(d) for d, t in outs],
        out_shape=[out_of(items, d, t) for d, t in outs],
        scratch_shapes=[pltpu.VMEM((rows, width), BF16), pltpu.VMEM((rows, width), F32)],
        compiler_params=params(),
        cost_estimate=pl.CostEstimate(flops=items * 2 * rows * width * (4 * width + 16 * rows), bytes_accessed=items * rows * (width * 24 + HEADS * rows * 2), transcendentals=0),
        name="attend_backward",
    )(count, dmem, dr, db, q, k, v, e, o, li, *fixed)


def call_weight_product(lefts, rights, step_left, step_right, dtype):
    parts = len(lefts)
    items, rows, n_left = lefts[0].shape
    n_right = rights[0].shape[2]
    left_spec = pl.BlockSpec((items, rows, step_left), lambda i, j: (0, 0, i))
    right_spec = pl.BlockSpec((items, rows, step_right), lambda i, j: (0, 0, j))
    return pl.pallas_call(
        functools.partial(weight_product, parts),
        grid=(n_left // step_left, n_right // step_right),
        in_specs=[left_spec] * parts + [right_spec] * parts,
        out_specs=pl.BlockSpec((step_left, step_right), lambda i, j: (i, j)),
        out_shape=jax.ShapeDtypeStruct((n_left, n_right), dtype),
        compiler_params=params(),
        cost_estimate=pl.CostEstimate(flops=2 * parts * items * rows * n_left * n_right, bytes_accessed=2 * parts * items * rows * (n_left + n_right), transcendentals=0),
        name="weight_product",
    )(*lefts, *rights)


AXES = ("dp", "shard")
UNIT = 24


def spot(z, y, c, x):
    return ((z * 2 + y) * 2 + c) * 2 + x


def swap(array, dz, dy, dc, dx):
    pairs = [
        (spot(z, y, c, x), spot(z ^ dz, y ^ dy, c ^ dc, x ^ dx))
        for z in range(4)
        for y in range(2)
        for c in range(2)
        for x in range(2)
    ]
    return lax.ppermute(array, AXES, pairs)


def coordinates():
    dp = lax.axis_index("dp")
    return jnp.stack([dp // 4, dp // 2 % 2, dp % 2, lax.axis_index("shard")]).astype(jnp.int32)


def join(*parts):
    return jnp.concatenate(parts, axis=0)


def gather_units(unit):
    own = unit[None]
    a = join(own, swap(own, 1, 0, 0, 0))
    b = join(swap(own, 2, 0, 0, 0), swap(own, 3, 0, 0, 0))
    a = join(a, swap(a, 0, 1, 0, 0))
    b = join(b, swap(b, 0, 0, 0, 1))
    mine = (a, swap(a, 0, 0, 0, 1), b, swap(b, 0, 1, 0, 0))
    return mine + tuple(swap(m, 0, 0, 1, 0) for m in mine)


def add_low(left, right):
    return (left.astype(F32) + right.astype(F32)).astype(BF16)


def reduce_units(keep, send):
    got = swap(send, 0, 0, 1, 0)
    send_a = add_low(keep[:2, :, 1], got[:2, :, 1])
    send_b = add_low(keep[2:, 1], got[2:, 1])
    got_a = swap(send_a, 0, 0, 0, 1)
    got_b = swap(send_b, 0, 1, 0, 0)
    a = keep[:2, :, 0].astype(F32) + got[:2, :, 0].astype(F32) + got_a.astype(F32)
    b = keep[2:, 0].astype(F32) + got[2:, 0].astype(F32) + got_b.astype(F32)
    got_a = swap(a[:, 1].astype(BF16), 0, 1, 0, 0)
    got_b = swap(b[:, 1].astype(BF16), 0, 0, 0, 1)
    a = a[:, 0] + got_a.astype(F32)
    b = b[:, 0] + got_b.astype(F32)
    one = swap(a[1].astype(BF16), 1, 0, 0, 0)
    two = swap(b[0].astype(BF16), 2, 0, 0, 0)
    three = swap(b[1].astype(BF16), 3, 0, 0, 0)
    return a[0] + one.astype(F32) + two.astype(F32) + three.astype(F32)


def unit_pairs(me, bufs, emit):
    mz, my, mc, mx = me[0], me[1], me[2], me[3]
    flip = jnp.broadcast_to(mx, (8, 128)) == 1

    def send(dz, dy, dc, near, far):
        dp = ((mz ^ dz) * 2 + (my ^ dy)) * 2 + (mc ^ dc)
        emit(dp, near, far)

    for dc in range(2):
        a, a_far, b, b_far = bufs[4 * dc : 4 * dc + 4]
        for i in range(2):
            for j in range(2):
                send(j, i, dc, (a, 2 * i + j), (a_far, 2 * i + j))
        for i, buf in enumerate((b, b_far)):
            for j in range(2):
                send(2 + j, i, dc, (buf, j), (buf, 2 + j))


def assemble_first(me, *refs):
    bufs, (wq, wk, wv, small) = refs[:8], refs[8:]
    mx = me[3]

    def emit(dp, near, far):
        n = near[0][near[1]].astype(F32)
        f = far[0][far[1]].astype(F32)
        low = jnp.where(mx == 0, n, f)
        high = jnp.where(mx == 0, f, n)
        at = pl.ds(pl.multiple_of(dp * 48, 16), 48)
        for w, ref in enumerate((wq, wk, wv)):
            ref[at, :] = jnp.concatenate(
                [low[UNIT * w : UNIT * (w + 1)], high[UNIT * w : UNIT * (w + 1)]], axis=0
            ).astype(BF16)
        small[dp * 2] = low[3 * UNIT : 3 * UNIT + 1]
        small[dp * 2 + 1] = high[3 * UNIT : 3 * UNIT + 1]

    unit_pairs(me, bufs, emit)


def assemble_second(me, *refs):
    bufs, (wo, wup) = refs[:8], refs[8:]
    mx = me[3]
    width = wo.shape[1]

    def emit(dp, near, far):
        at = pl.ds(pl.multiple_of(dp * 48, 16), 48)
        for w in range(5):
            n = near[0][near[1], w].astype(F32)
            f = far[0][far[1], w].astype(F32)
            low = jnp.where(mx == 0, n, f)
            high = jnp.where(mx == 0, f, n)
            rows = jnp.concatenate([low, high], axis=0).astype(BF16)
            if w == 0:
                wo[at, :] = rows
            else:
                wup[at, (w - 1) * width : w * width] = rows

    unit_pairs(me, bufs, emit)


def assemble_third(me, *refs):
    bufs, (wdown,) = refs[:8], refs[8:]
    mx = me[3]
    tall = 4 * UNIT

    def emit(dp, near, far):
        for (buf, i), x in ((near, mx), (far, 1 - mx)):
            at = pl.ds(pl.multiple_of((dp * 2 + x) * tall, 16), tall)
            wdown[at, :] = buf[i]

    unit_pairs(me, bufs, emit)


def call_assemble(body, me, bufs, outs, name):
    vm = pl.BlockSpec(memory_space=pltpu.VMEM)
    return pl.pallas_call(
        body,
        in_specs=[SCALARS] + [vm] * 8,
        out_specs=[vm] * len(outs),
        out_shape=[jax.ShapeDtypeStruct(d, t) for d, t in outs],
        compiler_params=params(),
        name=name,
    )(me, *bufs)


def emit_units(me, keep, send, value_of):
    mz, my, mc, mx = me[0], me[1], me[2], me[3]
    for core in range(2):

        @pl.when(mc == core)
        def _():
            for z in range(4):
                for y in range(2):
                    for x in range(2):
                        to = (z ^ mz, y ^ my, x ^ mx)
                        keep[to] = value_of(z, y, core, x)
                        send[to] = value_of(z, y, 1 - core, x)


def product_sum(lefts, rights):
    total = None
    for left, right in zip(lefts, rights):
        for i in range(left.shape[0]):
            term = dot_tn(left[i], right[i])
            total = term if total is None else total + term
    return total


def product_up(segments, me, *refs):
    o, db, h, du = (refs[segments * i : segments * (i + 1)] for i in range(4))
    keep, send, acc = refs[4 * segments :]

    @pl.when(pl.program_id(0) == 0)
    def _():
        acc[...] = product_sum(o, db)

    @pl.when(pl.program_id(0) > 0)
    def _():
        acc[...] = product_sum(h, du)

    def value_of(*at):
        idx = spot(*at)
        return acc[UNIT * idx : UNIT * (idx + 1), :].astype(BF16)

    emit_units(me, keep.at[:, :, :, 0], send.at[:, :, :, 0], value_of)


def product_down(segments, me, *refs):
    a, df = refs[:segments], refs[segments : 2 * segments]
    keep, send, acc = refs[2 * segments :]
    tall = 4 * UNIT
    acc[...] = product_sum(a, df)
    my, mc, mx = me[1], me[2], me[3]
    for core in range(2):

        @pl.when(mc == core)
        def _():
            for y in range(2):
                for x in range(2):
                    for ref, c in ((keep, core), (send, 1 - core)):
                        row = ((y * 2 + c) * 2 + x) * tall
                        ref[0, y ^ my, x ^ mx] = acc[row : row + tall, :].astype(BF16)


def product_first(segments, me, small, *refs):
    x, dq, dk, dv = (refs[segments * i : segments * (i + 1)] for i in range(4))
    keep, send, acc = refs[4 * segments :]
    step = pl.program_id(0)

    for w, right in enumerate((dq, dk, dv)):
        term = product_sum(x, right)

        @pl.when(step == 0)
        def _():
            acc[w] = term

        @pl.when(step > 0)
        def _():
            acc[w] += term

    @pl.when(step == pl.num_programs(0) - 1)
    def _():
        def value_of(*at):
            idx = spot(*at)
            rows = [acc[w, UNIT * idx : UNIT * (idx + 1), :] for w in range(3)]
            return jnp.concatenate(rows + [small[idx]], axis=0).astype(BF16)

        emit_units(me, keep, send, value_of)


def call_product_up(me, o, db, h, du):
    segments = len(o)
    items, rows, width = o[0].shape
    ff = du[0].shape[2]
    steps = ff // width
    fixed = [pl.BlockSpec((items, rows, width), lambda j, m: (0, 0, 0), pipeline_mode=pl.Buffered(1))] * (3 * segments)
    moving = [pl.BlockSpec((items, rows, width), lambda j, m: (0, 0, jnp.maximum(j - 1, 0)))] * segments
    dims = (4, 2, 2, steps + 1, UNIT, width)
    out = pl.BlockSpec((4, 2, 2, 1, UNIT, width), lambda j, m: (0, 0, 0, j, 0, 0))
    return pl.pallas_call(
        functools.partial(product_up, segments),
        grid_spec=pltpu.PrefetchScalarGridSpec(
            num_scalar_prefetch=1,
            grid=(steps + 1,),
            in_specs=fixed + moving,
            out_specs=[out, out],
            scratch_shapes=[pltpu.VMEM((width, width), F32)],
        ),
        out_shape=[jax.ShapeDtypeStruct(dims, BF16)] * 2,
        compiler_params=params(),
        cost_estimate=pl.CostEstimate(flops=2 * segments * items * rows * width * (ff + width), bytes_accessed=2 * segments * items * rows * (ff + 3 * width) + 2 * width * (ff + width), transcendentals=0),
        name="product_up",
    )(me, *o, *db, *h, *du)


def call_product_down(me, a, df):
    segments = len(a)
    items, rows, width = df[0].shape
    ff = a[0].shape[2]
    moving = [pl.BlockSpec((items, rows, ff // 4), lambda j, m: (0, 0, j ^ m[0]))] * segments
    fixed = [pl.BlockSpec((items, rows, width), lambda j, m: (0, 0, 0), pipeline_mode=pl.Buffered(1))] * segments
    dims = (4, 2, 2, 4 * UNIT, width)
    out = pl.BlockSpec((1, 2, 2, 4 * UNIT, width), lambda j, m: (j, 0, 0, 0, 0))
    return pl.pallas_call(
        functools.partial(product_down, segments),
        grid_spec=pltpu.PrefetchScalarGridSpec(
            num_scalar_prefetch=1,
            grid=(4,),
            in_specs=moving + fixed,
            out_specs=[out, out],
            scratch_shapes=[pltpu.VMEM((ff // 4, width), F32)],
        ),
        out_shape=[jax.ShapeDtypeStruct(dims, BF16)] * 2,
        compiler_params=params(),
        cost_estimate=pl.CostEstimate(flops=2 * segments * items * rows * width * ff, bytes_accessed=2 * segments * items * rows * (ff + width) + 2 * width * ff, transcendentals=0),
        name="product_down",
    )(me, *a, *df)


def call_product_first(me, small, x, dq, dk, dv):
    segments = len(x)
    items, rows, width = x[0].shape
    moving = [pl.BlockSpec((1, rows, width), lambda j, m: (j, 0, 0))] * (4 * segments)
    tall = 3 * UNIT + 8
    dims = (4, 2, 2, tall, width)
    out = pl.BlockSpec(dims, lambda j, m: (0,) * 5, pipeline_mode=pl.Buffered(1))
    return pl.pallas_call(
        functools.partial(product_first, segments),
        grid_spec=pltpu.PrefetchScalarGridSpec(
            num_scalar_prefetch=1,
            grid=(items,),
            in_specs=[pl.BlockSpec(small.shape, lambda j, m: (0, 0, 0), pipeline_mode=pl.Buffered(1))] + moving,
            out_specs=[out, out],
            scratch_shapes=[pltpu.VMEM((3, width, width), F32)],
        ),
        out_shape=[jax.ShapeDtypeStruct(dims, BF16)] * 2,
        compiler_params=params(),
        cost_estimate=pl.CostEstimate(flops=6 * segments * items * rows * width * width, bytes_accessed=8 * segments * items * rows * width + 6 * width * width, transcendentals=0),
        name="product_first",
    )(me, small, *x, *dq, *dk, *dv)


def unpack_small(small):
    devices = small.shape[0]
    per = small[:, : 18 * UNIT].reshape(devices, 18, UNIT)
    vectors = per.transpose(1, 0, 2).reshape(18, devices * UNIT)
    hidden = small[:, 18 * UNIT : 22 * UNIT].reshape(1, devices * 4 * UNIT)
    return vectors, hidden


def gather_weights(me, shards):
    mem, wq, wk, wv, wo, wup, wdown, bq, bv, bo, bup, bdown, g1, s1, g2, s2 = shards
    width = wq.shape[1]
    ff = wup.shape[1]
    vectors = jnp.concatenate([bq, bv, bo, bdown, g1, s1, mem.T.reshape(-1), g2, s2, bup])
    vectors = jnp.pad(vectors[None, :], ((0, 7), (0, width - vectors.shape[0])))
    first = gather_units(jnp.concatenate([wq, wk, wv, vectors], axis=0))
    up_blocks = wup.reshape(UNIT, ff // width, width).transpose(1, 0, 2)
    second = gather_units(jnp.concatenate([wo[None], up_blocks], axis=0))
    third = gather_units(wdown)
    square = ((width, width), BF16)
    wq, wk, wv, small = call_assemble(
        assemble_first, me, first, [square] * 3 + [((width // UNIT, 1, width), F32)], "assemble_first"
    )
    wo, wup = call_assemble(assemble_second, me, second, [square, ((width, ff), BF16)], "assemble_second")
    (wdown,) = call_assemble(assemble_third, me, third, [((ff, width), BF16)], "assemble_third")
    vectors, hidden = unpack_small(small[:, 0])
    return wq, wk, wv, wo, wup, wdown, vectors, hidden


def gather_plain(shards):
    mem, wq, wk, wv, wo, wup, wdown, bq, bv, bo, bup, bdown, g1, s1, g2, s2 = [
        lax.all_gather(a, AXES, axis=0, tiled=True) for a in shards
    ]
    rows = [bq, bv, bo, bdown, g1, s1, mem.T, g2, s2]
    vectors = jnp.concatenate([r.reshape(-1, wq.shape[1]) for r in rows], axis=0).astype(F32)
    return wq, wk, wv, wo, wup, wdown, vectors, bup.astype(F32)[None, :]


def reduce_plain(pieces, vectors, hidden):
    x, dq, dk, dv, o, db, h, du, a, df = pieces
    gq = call_weight_product(x, dq, 768, 256, F32)
    gk = call_weight_product(x, dk, 768, 256, F32)
    gv = call_weight_product(x, dv, 768, 256, F32)
    go = call_weight_product(o, db, 768, 256, F32)
    gup = call_weight_product(h, du, 768, 256, F32)
    gdown = call_weight_product(a, df, 256, 768, F32)
    terms = (vectors[6:16].T, gq, gk, gv, go, gup, gdown, hidden) + tuple(
        vectors[i] for i in (0, 1, 2, 3, 4, 5, 16, 17)
    )
    owned = lax.psum_scatter(terms, AXES, scatter_dimension=0, tiled=True)
    mem, gq, gk, gv, go, gup, gdown, bup, bq, bv, bo, bdown, g1, s1, g2, s2 = owned
    return mem, gq, gk, gv, go, gup, gdown, bq, bv, bo, bup, bdown, g1, s1, g2, s2


def local(*args):
    tokens, segment_count = args[:2]
    shards = args[2:18]
    cotangent, memory_cotangent = args[18:]
    items, segments, seg, width = tokens.shape
    mem_rows = shards[0].shape[1]
    pad = 16 - mem_rows
    planned = lax.axis_size("dp") == 16 and lax.axis_size("shard") == 2
    me = coordinates()
    weights = gather_weights(me, shards) if planned else gather_plain(shards)
    wq, wk, wv, wo, wup, wdown, vectors, bup = weights
    bq, bv, bo, bdown, g1, s1 = [vectors[i : i + 1] for i in range(6)]
    g2, s2 = vectors[16:17], vectors[17:18]
    mem = jnp.broadcast_to(vectors[None, :16], (items, 16, width))
    saved = []
    outputs = []
    for s in range(segments):
        x, q, k, v, e, o, li = call_attend_forward(s, tokens, mem, wq, wk, wv, bq, bv)
        y, mem, xh1, sc1, h, a, gp, xh2, sc2 = call_feed_forward(
            s, segment_count, tokens, mem, o, wo, wup, wdown, bo, g1, s1, bup, bdown, g2, s2
        )
        outputs.append(y)
        saved.append((x, q, k, v, e, o, li, xh1, sc1, h, a, gp, xh2, sc2))
    memory_final = mem[:, pad:].astype(BF16)
    dmem = jnp.pad(memory_cotangent.astype(F32), ((0, 0), (pad, 0), (0, 0)))
    grads = [None] * segments
    pieces = [None] * segments
    vec = 0.0
    vup = 0.0
    vat = 0.0
    for s in reversed(range(segments)):
        x, q, k, v, e, o, li, xh1, sc1, h, a, gp, xh2, sc2 = saved[s]
        df, du, dr, db, vec_s, vup_s = call_feed_backward(
            s, segment_count, cotangent, dmem, xh2, sc2, gp, xh1, sc1, wup, wdown, g1, g2
        )
        pieces[s] = (x, o, db, h, du, a, df)
        vec = vec + vec_s.sum(axis=0)
        vup = vup + vup_s.sum(axis=0)
        if s == 0 and planned:
            o_all, db_all, h_all, du_all, a_all, df_all = list(zip(*pieces))[1:]
            down = reduce_units(*call_product_down(me, a_all, df_all))
            up = reduce_units(*call_product_up(me, o_all, db_all, h_all, du_all))
        tg, dmem, dq, dk, dv, vat_s = call_attend_backward(
            s, seg, segment_count, dmem, dr, db, q, k, v, e, o, li, wo, wq, wk, wv
        )
        grads[s] = tg
        pieces[s] += (dq, dk, dv)
        vat = vat + vat_s.sum(axis=0)
    x, o, db, h, du, a, df, dq, dk, dv = zip(*pieces)
    vectors = jnp.concatenate(
        [vat[:2], vec[5:6], vec[4:5], vec[0:2], dmem[:, pad:].sum(axis=0), vec[2:4]], axis=0
    )
    if planned:
        devices = lax.axis_size(AXES)
        per = vectors.reshape(18, devices, UNIT).transpose(1, 0, 2).reshape(devices, 18 * UNIT)
        small = jnp.concatenate([per, vup.reshape(devices, 4 * UNIT)], axis=1)
        small = jnp.pad(small[:, None, :], ((0, 0), (0, 7), (0, width - small.shape[1])))
        first = reduce_units(*call_product_first(me, small, x, dq, dk, dv))
        gq, gk, gv = [first[UNIT * w : UNIT * (w + 1)] for w in range(3)]
        line = first[3 * UNIT]
        per = line[: 18 * UNIT].reshape(18, UNIT)
        bq, bv, bo, bdown, g1, s1 = [per[i] for i in range(6)]
        go = up[0]
        gup = up[1:].transpose(1, 0, 2).reshape(UNIT, -1)
        owned = (
            per[6:16].T, gq, gk, gv, go, gup, down, bq, bv, bo,
            line[18 * UNIT : 22 * UNIT], bdown, g1, s1, per[16], per[17],
        )
    else:
        owned = reduce_plain((x, dq, dk, dv, o, db, h, du, a, df), vectors, vup[0])
    return (jnp.stack(outputs, 1), memory_final, jnp.stack(grads, 1)) + tuple(owned)


def solution(mesh):
    rows = P(("dp", "shard"))
    return jax.shard_map(local, mesh=mesh, in_specs=(rows,) * 20, out_specs=(rows,) * 19, check_vma=False)
```

```python
import functools

import jax
import jax.numpy as jnp
from jax import lax
from jax.experimental import pallas as pl
from jax.experimental.pallas import tpu as pltpu
from jax.sharding import PartitionSpec as P

F32 = jnp.float32
BF16 = jnp.bfloat16
HEADS = 12
HEAD_DIM = 64
NORM_EPS = 1e-06
ROOT_HALF = 0.7071067811865476
ROOT_TWO_PI = 0.3989422804014327
VMEM_BYTES = 60 << 20


def dot_nn(left, right):
    return jnp.dot(left, right, preferred_element_type=F32)


def dot_nt(left, right):
    return lax.dot_general(left, right, (((1,), (1,)), ((), ())), preferred_element_type=F32)


def dot_tn(left, right):
    return lax.dot_general(left, right, (((0,), (0,)), ((), ())), preferred_element_type=F32)


def lane_masks(rows):
    lane = lax.broadcasted_iota(jnp.int32, (rows, 128), 1)
    first = jnp.where(lane < HEAD_DIM, 1.0, 0.0)
    return first, 1.0 - first


def key_counts(rows, tokens):
    row = lax.broadcasted_iota(jnp.int32, (rows, 128), 0)
    return jnp.where(row < tokens, 1.0, 2.0)


def gelu_parts(u):
    bell = jnp.exp(u * u * -0.5)
    t = pl.reciprocal(1.0 + (0.3275911 * ROOT_HALF) * jnp.abs(u))
    poly = t * (
        0.5 * 0.254829592
        + t * (0.5 * -0.284496736 + t * (0.5 * 1.421413741 + t * (0.5 * -1.453152027 + t * (0.5 * 1.061405429))))
    )
    tail = poly * bell
    cdf = jnp.where(u < 0.0, tail, 1.0 - tail)
    return u * cdf, cdf + u * bell * ROOT_TWO_PI


def attend_forward(tok, mem, wq, wk, wv, vec, x_o, q_o, k_o, v_o, e_o, o_o, li_o):
    bq, bv = vec[0, 0:1, :], vec[0, 1:2, :]
    seg = tok.shape[2]
    rows = x_o.shape[1]
    x_o[0, rows - 16 :, :] = mem[0].astype(BF16)
    x_o[0, :seg, :] = tok[0, 0]
    x = x_o[0]
    q_o[0] = ((dot_nn(x, wq[...]) + bq).astype(BF16).astype(F32) * 0.125).astype(BF16)
    k_o[0] = dot_nn(x, wk[...]).astype(BF16)
    v_o[0] = (dot_nn(x, wv[...]) + bv).astype(BF16)
    masks = lane_masks(rows)
    count = key_counts(rows, seg)
    low_masks = tuple(m.astype(BF16) for m in masks)

    def pair(p, carry):
        at = pl.ds(pl.multiple_of(p * 128, 128), 128)
        q2 = q_o[0, :, at]
        k2 = k_o[0, :, at]
        v2 = v_o[0, :, at].astype(F32) * count
        total = None
        for h in range(2):
            s = dot_nt(q2 * low_masks[h], k2)
            e = jnp.exp(s - jnp.max(s, axis=-1, keepdims=True)).astype(BF16)
            e_o[0, 2 * p + h] = e
            right = jnp.concatenate(
                [(v2 * masks[h]).astype(BF16), (count * masks[h]).astype(BF16)], axis=1
            )
            part = dot_nn(e, right)
            total = part if total is None else total + part
        inv = 1.0 / total[:, 128:]
        li_o[0, :, at] = inv
        o_o[0, :, at] = (total[:, :128] * inv).astype(BF16)
        return carry

    lax.fori_loop(0, HEADS // 2, pair, 0, unroll=True)


def norm_rows(r):
    mean = jnp.mean(r, axis=-1, keepdims=True)
    center = r - mean
    var = jnp.mean(center * center, axis=-1, keepdims=True)
    scale = lax.rsqrt(var + NORM_EPS)
    return center * scale, scale


def feed_forward(
    segment, step,
    count, tok, mem, o, wo, wup, wdown, vec, bup,
    y_o, mem_o, xh1_o, sc1_o, h_o, a_o, gp_o, xh2_o, sc2_o, x_s,
):
    seg = tok.shape[2]
    rows = o.shape[1]
    ff = wup.shape[1]
    bo, bdown, g1, s1, g2, s2 = (vec[0, r : r + 1, :] for r in (2, 3, 4, 5, 16, 17))
    x_s[rows - 16 :, :] = mem[0]
    x_s[:seg, :] = tok[0, 0].astype(F32)
    xh, sc = norm_rows(x_s[...] + dot_nn(o[0], wo[...]) + bo)
    xh1_o[0] = xh.astype(BF16)
    sc1_o[0] = jnp.broadcast_to(sc, (rows, 128))
    h1 = xh * g1 + s1
    h_o[0] = h1.astype(BF16)
    x_s[...] = h1 + bdown

    def chunk(j, carry):
        at = pl.ds(pl.multiple_of(j * step, step), step)
        act, slope = gelu_parts(dot_nn(h_o[0], wup[:, at]) + bup[:, at])
        a_o[0, :, at] = act.astype(BF16)
        gp_o[0, :, at] = slope.astype(BF16)
        x_s[...] += dot_nn(a_o[0, :, at], wdown[at, :])
        return carry

    lax.fori_loop(0, ff // step, chunk, 0, unroll=True)
    xh, sc = norm_rows(x_s[...])
    xh2_o[0] = xh.astype(BF16)
    sc2_o[0] = jnp.broadcast_to(sc, (rows, 128))
    x_s[...] = xh * g2 + s2
    active = count[pl.program_id(0)] > segment
    y_o[0, 0] = jnp.where(active, x_s[:seg, :], 0.0).astype(BF16)
    mem_o[0] = jnp.where(active, x_s[rows - 16 :, :], mem[0])


def norm_back(dy, xh, sc, gain):
    dxh = dy * gain
    m1 = jnp.mean(dxh, axis=-1, keepdims=True)
    m2 = jnp.mean(dxh * xh, axis=-1, keepdims=True)
    return sc * (dxh - m1 - xh * m2)


def col_sum(x):
    return jnp.sum(x, axis=0, keepdims=True)


def feed_backward(
    segment, step,
    count, cot, dmem, xh2, sc2, gp, xh1, sc1, wup, wdown, vec,
    df_o, du_o, dr_o, db_o, vec_o, vup_o, x_s,
):
    seg = cot.shape[2]
    rows = xh2.shape[1]
    ff = wup.shape[1]
    g1, g2 = vec[0, 4:5, :], vec[0, 16:17, :]
    active = jnp.where(count[pl.program_id(0)] > segment, 1.0, 0.0)
    x_s[rows - 16 :, :] = dmem[0] * active
    x_s[:seg, :] = cot[0, 0].astype(F32) * active
    dy = x_s[...]
    xh = xh2[0].astype(F32)
    vec_o[0, 4:5, :] = col_sum(dy * xh)
    vec_o[0, 5:6, :] = col_sum(dy)
    dr = norm_back(dy, xh, sc2[0, :, :1], g2)
    df = dr.astype(BF16)
    df_o[0] = df
    vec_o[0, 1:2, :] = col_sum(df.astype(F32))
    x_s[...] = dr

    def chunk(j, carry):
        at = pl.ds(pl.multiple_of(j * step, step), step)
        du = dot_nt(df_o[0], wdown[at, :]) * gp[0, :, at].astype(F32)
        vup_o[0, :, at] = col_sum(du)
        du_o[0, :, at] = du.astype(BF16)
        x_s[...] += dot_nt(du_o[0, :, at], wup[:, at])
        return carry

    lax.fori_loop(0, ff // step, chunk, 0, unroll=True)
    dh = x_s[...]
    xh = xh1[0].astype(F32)
    vec_o[0, 2:3, :] = col_sum(dh * xh)
    vec_o[0, 3:4, :] = col_sum(dh)
    dr = norm_back(dh, xh, sc1[0, :, :1], g1)
    dr_o[0] = dr
    db_o[0] = dr.astype(BF16)
    vec_o[0, 0:1, :] = col_sum(dr)


def attend_backward(
    segment, first,
    count, dmem, dr, db, q, k, v, e, o, li, wo, wq, wk, wv,
    tg_o, dmem_o, dq_o, dk_o, dv_o, vec_o, do_s, x_s,
):
    seg = tg_o.shape[2]
    rows = q.shape[1]
    do_s[...] = dot_nt(db[0], wo[...]).astype(BF16)
    masks = lane_masks(rows)
    count2 = key_counts(rows, seg)
    low_masks = tuple(m.astype(BF16) for m in masks)
    ones = jnp.ones((rows, 128), BF16)

    def pair(p, carry):
        at = pl.ds(pl.multiple_of(p * 128, 128), 128)
        dop = do_s[:, at].astype(F32) * li[0, :, at]
        pr = (dop * o[0, :, at].astype(F32) * -1.0).astype(BF16)
        dop = dop.astype(BF16)
        q2 = q[0, :, at]
        k2 = (k[0, :, at].astype(F32) * (count2 * 0.125)).astype(BF16)
        right = jnp.concatenate([v[0, :, at], ones], axis=1)
        dq = dk = dv = None
        for h in range(2):
            e_h = e[0, 2 * p + h]
            d_h = dop * low_masks[h]
            left = jnp.concatenate([d_h, pr * low_masks[h]], axis=1)
            ds = (e_h.astype(F32) * dot_nt(left, right)).astype(BF16)
            q_t = dot_nn(ds, k2 * low_masks[h])
            k_t = dot_tn(ds, q2 * low_masks[h])
            v_t = dot_tn(e_h, d_h)
            dq = q_t if dq is None else dq + q_t
            dk = k_t if dk is None else dk + k_t
            dv = v_t if dv is None else dv + v_t
        dq_o[0, :, at] = dq.astype(BF16)
        dk_o[0, :, at] = (dk * count2).astype(BF16)
        dv_o[0, :, at] = (dv * count2).astype(BF16)
        return carry

    lax.fori_loop(0, HEADS // 2, pair, 0, unroll=True)
    vec_o[0, 0:1, :] = col_sum(dq_o[0].astype(F32))
    vec_o[0, 1:2, :] = col_sum(dv_o[0].astype(F32))
    x_s[...] = (
        dr[0]
        + dot_nt(dq_o[0], wq[...])
        + dot_nt(dk_o[0], wk[...])
        + dot_nt(dv_o[0], wv[...])
    )
    tg_o[0, 0] = x_s[:seg, :].astype(BF16)
    kept = jnp.where(count[pl.program_id(0) + first] > segment, 0.0, 1.0)
    dmem_o[0] = dmem[0] * kept + x_s[rows - 16 :, :]


def weight_product(parts, *refs):
    lefts = refs[:parts]
    rights = refs[parts : 2 * parts]
    out = refs[2 * parts]
    total = None
    for left, right in zip(lefts, rights):
        for i in range(left.shape[0]):
            term = dot_tn(left[i], right[i])
            total = term if total is None else total + term
    out[...] = total.astype(out.dtype)


def whole(array):
    dims = array.shape
    return pl.BlockSpec(dims, lambda *g: (0,) * len(dims), pipeline_mode=pl.Buffered(1))


def per_item(dims, first=0):
    return pl.BlockSpec((1,) + dims, lambda i: (i + first,) + (0,) * len(dims))


def per_segment(dims, segment, first=0):
    return pl.BlockSpec((1, 1) + dims, lambda i: (i + first, segment) + (0,) * len(dims))


def memory_spec(array, first=0):
    shared = array.shape[0] == 1
    return pl.BlockSpec((1, 16, array.shape[2]), lambda i: (0 if shared else i + first, 0, 0))


def out_of(items, dims, dtype):
    return jax.ShapeDtypeStruct((items,) + dims, dtype)


SCALARS = pl.BlockSpec(memory_space=pltpu.SMEM)


def params(**more):
    return pltpu.CompilerParams(vmem_limit_bytes=VMEM_BYTES, **more)


def launch(body, grid, args, in_specs, out_specs, out_shape, into=None, **more):
    into = into or {}
    n_in = len(args)
    aliases = {n_in + k: o for k, o in enumerate(into)}

    def run(*refs):
        body(*refs[:n_in], *refs[n_in + len(into) :])

    return pl.pallas_call(
        run if into else body,
        grid=grid,
        in_specs=list(in_specs) + [pl.BlockSpec(memory_space=pl.ANY)] * len(into),
        out_specs=out_specs,
        out_shape=out_shape,
        input_output_aliases=aliases,
        compiler_params=params(),
        **more,
    )(*args, *into.values())


def call_attend_forward(segment, tokens, mem, wq, wk, wv, vec, first=0, many=None, into=None):
    items, _, seg, width = tokens.shape
    many = many or items
    rows = seg + 10
    outs = [((rows, width), BF16)] * 4 + [((HEADS, rows, rows), BF16), ((rows, width), BF16), ((rows, width), F32)]
    return launch(
        attend_forward,
        (many,),
        (tokens, mem, wq, wk, wv, vec),
        [per_segment((seg, width), segment, first), memory_spec(mem, first)] + [whole(w) for w in (wq, wk, wv, vec)],
        [per_item(d, first) for d, t in outs],
        [out_of(items, d, t) for d, t in outs],
        into=dict(enumerate(into)) if into else None,
        cost_estimate=pl.CostEstimate(flops=many * 2 * rows * (3 * width * width + 8 * rows * width), bytes_accessed=many * rows * (width * 14 + HEADS * rows * 2), transcendentals=0),
        name="attend_forward",
    )


def call_feed_forward(segment, count, tokens, mem, o, wo, wup, wdown, vec, bup, into=None):
    items, segments, seg, width = tokens.shape
    rows = o.shape[1]
    ff = wup.shape[1]
    outs = [
        ((16, width), F32), ((rows, width), BF16), ((rows, 128), F32), ((rows, width), BF16),
        ((rows, ff), BF16), ((rows, ff), BF16), ((rows, width), BF16), ((rows, 128), F32),
    ]
    fixed = (wo, wup, wdown, vec, bup)

    def body(*refs):
        feed_forward(segment, 768, *refs)

    return pl_scratch(
        body, (items,), (count, tokens, mem, o) + fixed,
        [SCALARS, per_segment((seg, width), segment), memory_spec(mem), per_item((rows, width))] + [whole(w) for w in fixed],
        [per_segment((seg, width), segment)] + [per_item(d) for d, t in outs],
        [out_of(items, (segments, seg, width), BF16)] + [out_of(items, d, t) for d, t in outs],
        [pltpu.VMEM((rows, width), F32)],
        into={0: into} if into is not None else None,
        cost_estimate=pl.CostEstimate(flops=items * 2 * rows * width * (width + 2 * ff), bytes_accessed=items * rows * (width * 14 + ff * 4), transcendentals=0),
        name="feed_forward",
    )


def pl_scratch(body, grid, args, in_specs, out_specs, out_shape, scratch, into=None, **more):
    return launch(body, grid, args, in_specs, out_specs, out_shape, into=into, scratch_shapes=scratch, **more)


def call_feed_backward(segment, count, cot, dmem, xh2, sc2, gp, xh1, sc1, wup, wdown, vec):
    items, _, seg, width = cot.shape
    rows = xh2.shape[1]
    ff = wup.shape[1]
    outs = [((rows, width), BF16), ((rows, ff), BF16), ((rows, width), F32), ((rows, width), BF16), ((8, width), F32), ((1, ff), F32)]
    fixed = (wup, wdown, vec)

    def body(*refs):
        feed_backward(segment, 768, *refs)

    return pl_scratch(
        body, (items,), (count, cot, dmem, xh2, sc2, gp, xh1, sc1) + fixed,
        [SCALARS, per_segment((seg, width), segment)] + [per_item(a.shape[1:]) for a in (dmem, xh2, sc2, gp, xh1, sc1)] + [whole(w) for w in fixed],
        [per_item(d) for d, t in outs],
        [out_of(items, d, t) for d, t in outs],
        [pltpu.VMEM((rows, width), F32)],
        cost_estimate=pl.CostEstimate(flops=items * 4 * rows * width * ff, bytes_accessed=items * rows * (width * 14 + ff * 4), transcendentals=0),
        name="feed_backward",
    )


def call_attend_backward(segment, segments, seg, count, dmem, dr, db, q, k, v, e, o, li, wo, wq, wk, wv, first=0, many=None, into=None):
    items, rows, width = q.shape
    many = many or items
    outs = [((16, width), F32)] + [((rows, width), BF16)] * 3 + [((8, width), F32)]
    fixed = (wo, wq, wk, wv)

    def body(*refs):
        attend_backward(segment, first, *refs)

    return pl_scratch(
        body, (many,), (count, dmem, dr, db, q, k, v, e, o, li) + fixed,
        [SCALARS] + [per_item(a.shape[1:], first) for a in (dmem, dr, db, q, k, v, e, o, li)] + [whole(w) for w in fixed],
        [per_segment((seg, width), segment, first)] + [per_item(d, first) for d, t in outs],
        [out_of(items, (segments, seg, width), BF16)] + [out_of(items, d, t) for d, t in outs],
        [pltpu.VMEM((rows, width), BF16), pltpu.VMEM((rows, width), F32)],
        into=into,
        cost_estimate=pl.CostEstimate(flops=many * 2 * rows * width * (4 * width + 16 * rows), bytes_accessed=many * rows * (width * 24 + HEADS * rows * 2), transcendentals=0),
        name="attend_backward",
    )


def call_weight_product(lefts, rights, step_left, step_right, dtype):
    parts = len(lefts)
    items, rows, n_left = lefts[0].shape
    n_right = rights[0].shape[2]
    left_spec = pl.BlockSpec((items, rows, step_left), lambda i, j: (0, 0, i))
    right_spec = pl.BlockSpec((items, rows, step_right), lambda i, j: (0, 0, j))
    return pl.pallas_call(
        functools.partial(weight_product, parts),
        grid=(n_left // step_left, n_right // step_right),
        in_specs=[left_spec] * parts + [right_spec] * parts,
        out_specs=pl.BlockSpec((step_left, step_right), lambda i, j: (i, j)),
        out_shape=jax.ShapeDtypeStruct((n_left, n_right), dtype),
        compiler_params=params(),
        cost_estimate=pl.CostEstimate(flops=2 * parts * items * rows * n_left * n_right, bytes_accessed=2 * parts * items * rows * (n_left + n_right), transcendentals=0),
        name="weight_product",
    )(*lefts, *rights)


AXES = ("dp", "shard")
UNIT = 24


def spot(z, y, c, x):
    return ((z * 2 + y) * 2 + c) * 2 + x


def swap(array, dz, dy, dc, dx):
    pairs = [
        (spot(z, y, c, x), spot(z ^ dz, y ^ dy, c ^ dc, x ^ dx))
        for z in range(4)
        for y in range(2)
        for c in range(2)
        for x in range(2)
    ]
    return lax.ppermute(array, AXES, pairs)


def coordinates():
    dp = lax.axis_index("dp")
    return jnp.stack([dp // 4, dp // 2 % 2, dp % 2, lax.axis_index("shard")]).astype(jnp.int32)


def join(*parts):
    return jnp.concatenate(parts, axis=0)


def after(array, *others):
    return lax.optimization_barrier((array,) + others)[0]


def gather_z(unit):
    one, two, three = swap(unit, 1, 0, 0, 0), swap(unit, 2, 0, 0, 0), swap(unit, 3, 0, 0, 0)
    return jnp.stack([unit, one]), jnp.stack([two, three])


def gather_near(a, b):
    return join(a, swap(a, 0, 1, 0, 0)), join(b, swap(b, 0, 0, 0, 1))


def gather_far(a, b):
    return (a, swap(a, 0, 0, 0, 1), b, swap(b, 0, 1, 0, 0))


def gather_core(mine):
    return mine + tuple(swap(m, 0, 0, 1, 0) for m in mine)


def add_low(left, right):
    return (left.astype(F32) + right.astype(F32)).astype(BF16)


def reduce_core(keep, send):
    got = swap(send, 0, 0, 1, 0)
    send_a = add_low(keep[:2, :, 1], got[:2, :, 1])
    send_b = add_low(keep[2:, 1], got[2:, 1])
    return (send_a, send_b), (keep, got)


def reduce_far(sends, held):
    keep, got = held
    got_a = swap(sends[0], 0, 0, 0, 1)
    got_b = swap(sends[1], 0, 1, 0, 0)
    a = keep[:2, :, 0].astype(F32) + got[:2, :, 0].astype(F32) + got_a.astype(F32)
    b = keep[2:, 0].astype(F32) + got[2:, 0].astype(F32) + got_b.astype(F32)
    return (a[:, 1].astype(BF16), b[:, 1].astype(BF16)), (a[:, 0], b[:, 0])


def reduce_near(sends, held):
    a = held[0] + swap(sends[0], 0, 1, 0, 0).astype(F32)
    b = held[1] + swap(sends[1], 0, 0, 0, 1).astype(F32)
    return (a[1].astype(BF16), b[0].astype(BF16), b[1].astype(BF16)), a[0]


def reduce_z(sends, held):
    for step, array in enumerate(sends):
        held = held + swap(array, step + 1, 0, 0, 0).astype(F32)
    return held


def unit_pairs(me, bufs, emit):
    mz, my, mc, mx = me[0], me[1], me[2], me[3]
    flip = jnp.broadcast_to(mx, (8, 128)) == 1

    def send(dz, dy, dc, near, far):
        dp = ((mz ^ dz) * 2 + (my ^ dy)) * 2 + (mc ^ dc)
        emit(dp, near, far)

    for dc in range(2):
        a, a_far, b, b_far = bufs[4 * dc : 4 * dc + 4]
        for i in range(2):
            for j in range(2):
                send(j, i, dc, (a, 2 * i + j), (a_far, 2 * i + j))
        for i, buf in enumerate((b, b_far)):
            for j in range(2):
                send(2 + j, i, dc, (buf, j), (buf, 2 + j))


def pack_first(wq, wk, wv, vec, bup, out):
    blocks = [vec[8 * c : 8 * c + 8, :] for c in range(3)] + [jnp.broadcast_to(bup[...], (8, 128))]
    width = out.shape[1]
    tail = jnp.concatenate(blocks + [jnp.zeros((8, width - 512), F32)], axis=1)
    out[...] = jnp.concatenate([w[...].astype(F32) for w in (wq, wk, wv)] + [tail], axis=0).astype(BF16)


def assemble_first(me, *refs):
    bufs, (wq, wk, wv, vec, bup, small) = refs[:8], refs[8:]
    mx = me[3]

    def emit(dp, near, far):
        n = near[0][near[1]].astype(F32)
        f = far[0][far[1]].astype(F32)
        low = jnp.where(mx == 0, n, f)
        high = jnp.where(mx == 0, f, n)
        at = pl.ds(pl.multiple_of(dp * 48, 16), 48)
        for w, ref in enumerate((wq, wk, wv)):
            ref[at, :] = jnp.concatenate(
                [low[UNIT * w : UNIT * (w + 1)], high[UNIT * w : UNIT * (w + 1)]], axis=0
            ).astype(BF16)
        for x, rows in enumerate((low, high)):
            for c in range(4):
                small[dp * 2 + x, 8 * c : 8 * c + 8, :] = rows[3 * UNIT :, 128 * c : 128 * c + 128]

    unit_pairs(me, bufs, emit)
    for idx in range(small.shape[0]):
        vec[0, :, UNIT * idx : UNIT * (idx + 1)] = small[idx, :24, :UNIT]
        bup[:, 4 * UNIT * idx : 4 * UNIT * (idx + 1)] = small[idx, 24:25, : 4 * UNIT]


def assemble_rest(units, wo, wup, wdown):
    count = units.shape[0]
    width = wo.shape[1]
    for w in range(5):
        rows = jnp.concatenate([units[i, w].astype(F32) for i in range(count)], axis=0).astype(BF16)
        if w == 0:
            wo[...] = rows
        else:
            wup[:, (w - 1) * width : w * width] = rows
    for i in range(0, count):
        rows = jnp.concatenate([units[i, w].astype(F32) for w in range(5, 9)], axis=0)
        wdown[4 * UNIT * i : 4 * UNIT * (i + 1), :] = rows.astype(BF16)


def call_assemble_rest(units, ff):
    devices, blocks, rows, width = units.shape
    step = 8
    return pl.pallas_call(
        assemble_rest,
        grid=(devices // step,),
        in_specs=[pl.BlockSpec((step, blocks, rows, width), lambda i: (i, 0, 0, 0))],
        out_specs=[
            pl.BlockSpec((step * rows, width), lambda i: (i, 0)),
            pl.BlockSpec((step * rows, ff), lambda i: (i, 0)),
            pl.BlockSpec((step * rows * 4, width), lambda i: (i, 0)),
        ],
        out_shape=[jax.ShapeDtypeStruct(d, BF16) for d in ((width, width), (width, ff), (ff, width))],
        compiler_params=params(),
        name="assemble_rest",
    )(units)


def call_pack_first(wq, wk, wv, vec, bup):
    return pl.pallas_call(
        pack_first, out_shape=jax.ShapeDtypeStruct((3 * UNIT + 8, wq.shape[1]), BF16), name="pack_first"
    )(wq, wk, wv, vec, bup)


def call_assemble(body, me, bufs, outs, name, scratch=()):
    vm = pl.BlockSpec(memory_space=pltpu.VMEM)
    return pl.pallas_call(
        body,
        in_specs=[SCALARS] + [vm] * 8,
        out_specs=[vm] * len(outs),
        out_shape=[jax.ShapeDtypeStruct(d, t) for d, t in outs],
        scratch_shapes=list(scratch),
        compiler_params=params(),
        name=name,
    )(me, *bufs)


def emit_units(me, keep, send, value_of):
    mz, my, mc, mx = me[0], me[1], me[2], me[3]
    for core in range(2):

        @pl.when(mc == core)
        def _():
            for z in range(4):
                for y in range(2):
                    for x in range(2):
                        to = (z ^ mz, y ^ my, x ^ mx)
                        keep[to] = value_of(z, y, core, x)
                        send[to] = value_of(z, y, 1 - core, x)


def product_sum(lefts, rights):
    total = None
    for left, right in zip(lefts, rights):
        for i in range(left.shape[0]):
            term = dot_tn(left[i], right[i])
            total = term if total is None else total + term
    return total


def product_up(segments, me, *refs):
    o, db, h, du = (refs[segments * i : segments * (i + 1)] for i in range(4))
    keep, send, acc = refs[4 * segments :]

    @pl.when(pl.program_id(0) == 0)
    def _():
        acc[...] = product_sum(o, db)

    @pl.when(pl.program_id(0) > 0)
    def _():
        acc[...] = product_sum(h, du)

    def value_of(*at):
        idx = spot(*at)
        return acc[UNIT * idx : UNIT * (idx + 1), :].astype(BF16)

    emit_units(me, keep.at[:, :, :, 0], send.at[:, :, :, 0], value_of)


def product_down(segments, me, *refs):
    a, df = refs[:segments], refs[segments : 2 * segments]
    keep, send, acc = refs[2 * segments :]
    tall = 4 * UNIT
    acc[...] = product_sum(a, df)
    my, mc, mx = me[1], me[2], me[3]
    for core in range(2):

        @pl.when(mc == core)
        def _():
            for y in range(2):
                for x in range(2):
                    for ref, c in ((keep, core), (send, 1 - core)):
                        row = ((y * 2 + c) * 2 + x) * tall
                        ref[0, y ^ my, x ^ mx] = acc[row : row + tall, :].astype(BF16)


def product_first(segments, me, *refs):
    vat, vec, vup = (refs[segments * i : segments * (i + 1)] for i in range(3))
    dmem = refs[3 * segments]
    refs = refs[3 * segments + 1 :]
    x, dq, dk, dv = (refs[segments * i : segments * (i + 1)] for i in range(4))
    keep, send, acc, vec_s, bup_s = refs[4 * segments :]
    step = pl.program_id(0)

    for w, right in enumerate((dq, dk, dv)):
        term = product_sum(x, right)

        @pl.when(step == 0)
        def _():
            acc[w] = term

        @pl.when(step > 0)
        def _():
            acc[w] += term

    @pl.when(step == pl.num_programs(0) - 1)
    def _():
        vat_sum = sum(v[...].sum(axis=0) for v in vat)
        vec_sum = sum(v[...].sum(axis=0) for v in vec)
        vec_s[...] = jnp.zeros_like(vec_s)
        vec_s[0:16, :] = dmem[...].sum(axis=0)
        vec_s[0:2, :] = vat_sum[0:2]
        vec_s[2:6, :] = vec_sum[0:4]
        vec_s[16:18, :] = vec_sum[4:6]
        bup_s[...] = sum(v[...].sum(axis=0) for v in vup)
        width = acc.shape[2]
        blank = jnp.zeros((8, width - 512), F32)

        def turned(array, shift):
            return array if shift == 0 else pltpu.roll(array, array.shape[1] - shift, 1)

        def value_of(*at):
            idx = spot(*at)
            rows = [acc[w, UNIT * idx : UNIT * (idx + 1), :] for w in range(3)]
            vectors = turned(vec_s[...], UNIT * idx)[:, :128]
            hidden = turned(jnp.broadcast_to(bup_s[...], (8, bup_s.shape[1])), 4 * UNIT * idx)[:, :128]
            tail = jnp.concatenate([vectors[0:8], vectors[8:16], vectors[16:24], hidden, blank], axis=1)
            return jnp.concatenate(rows + [tail], axis=0).astype(BF16)

        emit_units(me, keep, send, value_of)


def call_product_up(me, o, db, h, du):
    segments = len(o)
    items, rows, width = o[0].shape
    ff = du[0].shape[2]
    steps = ff // width
    fixed = [pl.BlockSpec((items, rows, width), lambda j, m: (0, 0, 0), pipeline_mode=pl.Buffered(1))] * (3 * segments)
    moving = [pl.BlockSpec((items, rows, width), lambda j, m: (0, 0, jnp.maximum(j - 1, 0)))] * segments
    dims = (4, 2, 2, steps + 1, UNIT, width)
    out = pl.BlockSpec((4, 2, 2, 1, UNIT, width), lambda j, m: (0, 0, 0, j, 0, 0))
    return pl.pallas_call(
        functools.partial(product_up, segments),
        grid_spec=pltpu.PrefetchScalarGridSpec(
            num_scalar_prefetch=1,
            grid=(steps + 1,),
            in_specs=fixed + moving,
            out_specs=[out, out],
            scratch_shapes=[pltpu.VMEM((width, width), F32)],
        ),
        out_shape=[jax.ShapeDtypeStruct(dims, BF16)] * 2,
        compiler_params=params(),
        cost_estimate=pl.CostEstimate(flops=2 * segments * items * rows * width * (ff + width), bytes_accessed=2 * segments * items * rows * (ff + 3 * width) + 2 * width * (ff + width), transcendentals=0),
        name="product_up",
    )(me, *o, *db, *h, *du)


def call_product_down(me, a, df):
    segments = len(a)
    items, rows, width = df[0].shape
    ff = a[0].shape[2]
    moving = [pl.BlockSpec((items, rows, ff // 4), lambda j, m: (0, 0, j ^ m[0]))] * segments
    fixed = [pl.BlockSpec((items, rows, width), lambda j, m: (0, 0, 0), pipeline_mode=pl.Buffered(1))] * segments
    dims = (4, 2, 2, 4 * UNIT, width)
    out = pl.BlockSpec((1, 2, 2, 4 * UNIT, width), lambda j, m: (j, 0, 0, 0, 0))
    return pl.pallas_call(
        functools.partial(product_down, segments),
        grid_spec=pltpu.PrefetchScalarGridSpec(
            num_scalar_prefetch=1,
            grid=(4,),
            in_specs=moving + fixed,
            out_specs=[out, out],
            scratch_shapes=[pltpu.VMEM((ff // 4, width), F32)],
        ),
        out_shape=[jax.ShapeDtypeStruct(dims, BF16)] * 2,
        compiler_params=params(),
        cost_estimate=pl.CostEstimate(flops=2 * segments * items * rows * width * ff, bytes_accessed=2 * segments * items * rows * (ff + width) + 2 * width * ff, transcendentals=0),
        name="product_down",
    )(me, *a, *df)


def call_product_first(me, vat, vec, vup, dmem, x, dq, dk, dv):
    segments = len(x)
    items, rows, width = x[0].shape
    fixed = (*vat, *vec, *vup, dmem)
    moving = [pl.BlockSpec((1, rows, width), lambda j, m: (j, 0, 0))] * (4 * segments)
    tall = 3 * UNIT + 8
    dims = (4, 2, 2, tall, width)
    out = pl.BlockSpec(dims, lambda j, m: (0,) * 5, pipeline_mode=pl.Buffered(1))
    return pl.pallas_call(
        functools.partial(product_first, segments),
        grid_spec=pltpu.PrefetchScalarGridSpec(
            num_scalar_prefetch=1,
            grid=(items,),
            in_specs=[whole(a) for a in fixed] + moving,
            out_specs=[out, out],
            scratch_shapes=[
                pltpu.VMEM((3, width, width), F32),
                pltpu.VMEM((24, width), F32),
                pltpu.VMEM(vup[0].shape[1:], F32),
            ],
        ),
        out_shape=[jax.ShapeDtypeStruct(dims, BF16)] * 2,
        compiler_params=params(),
        cost_estimate=pl.CostEstimate(flops=6 * segments * items * rows * width * width, bytes_accessed=8 * segments * items * rows * width + 6 * width * width, transcendentals=0),
        name="product_first",
    )(me, *fixed, *x, *dq, *dk, *dv)


def shown(array):
    return lax.optimization_barrier(array.transpose(0, 2, 1, 3))


def gather_weights(me, shards):
    mem, wq, wk, wv, wo, wup, wdown, bq, bv, bo, bup, bdown, g1, s1, g2, s2 = shards
    width = wq.shape[1]
    ff = wup.shape[1]
    vec = jnp.concatenate([jnp.stack([bq, bv, bo, bdown, g1, s1]), mem.T, jnp.stack([g2, s2])], axis=0)
    vec = jnp.pad(vec, ((0, 6), (0, 128 - UNIT))).astype(F32)
    hidden = jnp.pad(bup[None], ((0, 0), (0, 128 - 4 * UNIT))).astype(F32)
    up_blocks = wup.reshape(UNIT, ff // width, width).transpose(1, 0, 2)
    units = jnp.concatenate([wo[None], up_blocks, wdown.reshape(4, UNIT, width)], axis=0)
    units = lax.all_gather(units, AXES, axis=0)
    first = gather_core(gather_far(*gather_near(*gather_z(call_pack_first(wq, wk, wv, vec, hidden)))))
    square = ((width, width), BF16)
    wq, wk, wv, vec, bup = call_assemble(
        assemble_first, me, first, [square] * 3 + [((1, 24, width), F32), ((1, ff), F32)],
        "assemble_first", [pltpu.VMEM((width // UNIT, 32, 128), F32)],
    )
    return (wq, wk, wv, vec, bup), units


def gather_plain(shards):
    mem, wq, wk, wv, wo, wup, wdown, bq, bv, bo, bup, bdown, g1, s1, g2, s2 = [
        lax.all_gather(a, AXES, axis=0, tiled=True) for a in shards
    ]
    rows = [bq, bv, bo, bdown, g1, s1, mem.T, g2, s2]
    vectors = jnp.concatenate([r.reshape(-1, wq.shape[1]) for r in rows], axis=0).astype(F32)
    vectors = jnp.pad(vectors, ((0, 6), (0, 0)))[None]
    return (wq, wk, wv, vectors, bup.astype(F32)[None, :]), (wo, wup, wdown)


def reduce_plain(pieces, vat, vec, vup, dmem):
    x, o, db, h, du, a, df, dq, dk, dv = pieces
    vat = sum(v.sum(axis=0) for v in vat)
    vec = sum(v.sum(axis=0) for v in vec)
    gq = call_weight_product(x, dq, 768, 256, F32)
    gk = call_weight_product(x, dk, 768, 256, F32)
    gv = call_weight_product(x, dv, 768, 256, F32)
    go = call_weight_product(o, db, 768, 256, F32)
    gup = call_weight_product(h, du, 768, 256, F32)
    gdown = call_weight_product(a, df, 256, 768, F32)
    terms = (dmem.sum(axis=0)[6:16].T, gq, gk, gv, go, gup, gdown, sum(v.sum(axis=(0, 1)) for v in vup))
    terms += (vat[0], vat[1]) + tuple(vec[i] for i in range(6))
    owned = lax.psum_scatter(terms, AXES, scatter_dimension=0, tiled=True)
    mem, gq, gk, gv, go, gup, gdown, bup, bq, bv, bo, bdown, g1, s1, g2, s2 = owned
    return mem, gq, gk, gv, go, gup, gdown, bq, bv, bo, bup, bdown, g1, s1, g2, s2


def local(*args):
    tokens, segment_count = args[:2]
    shards = args[2:18]
    cotangent, memory_cotangent = args[18:]
    items, segments, seg, width = tokens.shape
    pad = 16 - shards[0].shape[1]
    planned = lax.axis_size("dp") == 16 and lax.axis_size("shard") == 2
    me = coordinates()
    gathered = gather_weights(me, shards) if planned else gather_plain(shards)
    (wq, wk, wv, vec, bup), rest = gathered
    mem = vec
    saved = []
    y = None
    for s in range(segments):
        part = call_attend_forward(s, tokens, mem, wq, wk, wv, vec)
        if s == 0:
            if planned:
                rest = call_assemble_rest(after(rest, part[0]), 4 * width)
            wo, wup, wdown = rest
        o = part[5]
        y, mem, *more = call_feed_forward(s, segment_count, tokens, mem, o, wo, wup, wdown, vec, bup, y)
        saved.append((*part, *more))
    memory_final = mem[:, pad:].astype(BF16)
    dmem = jnp.pad(memory_cotangent.astype(F32), ((0, 0), (pad, 0), (0, 0)))
    tg = None
    pieces = [None] * segments
    vecs, vups, vats = [], [], []
    for s in reversed(range(segments)):
        x, q, k, v, e, o, li, xh1, sc1, h, a, gp, xh2, sc2 = saved[s]
        df, du, dr, db, vec_s, vup_s = call_feed_backward(
            s, segment_count, cotangent, dmem, xh2, sc2, gp, xh1, sc1, wup, wdown, vec
        )
        pieces[s] = (x, o, db, h, du, a, df)
        vecs.append(vec_s)
        vups.append(vup_s)
        into = {} if tg is None else {0: tg}
        back = functools.partial(call_attend_backward, s, segments, seg)
        tail = (q, k, v, e, o, li, wo, wq, wk, wv)
        if s > 0 or not planned:
            tg, dmem, dq, dk, dv, vat_s = back(segment_count, dmem, dr, db, *tail, into=into)
        else:
            o_all, db_all, h_all, du_all, a_all, df_all = list(zip(*pieces))[1:]
            down = call_weight_product(a_all, df_all, 768, 768, BF16)
            o_all = (after(o_all[0], down),) + tuple(o_all[1:])
            down = lax.psum_scatter(down, AXES, scatter_dimension=0, tiled=True).astype(F32)
            up = reduce_core(*call_product_up(me, o_all, db_all, h_all, du_all))
            gate = up[0]
            up_far = reduce_far(*up)
            part = back(segment_count, dmem, after(dr, *gate), db, *tail, first=0, many=1, into=into)
            for item in range(1, items):
                part = back(
                    segment_count, dmem, after(dr, part[1], *up_far[0]), db, *tail,
                    first=item, many=1, into=dict(enumerate(part)),
                )
            tg, dmem, dq, dk, dv, vat_s = part
            up_near = reduce_near(*up_far)
        pieces[s] += (dq, dk, dv)
        vats.append(vat_s)
    pieces = tuple(zip(*pieces))
    if planned:
        x, dq, dk, dv = pieces[0], *pieces[7:]
        x = (after(x[0], *up_near[0]),) + x[1:]
        first = reduce_core(*call_product_first(me, vats, vecs, vups, dmem, x, dq, dk, dv))
        up = reduce_z(*up_near)
        y = shown(after(y, *first[0]))
        first = reduce_far(*first)
        tg = shown(after(tg, *first[0]))
        sends, held = reduce_near(*first)
        sends, y, tg = lax.optimization_barrier((sends, y, tg))
        first = reduce_z(sends, held)
        y, tg = y.transpose(0, 2, 1, 3), tg.transpose(0, 2, 1, 3)
        gq, gk, gv = [first[UNIT * w : UNIT * (w + 1)] for w in range(3)]
        tail = first[3 * UNIT :]
        per = jnp.concatenate([tail[:, 128 * c : 128 * c + UNIT] for c in range(3)], axis=0)
        bq, bv, bo, bdown, g1, s1 = [per[i] for i in range(6)]
        owned = (
            per[6:16].T, gq, gk, gv, up[0], up[1:].transpose(1, 0, 2).reshape(UNIT, -1), down, bq, bv, bo,
            tail[0, 384 : 384 + 4 * UNIT], bdown, g1, s1, per[16], per[17],
        )
    else:
        owned = reduce_plain(pieces, vats, vecs, vups, dmem)
    return (y, memory_final, tg) + tuple(owned)


def solution(mesh):
    rows = P(("dp", "shard"))
    return jax.shard_map(local, mesh=mesh, in_specs=(rows,) * 20, out_specs=(rows,) * 19, check_vma=False)
```

```python
import functools

import jax
import jax.numpy as jnp
from jax import lax
from jax.experimental import pallas as pl
from jax.experimental.pallas import tpu as pltpu
from jax.sharding import PartitionSpec as P

F32 = jnp.float32
BF16 = jnp.bfloat16
HEADS = 12
HEAD_DIM = 64
NORM_EPS = 1e-06
ROOT_HALF = 0.7071067811865476
ROOT_TWO_PI = 0.3989422804014327


def dot_nn(left, right):
    return jnp.dot(left, right, preferred_element_type=F32)


def dot_nt(left, right):
    return lax.dot_general(left, right, (((1,), (1,)), ((), ())), preferred_element_type=F32)


def dot_tn(left, right):
    return lax.dot_general(left, right, (((0,), (0,)), ((), ())), preferred_element_type=F32)


def lane_masks(rows):
    lane = lax.broadcasted_iota(jnp.int32, (rows, 128), 1)
    first = jnp.where(lane < HEAD_DIM, 1.0, 0.0)
    return first, 1.0 - first


def key_counts(rows, tokens):
    row = lax.broadcasted_iota(jnp.int32, (rows, 128), 0)
    return jnp.where(row < tokens, 1.0, 2.0)


def gelu_parts(u):
    bell = jnp.exp(u * u * -0.5)
    t = pl.reciprocal(1.0 + (0.3275911 * ROOT_HALF) * jnp.abs(u))
    poly = t * (
        0.5 * 0.254829592
        + t * (0.5 * -0.284496736 + t * (0.5 * 1.421413741 + t * (0.5 * -1.453152027 + t * (0.5 * 1.061405429))))
    )
    tail = poly * bell
    cdf = jnp.where(u < 0.0, tail, 1.0 - tail)
    return u * cdf, cdf + u * bell * ROOT_TWO_PI


def attend_forward(tok, mem, wq, wk, wv, vec, x_o, q_o, k_o, v_o, e_o, o_o, li_o):
    bq, bv = vec[0, 0:1, :], vec[0, 1:2, :]
    seg = tok.shape[2]
    rows = x_o.shape[1]
    x_o[0, rows - 16 :, :] = mem[0].astype(BF16)
    x_o[0, :seg, :] = tok[0, 0]
    x = x_o[0]
    q_o[0] = ((dot_nn(x, wq[...]) + bq).astype(BF16).astype(F32) * 0.125).astype(BF16)
    k_o[0] = dot_nn(x, wk[...]).astype(BF16)
    v_o[0] = (dot_nn(x, wv[...]) + bv).astype(BF16)
    masks = lane_masks(rows)
    count = key_counts(rows, seg)
    low_masks = tuple(m.astype(BF16) for m in masks)

    def pair(p, carry):
        at = pl.ds(pl.multiple_of(p * 128, 128), 128)
        q2 = q_o[0, :, at]
        k2 = k_o[0, :, at]
        v2 = v_o[0, :, at].astype(F32) * count
        total = None
        for h in range(2):
            s = dot_nt(q2 * low_masks[h], k2)
            e = jnp.exp(s - jnp.max(s, axis=-1, keepdims=True)).astype(BF16)
            e_o[0, 2 * p + h] = e
            right = jnp.concatenate(
                [(v2 * masks[h]).astype(BF16), (count * masks[h]).astype(BF16)], axis=1
            )
            part = dot_nn(e, right)
            total = part if total is None else total + part
        inv = 1.0 / total[:, 128:]
        li_o[0, :, at] = inv
        o_o[0, :, at] = (total[:, :128] * inv).astype(BF16)
        return carry

    lax.fori_loop(0, HEADS // 2, pair, 0, unroll=True)


def norm_rows(r):
    mean = jnp.mean(r, axis=-1, keepdims=True)
    center = r - mean
    var = jnp.mean(center * center, axis=-1, keepdims=True)
    scale = lax.rsqrt(var + NORM_EPS)
    return center * scale, scale


def feed_forward(
    segment, step,
    count, tok, mem, o, wo, wup, wdown, vec, bup,
    y_o, mem_o, xh1_o, sc1_o, h_o, a_o, gp_o, xh2_o, sc2_o, x_s,
):
    seg = tok.shape[2]
    rows = o.shape[1]
    ff = wup.shape[1]
    bo, bdown, g1, s1, g2, s2 = (vec[0, r : r + 1, :] for r in (2, 3, 4, 5, 16, 17))
    x_s[rows - 16 :, :] = mem[0]
    x_s[:seg, :] = tok[0, 0].astype(F32)
    xh, sc = norm_rows(x_s[...] + dot_nn(o[0], wo[...]) + bo)
    xh1_o[0] = xh.astype(BF16)
    sc1_o[0] = jnp.broadcast_to(sc, (rows, 128))
    h1 = xh * g1 + s1
    h_o[0] = h1.astype(BF16)
    x_s[...] = h1 + bdown

    def chunk(j, carry):
        at = pl.ds(pl.multiple_of(j * step, step), step)
        act, slope = gelu_parts(dot_nn(h_o[0], wup[:, at]) + bup[:, at])
        a_o[0, :, at] = act.astype(BF16)
        gp_o[0, :, at] = slope.astype(BF16)
        x_s[...] += dot_nn(a_o[0, :, at], wdown[at, :])
        return carry

    lax.fori_loop(0, ff // step, chunk, 0, unroll=True)
    xh, sc = norm_rows(x_s[...])
    xh2_o[0] = xh.astype(BF16)
    sc2_o[0] = jnp.broadcast_to(sc, (rows, 128))
    x_s[...] = xh * g2 + s2
    active = count[pl.program_id(0)] > segment
    y_o[0, 0] = jnp.where(active, x_s[:seg, :], 0.0).astype(BF16)
    mem_o[0] = jnp.where(active, x_s[rows - 16 :, :], mem[0])


def norm_back(dy, xh, sc, gain):
    dxh = dy * gain
    m1 = jnp.mean(dxh, axis=-1, keepdims=True)
    m2 = jnp.mean(dxh * xh, axis=-1, keepdims=True)
    return sc * (dxh - m1 - xh * m2)


def col_sum(x):
    return jnp.sum(x, axis=0, keepdims=True)


def feed_backward(
    segment, step,
    count, cot, dmem, xh2, sc2, gp, xh1, sc1, wup, wdown, vec,
    df_o, du_o, dr_o, db_o, vec_o, vup_o, x_s,
):
    seg = cot.shape[2]
    rows = xh2.shape[1]
    ff = wup.shape[1]
    g1, g2 = vec[0, 4:5, :], vec[0, 16:17, :]
    active = jnp.where(count[pl.program_id(0)] > segment, 1.0, 0.0)
    x_s[rows - 16 :, :] = dmem[0] * active
    x_s[:seg, :] = cot[0, 0].astype(F32) * active
    dy = x_s[...]
    xh = xh2[0].astype(F32)
    vec_o[0, 4:5, :] = col_sum(dy * xh)
    vec_o[0, 5:6, :] = col_sum(dy)
    dr = norm_back(dy, xh, sc2[0, :, :1], g2)
    df = dr.astype(BF16)
    df_o[0] = df
    vec_o[0, 1:2, :] = col_sum(df.astype(F32))
    x_s[...] = dr

    def chunk(j, carry):
        at = pl.ds(pl.multiple_of(j * step, step), step)
        du = dot_nt(df_o[0], wdown[at, :]) * gp[0, :, at].astype(F32)
        vup_o[0, :, at] = col_sum(du)
        du_o[0, :, at] = du.astype(BF16)
        x_s[...] += dot_nt(du_o[0, :, at], wup[:, at])
        return carry

    lax.fori_loop(0, ff // step, chunk, 0, unroll=True)
    dh = x_s[...]
    xh = xh1[0].astype(F32)
    vec_o[0, 2:3, :] = col_sum(dh * xh)
    vec_o[0, 3:4, :] = col_sum(dh)
    dr = norm_back(dh, xh, sc1[0, :, :1], g1)
    dr_o[0] = dr
    db_o[0] = dr.astype(BF16)
    vec_o[0, 0:1, :] = col_sum(dr)


def attend_backward(
    segment, first,
    count, dmem, dr, db, q, k, v, e, o, li, wo, wq, wk, wv,
    tg_o, dmem_o, dq_o, dk_o, dv_o, vec_o, do_s, x_s,
):
    seg = tg_o.shape[2]
    rows = q.shape[1]
    do_s[...] = dot_nt(db[0], wo[...]).astype(BF16)
    masks = lane_masks(rows)
    count2 = key_counts(rows, seg)
    low_masks = tuple(m.astype(BF16) for m in masks)
    ones = jnp.ones((rows, 128), BF16)

    def pair(p, carry):
        at = pl.ds(pl.multiple_of(p * 128, 128), 128)
        dop = do_s[:, at].astype(F32) * li[0, :, at]
        pr = (dop * o[0, :, at].astype(F32) * -1.0).astype(BF16)
        dop = dop.astype(BF16)
        q2 = q[0, :, at]
        k2 = (k[0, :, at].astype(F32) * (count2 * 0.125)).astype(BF16)
        right = jnp.concatenate([v[0, :, at], ones], axis=1)
        d_turned = dop.T
        q_turned = q2.T
        dq = None
        dk, dv = [], []
        for h in range(2):
            e_h = e[0, 2 * p + h]
            left = jnp.concatenate([dop * low_masks[h], pr * low_masks[h]], axis=1)
            ds = (e_h.astype(F32) * dot_nt(left, right)).astype(BF16)
            q_t = dot_nn(ds, k2 * low_masks[h])
            dq = q_t if dq is None else dq + q_t
            own = slice(HEAD_DIM * h, HEAD_DIM * (h + 1))
            dk.append(dot_nn(q_turned[own], ds))
            dv.append(dot_nn(d_turned[own], e_h))
        dq_o[0, :, at] = dq.astype(BF16)
        dk_o[0, :, at] = (jnp.concatenate(dk, axis=0).T * count2).astype(BF16)
        dv_o[0, :, at] = (jnp.concatenate(dv, axis=0).T * count2).astype(BF16)
        return carry

    lax.fori_loop(0, HEADS // 2, pair, 0, unroll=True)
    vec_o[0, 0:1, :] = col_sum(dq_o[0].astype(F32))
    vec_o[0, 1:2, :] = col_sum(dv_o[0].astype(F32))
    x_s[...] = (
        dr[0]
        + dot_nt(dq_o[0], wq[...])
        + dot_nt(dk_o[0], wk[...])
        + dot_nt(dv_o[0], wv[...])
    )
    tg_o[0, 0] = x_s[:seg, :].astype(BF16)
    kept = jnp.where(count[pl.program_id(0) + first] > segment, 0.0, 1.0)
    dmem_o[0] = dmem[0] * kept + x_s[rows - 16 :, :]


def weight_product(parts, *refs):
    lefts = refs[:parts]
    rights = refs[parts : 2 * parts]
    out = refs[2 * parts]
    total = None
    for left, right in zip(lefts, rights):
        for i in range(left.shape[0]):
            term = dot_tn(left[i], right[i])
            total = term if total is None else total + term
    out[...] = total.astype(out.dtype)


def whole(array):
    dims = array.shape
    return pl.BlockSpec(dims, lambda *g: (0,) * len(dims), pipeline_mode=pl.Buffered(1))


def per_item(dims, first=0):
    return pl.BlockSpec((1,) + dims, lambda i: (i + first,) + (0,) * len(dims))


def per_segment(dims, segment, first=0):
    return pl.BlockSpec((1, 1) + dims, lambda i: (i + first, segment) + (0,) * len(dims))


def memory_spec(array, first=0):
    shared = array.shape[0] == 1
    return pl.BlockSpec((1, 16, array.shape[2]), lambda i: (0 if shared else i + first, 0, 0))


def out_of(items, dims, dtype):
    return jax.ShapeDtypeStruct((items,) + dims, dtype)


SCALARS = pl.BlockSpec(memory_space=pltpu.SMEM)


def params(mib=60):
    return pltpu.CompilerParams(vmem_limit_bytes=mib << 20)


def launch(body, grid, args, in_specs, out_specs, out_shape, into=None, mib=60, **more):
    into = into or {}
    n_in = len(args)
    aliases = {n_in + k: o for k, o in enumerate(into)}

    def run(*refs):
        body(*refs[:n_in], *refs[n_in + len(into) :])

    return pl.pallas_call(
        run if into else body,
        grid=grid,
        in_specs=list(in_specs) + [pl.BlockSpec(memory_space=pl.ANY)] * len(into),
        out_specs=out_specs,
        out_shape=out_shape,
        input_output_aliases=aliases,
        compiler_params=params(mib),
        **more,
    )(*args, *into.values())


def call_attend_forward(segment, tokens, mem, wq, wk, wv, vec, first=0, many=None, into=None):
    items, _, seg, width = tokens.shape
    many = many or items
    rows = seg + 10
    outs = [((rows, width), BF16)] * 4 + [((HEADS, rows, rows), BF16), ((rows, width), BF16), ((rows, width), F32)]
    return launch(
        attend_forward,
        (many,),
        (tokens, mem, wq, wk, wv, vec),
        [per_segment((seg, width), segment, first), memory_spec(mem, first)] + [whole(w) for w in (wq, wk, wv, vec)],
        [per_item(d, first) for d, t in outs],
        [out_of(items, d, t) for d, t in outs],
        into=dict(enumerate(into)) if into else None,
        cost_estimate=pl.CostEstimate(flops=many * 2 * rows * (3 * width * width + 8 * rows * width), bytes_accessed=many * rows * (width * 14 + HEADS * rows * 2), transcendentals=0),
        name="attend_forward",
    )


def call_feed_forward(segment, count, tokens, mem, o, wo, wup, wdown, vec, bup, into=None):
    items, segments, seg, width = tokens.shape
    rows = o.shape[1]
    ff = wup.shape[1]
    outs = [
        ((16, width), F32), ((rows, width), BF16), ((rows, 128), F32), ((rows, width), BF16),
        ((rows, ff), BF16), ((rows, ff), BF16), ((rows, width), BF16), ((rows, 128), F32),
    ]
    fixed = (wo, wup, wdown, vec, bup)

    def body(*refs):
        feed_forward(segment, 768, *refs)

    return pl_scratch(
        body, (items,), (count, tokens, mem, o) + fixed,
        [SCALARS, per_segment((seg, width), segment), memory_spec(mem), per_item((rows, width))] + [whole(w) for w in fixed],
        [per_segment((seg, width), segment)] + [per_item(d) for d, t in outs],
        [out_of(items, (segments, seg, width), BF16)] + [out_of(items, d, t) for d, t in outs],
        [pltpu.VMEM((rows, width), F32)],
        into={0: into} if into is not None else None,
        cost_estimate=pl.CostEstimate(flops=items * 2 * rows * width * (width + 2 * ff), bytes_accessed=items * rows * (width * 14 + ff * 4), transcendentals=0),
        name="feed_forward",
    )


def pl_scratch(body, grid, args, in_specs, out_specs, out_shape, scratch, into=None, **more):
    return launch(body, grid, args, in_specs, out_specs, out_shape, into=into, scratch_shapes=scratch, **more)


def call_feed_backward(segment, count, cot, dmem, xh2, sc2, gp, xh1, sc1, wup, wdown, vec):
    items, _, seg, width = cot.shape
    rows = xh2.shape[1]
    ff = wup.shape[1]
    outs = [((rows, width), BF16), ((rows, ff), BF16), ((rows, width), F32), ((rows, width), BF16), ((8, width), F32), ((1, ff), F32)]
    fixed = (wup, wdown, vec)

    def body(*refs):
        feed_backward(segment, 768, *refs)

    return pl_scratch(
        body, (items,), (count, cot, dmem, xh2, sc2, gp, xh1, sc1) + fixed,
        [SCALARS, per_segment((seg, width), segment)] + [per_item(a.shape[1:]) for a in (dmem, xh2, sc2, gp, xh1, sc1)] + [whole(w) for w in fixed],
        [per_item(d) for d, t in outs],
        [out_of(items, d, t) for d, t in outs],
        [pltpu.VMEM((rows, width), F32)],
        cost_estimate=pl.CostEstimate(flops=items * 4 * rows * width * ff, bytes_accessed=items * rows * (width * 14 + ff * 4), transcendentals=0),
        name="feed_backward",
    )


def call_attend_backward(segment, segments, seg, count, dmem, dr, db, q, k, v, e, o, li, wo, wq, wk, wv, first=0, many=None, into=None):
    items, rows, width = q.shape
    many = many or items
    outs = [((16, width), F32)] + [((rows, width), BF16)] * 3 + [((8, width), F32)]
    fixed = (wo, wq, wk, wv)

    def body(*refs):
        attend_backward(segment, first, *refs)

    return pl_scratch(
        body, (many,), (count, dmem, dr, db, q, k, v, e, o, li) + fixed,
        [SCALARS] + [per_item(a.shape[1:], first) for a in (dmem, dr, db, q, k, v, e, o, li)] + [whole(w) for w in fixed],
        [per_segment((seg, width), segment, first)] + [per_item(d, first) for d, t in outs],
        [out_of(items, (segments, seg, width), BF16)] + [out_of(items, d, t) for d, t in outs],
        [pltpu.VMEM((rows, width), BF16), pltpu.VMEM((rows, width), F32)],
        into=into,
        cost_estimate=pl.CostEstimate(flops=many * 2 * rows * width * (4 * width + 16 * rows), bytes_accessed=many * rows * (width * 24 + HEADS * rows * 2), transcendentals=0),
        name="attend_backward",
    )


def call_weight_product(lefts, rights, step_left, step_right, dtype):
    parts = len(lefts)
    items, rows, n_left = lefts[0].shape
    n_right = rights[0].shape[2]
    left_spec = pl.BlockSpec((items, rows, step_left), lambda i, j: (0, 0, i))
    right_spec = pl.BlockSpec((items, rows, step_right), lambda i, j: (0, 0, j))
    return pl.pallas_call(
        functools.partial(weight_product, parts),
        grid=(n_left // step_left, n_right // step_right),
        in_specs=[left_spec] * parts + [right_spec] * parts,
        out_specs=pl.BlockSpec((step_left, step_right), lambda i, j: (i, j)),
        out_shape=jax.ShapeDtypeStruct((n_left, n_right), dtype),
        compiler_params=params(),
        cost_estimate=pl.CostEstimate(flops=2 * parts * items * rows * n_left * n_right, bytes_accessed=2 * parts * items * rows * (n_left + n_right), transcendentals=0),
        name="weight_product",
    )(*lefts, *rights)


AXES = ("dp", "shard")
UNIT = 24


def spot(z, y, c, x):
    return ((z * 2 + y) * 2 + c) * 2 + x


def swap(array, dz, dy, dc, dx):
    pairs = [
        (spot(z, y, c, x), spot(z ^ dz, y ^ dy, c ^ dc, x ^ dx))
        for z in range(4)
        for y in range(2)
        for c in range(2)
        for x in range(2)
    ]
    return lax.ppermute(array, AXES, pairs)


def coordinates():
    dp = lax.axis_index("dp")
    return jnp.stack([dp // 4, dp // 2 % 2, dp % 2, lax.axis_index("shard")]).astype(jnp.int32)


def join(*parts):
    return jnp.concatenate(parts, axis=0)


def after(array, *others):
    return lax.optimization_barrier((array,) + others)[0]


def gather_z(unit):
    one, two, three = swap(unit, 1, 0, 0, 0), swap(unit, 2, 0, 0, 0), swap(unit, 3, 0, 0, 0)
    return jnp.stack([unit, one]), jnp.stack([two, three])


def gather_near(a, b):
    return join(a, swap(a, 0, 1, 0, 0)), join(b, swap(b, 0, 0, 0, 1))


def gather_far(a, b):
    return (a, swap(a, 0, 0, 0, 1), b, swap(b, 0, 1, 0, 0))


def gather_core(mine):
    return mine + tuple(swap(m, 0, 0, 1, 0) for m in mine)


def add_low(left, right):
    return (left.astype(F32) + right.astype(F32)).astype(BF16)


def reduce_core(keep, send, *gate):
    got = after(swap(send, 0, 0, 1, 0), *gate)
    send_a = add_low(keep[:2, :, 1], got[:2, :, 1])
    send_b = add_low(keep[2:, 1], got[2:, 1])
    return (send_a, send_b), (keep, got)


def reduce_far(sends, held, *gate):
    keep, got = held
    got_a = after(swap(sends[0], 0, 0, 0, 1), *gate)
    got_b = after(swap(sends[1], 0, 1, 0, 0), *gate)
    a = keep[:2, :, 0].astype(F32) + got[:2, :, 0].astype(F32) + got_a.astype(F32)
    b = keep[2:, 0].astype(F32) + got[2:, 0].astype(F32) + got_b.astype(F32)
    return (a[:, 1].astype(BF16), b[:, 1].astype(BF16)), (a[:, 0], b[:, 0])


def reduce_near(sends, held):
    a = held[0] + swap(sends[0], 0, 1, 0, 0).astype(F32)
    b = held[1] + swap(sends[1], 0, 0, 0, 1).astype(F32)
    return (a[1].astype(BF16), b[0].astype(BF16), b[1].astype(BF16)), a[0]


def reduce_z(sends, held, *gate):
    for step, array in enumerate(sends):
        held = held + after(swap(array, step + 1, 0, 0, 0), *gate).astype(F32)
    return held


def unit_pairs(me, bufs, emit):
    mz, my, mc, mx = me[0], me[1], me[2], me[3]
    flip = jnp.broadcast_to(mx, (8, 128)) == 1

    def send(dz, dy, dc, near, far):
        dp = ((mz ^ dz) * 2 + (my ^ dy)) * 2 + (mc ^ dc)
        emit(dp, near, far)

    for dc in range(2):
        a, a_far, b, b_far = bufs[4 * dc : 4 * dc + 4]
        for i in range(2):
            for j in range(2):
                send(j, i, dc, (a, 2 * i + j), (a_far, 2 * i + j))
        for i, buf in enumerate((b, b_far)):
            for j in range(2):
                send(2 + j, i, dc, (buf, j), (buf, 2 + j))


def pack_first(wq, wk, wv, vec, bup, out):
    blocks = [vec[8 * c : 8 * c + 8, :] for c in range(3)] + [jnp.broadcast_to(bup[...], (8, 128))]
    width = out.shape[1]
    tail = jnp.concatenate(blocks + [jnp.zeros((8, width - 512), F32)], axis=1)
    out[...] = jnp.concatenate([w[...].astype(F32) for w in (wq, wk, wv)] + [tail], axis=0).astype(BF16)


def assemble_first(me, *refs):
    bufs, (wq, wk, wv, vec, bup, small) = refs[:8], refs[8:]
    mx = me[3]

    def emit(dp, near, far):
        n = near[0][near[1]].astype(F32)
        f = far[0][far[1]].astype(F32)
        low = jnp.where(mx == 0, n, f)
        high = jnp.where(mx == 0, f, n)
        at = pl.ds(pl.multiple_of(dp * 48, 16), 48)
        for w, ref in enumerate((wq, wk, wv)):
            ref[at, :] = jnp.concatenate(
                [low[UNIT * w : UNIT * (w + 1)], high[UNIT * w : UNIT * (w + 1)]], axis=0
            ).astype(BF16)
        for x, rows in enumerate((low, high)):
            for c in range(4):
                small[dp * 2 + x, 8 * c : 8 * c + 8, :] = rows[3 * UNIT :, 128 * c : 128 * c + 128]

    unit_pairs(me, bufs, emit)
    for idx in range(small.shape[0]):
        vec[0, :, UNIT * idx : UNIT * (idx + 1)] = small[idx, :24, :UNIT]
        bup[:, 4 * UNIT * idx : 4 * UNIT * (idx + 1)] = small[idx, 24:25, : 4 * UNIT]


def assemble_rest(units, wo, wup, wdown):
    count = units.shape[0]
    width = wo.shape[1]
    for w in range(5):
        rows = jnp.concatenate([units[i, w].astype(F32) for i in range(count)], axis=0).astype(BF16)
        if w == 0:
            wo[...] = rows
        else:
            wup[:, (w - 1) * width : w * width] = rows
    for i in range(0, count):
        rows = jnp.concatenate([units[i, w].astype(F32) for w in range(5, 9)], axis=0)
        wdown[4 * UNIT * i : 4 * UNIT * (i + 1), :] = rows.astype(BF16)


def call_assemble_rest(units, ff):
    devices, blocks, rows, width = units.shape
    step = 8
    return pl.pallas_call(
        assemble_rest,
        grid=(devices // step,),
        in_specs=[pl.BlockSpec((step, blocks, rows, width), lambda i: (i, 0, 0, 0))],
        out_specs=[
            pl.BlockSpec((step * rows, width), lambda i: (i, 0)),
            pl.BlockSpec((step * rows, ff), lambda i: (i, 0)),
            pl.BlockSpec((step * rows * 4, width), lambda i: (i, 0)),
        ],
        out_shape=[jax.ShapeDtypeStruct(d, BF16) for d in ((width, width), (width, ff), (ff, width))],
        compiler_params=params(),
        name="assemble_rest",
    )(units)


def call_pack_first(wq, wk, wv, vec, bup):
    return pl.pallas_call(
        pack_first, out_shape=jax.ShapeDtypeStruct((3 * UNIT + 8, wq.shape[1]), BF16), name="pack_first"
    )(wq, wk, wv, vec, bup)


def call_assemble(body, me, bufs, outs, name, scratch=()):
    vm = pl.BlockSpec(memory_space=pltpu.VMEM)
    return pl.pallas_call(
        body,
        in_specs=[SCALARS] + [vm] * 8,
        out_specs=[vm] * len(outs),
        out_shape=[jax.ShapeDtypeStruct(d, t) for d, t in outs],
        scratch_shapes=list(scratch),
        compiler_params=params(),
        name=name,
    )(me, *bufs)


def emit_units(me, keep, send, value_of):
    mz, my, mc, mx = me[0], me[1], me[2], me[3]
    for core in range(2):

        @pl.when(mc == core)
        def _():
            for z in range(4):
                for y in range(2):
                    for x in range(2):
                        to = (z ^ mz, y ^ my, x ^ mx)
                        keep[to] = value_of(z, y, core, x)
                        send[to] = value_of(z, y, 1 - core, x)


def product_sum(lefts, rights):
    total = None
    for left, right in zip(lefts, rights):
        for i in range(left.shape[0]):
            term = dot_tn(left[i], right[i])
            total = term if total is None else total + term
    return total


def product_up(segments, me, *refs):
    o, db, h, du = (refs[segments * i : segments * (i + 1)] for i in range(4))
    keep, send, acc = refs[4 * segments :]

    @pl.when(pl.program_id(0) == 0)
    def _():
        acc[...] = product_sum(o, db)

    @pl.when(pl.program_id(0) > 0)
    def _():
        acc[...] = product_sum(h, du)

    def value_of(*at):
        idx = spot(*at)
        return acc[UNIT * idx : UNIT * (idx + 1), :].astype(BF16)

    emit_units(me, keep.at[:, :, :, 0], send.at[:, :, :, 0], value_of)


def product_down(segments, me, *refs):
    a, df = refs[:segments], refs[segments : 2 * segments]
    keep, send, acc = refs[2 * segments :]
    tall = 4 * UNIT
    acc[...] = product_sum(a, df)
    my, mc, mx = me[1], me[2], me[3]
    for core in range(2):

        @pl.when(mc == core)
        def _():
            for y in range(2):
                for x in range(2):
                    for ref, c in ((keep, core), (send, 1 - core)):
                        row = ((y * 2 + c) * 2 + x) * tall
                        ref[0, y ^ my, x ^ mx] = acc[row : row + tall, :].astype(BF16)


def product_first(segments, me, *refs):
    vat, vec, vup = (refs[segments * i : segments * (i + 1)] for i in range(3))
    dmem = refs[3 * segments]
    refs = refs[3 * segments + 1 :]
    x, dq, dk, dv = (refs[segments * i : segments * (i + 1)] for i in range(4))
    keep, send, acc, vec_s, bup_s = refs[4 * segments :]
    step = pl.program_id(0)

    for w, right in enumerate((dq, dk, dv)):
        term = product_sum(x, right)

        @pl.when(step == 0)
        def _():
            acc[w] = term

        @pl.when(step > 0)
        def _():
            acc[w] += term

    @pl.when(step == pl.num_programs(0) - 1)
    def _():
        vat_sum = sum(v[...].sum(axis=0) for v in vat)
        vec_sum = sum(v[...].sum(axis=0) for v in vec)
        vec_s[...] = jnp.zeros_like(vec_s)
        vec_s[0:16, :] = dmem[...].sum(axis=0)
        vec_s[0:2, :] = vat_sum[0:2]
        vec_s[2:6, :] = vec_sum[0:4]
        vec_s[16:18, :] = vec_sum[4:6]
        bup_s[...] = jnp.broadcast_to(sum(v[...].sum(axis=0) for v in vup), bup_s.shape)
        width = acc.shape[2]
        blank = jnp.zeros((8, width - 512), F32)

        def window(ref, at):
            low = min(at // 128 * 128, ref.shape[1] - 256)
            two = ref[:, low : low + 256]
            return (two if at == low else pltpu.roll(two, 256 - (at - low), 1))[:, :128]

        def value_of(*at):
            idx = spot(*at)
            rows = [acc[w, UNIT * idx : UNIT * (idx + 1), :] for w in range(3)]
            vectors = window(vec_s, UNIT * idx)
            hidden = window(bup_s, 4 * UNIT * idx)
            tail = jnp.concatenate([vectors[0:8], vectors[8:16], vectors[16:24], hidden, blank], axis=1)
            return jnp.concatenate(rows + [tail], axis=0).astype(BF16)

        emit_units(me, keep, send, value_of)


def call_product_up(me, o, db, h, du):
    segments = len(o)
    items, rows, width = o[0].shape
    ff = du[0].shape[2]
    steps = ff // width
    fixed = [pl.BlockSpec((items, rows, width), lambda j, m: (0, 0, 0), pipeline_mode=pl.Buffered(1))] * (3 * segments)
    moving = [pl.BlockSpec((items, rows, width), lambda j, m: (0, 0, jnp.maximum(j - 1, 0)))] * segments
    dims = (4, 2, 2, steps + 1, UNIT, width)
    out = pl.BlockSpec((4, 2, 2, 1, UNIT, width), lambda j, m: (0, 0, 0, j, 0, 0))
    return pl.pallas_call(
        functools.partial(product_up, segments),
        grid_spec=pltpu.PrefetchScalarGridSpec(
            num_scalar_prefetch=1,
            grid=(steps + 1,),
            in_specs=fixed + moving,
            out_specs=[out, out],
            scratch_shapes=[pltpu.VMEM((width, width), F32)],
        ),
        out_shape=[jax.ShapeDtypeStruct(dims, BF16)] * 2,
        compiler_params=params(),
        cost_estimate=pl.CostEstimate(flops=2 * segments * items * rows * width * (ff + width), bytes_accessed=2 * segments * items * rows * (ff + 3 * width) + 2 * width * (ff + width), transcendentals=0),
        name="product_up",
    )(me, *o, *db, *h, *du)


def call_product_down(me, a, df):
    segments = len(a)
    items, rows, width = df[0].shape
    ff = a[0].shape[2]
    moving = [pl.BlockSpec((items, rows, ff // 4), lambda j, m: (0, 0, j ^ m[0]))] * segments
    fixed = [pl.BlockSpec((items, rows, width), lambda j, m: (0, 0, 0), pipeline_mode=pl.Buffered(1))] * segments
    dims = (4, 2, 2, 4 * UNIT, width)
    out = pl.BlockSpec((1, 2, 2, 4 * UNIT, width), lambda j, m: (j, 0, 0, 0, 0))
    return pl.pallas_call(
        functools.partial(product_down, segments),
        grid_spec=pltpu.PrefetchScalarGridSpec(
            num_scalar_prefetch=1,
            grid=(4,),
            in_specs=moving + fixed,
            out_specs=[out, out],
            scratch_shapes=[pltpu.VMEM((ff // 4, width), F32)],
        ),
        out_shape=[jax.ShapeDtypeStruct(dims, BF16)] * 2,
        compiler_params=params(),
        cost_estimate=pl.CostEstimate(flops=2 * segments * items * rows * width * ff, bytes_accessed=2 * segments * items * rows * (ff + width) + 2 * width * ff, transcendentals=0),
        name="product_down",
    )(me, *a, *df)


def call_product_first(me, vat, vec, vup, dmem, x, dq, dk, dv):
    segments = len(x)
    items, rows, width = x[0].shape
    fixed = (*vat, *vec, *vup, dmem)
    moving = [pl.BlockSpec((1, rows, width), lambda j, m: (j, 0, 0))] * (4 * segments)
    tall = 3 * UNIT + 8
    dims = (4, 2, 2, tall, width)
    out = pl.BlockSpec(dims, lambda j, m: (0,) * 5, pipeline_mode=pl.Buffered(1))
    return pl.pallas_call(
        functools.partial(product_first, segments),
        grid_spec=pltpu.PrefetchScalarGridSpec(
            num_scalar_prefetch=1,
            grid=(items,),
            in_specs=[whole(a) for a in fixed] + moving,
            out_specs=[out, out],
            scratch_shapes=[
                pltpu.VMEM((3, width, width), F32),
                pltpu.VMEM((24, width), F32),
                pltpu.VMEM((8, vup[0].shape[2]), F32),
            ],
        ),
        out_shape=[jax.ShapeDtypeStruct(dims, BF16)] * 2,
        compiler_params=params(),
        cost_estimate=pl.CostEstimate(flops=6 * segments * items * rows * width * width, bytes_accessed=8 * segments * items * rows * width + 6 * width * width, transcendentals=0),
        name="product_first",
    )(me, *fixed, *x, *dq, *dk, *dv)


def shown(array):
    return lax.optimization_barrier(array.transpose(0, 2, 1, 3))


def gather_weights(me, shards, *rows):
    mem, wq, wk, wv, wo, wup, wdown, bq, bv, bo, bup, bdown, g1, s1, g2, s2 = shards
    width = wq.shape[1]
    ff = wup.shape[1]
    vec = jnp.concatenate([jnp.stack([bq, bv, bo, bdown, g1, s1]), mem.T, jnp.stack([g2, s2])], axis=0)
    vec = jnp.pad(vec, ((0, 6), (0, 128 - UNIT))).astype(F32)
    hidden = jnp.pad(bup[None], ((0, 0), (0, 128 - 4 * UNIT))).astype(F32)
    up_blocks = wup.reshape(UNIT, ff // width, width).transpose(1, 0, 2)
    units = jnp.concatenate([wo[None], up_blocks, wdown.reshape(4, UNIT, width)], axis=0)
    units = lax.all_gather(units, AXES, axis=0)
    a, b = gather_near(*gather_z(call_pack_first(wq, wk, wv, vec, hidden)))
    rows = tuple(lax.optimization_barrier(after(r.transpose(0, 2, 1, 3), b).transpose(0, 2, 1, 3)) for r in rows)
    far = gather_far(a, b)
    *far, tokens, cotangent = lax.optimization_barrier((*far, *rows))
    first = gather_core(tuple(far))
    square = ((width, width), BF16)
    wq, wk, wv, vec, bup = call_assemble(
        assemble_first, me, first, [square] * 3 + [((1, 24, width), F32), ((1, ff), F32)],
        "assemble_first", [pltpu.VMEM((width // UNIT, 32, 128), F32)],
    )
    return (wq, wk, wv, vec, bup), units, (tokens, cotangent)


def gather_plain(shards):
    mem, wq, wk, wv, wo, wup, wdown, bq, bv, bo, bup, bdown, g1, s1, g2, s2 = [
        lax.all_gather(a, AXES, axis=0, tiled=True) for a in shards
    ]
    rows = [bq, bv, bo, bdown, g1, s1, mem.T, g2, s2]
    vectors = jnp.concatenate([r.reshape(-1, wq.shape[1]) for r in rows], axis=0).astype(F32)
    vectors = jnp.pad(vectors, ((0, 6), (0, 0)))[None]
    return (wq, wk, wv, vectors, bup.astype(F32)[None, :]), (wo, wup, wdown)


def reduce_plain(pieces, vat, vec, vup, dmem):
    x, o, db, h, du, a, df, dq, dk, dv = pieces
    vat = sum(v.sum(axis=0) for v in vat)
    vec = sum(v.sum(axis=0) for v in vec)
    gq = call_weight_product(x, dq, 768, 256, F32)
    gk = call_weight_product(x, dk, 768, 256, F32)
    gv = call_weight_product(x, dv, 768, 256, F32)
    go = call_weight_product(o, db, 768, 256, F32)
    gup = call_weight_product(h, du, 768, 256, F32)
    gdown = call_weight_product(a, df, 256, 768, F32)
    terms = (dmem.sum(axis=0)[6:16].T, gq, gk, gv, go, gup, gdown, sum(v.sum(axis=(0, 1)) for v in vup))
    terms += (vat[0], vat[1]) + tuple(vec[i] for i in range(6))
    owned = lax.psum_scatter(terms, AXES, scatter_dimension=0, tiled=True)
    mem, gq, gk, gv, go, gup, gdown, bup, bq, bv, bo, bdown, g1, s1, g2, s2 = owned
    return mem, gq, gk, gv, go, gup, gdown, bq, bv, bo, bup, bdown, g1, s1, g2, s2


def local(*args):
    tokens, segment_count = args[:2]
    shards = args[2:18]
    cotangent, memory_cotangent = args[18:]
    items, segments, seg, width = tokens.shape
    pad = 16 - shards[0].shape[1]
    planned = lax.axis_size("dp") == 16 and lax.axis_size("shard") == 2
    me = coordinates()
    gathered = gather_weights(me, shards, tokens, cotangent) if planned else gather_plain(shards)
    (wq, wk, wv, vec, bup), rest = gathered[:2]
    if planned:
        tokens, cotangent = gathered[2]
    mem = vec
    saved = []
    y = None
    for s in range(segments):
        part = call_attend_forward(s, tokens, mem, wq, wk, wv, vec)
        if s == 0:
            if planned:
                rest = call_assemble_rest(after(rest, part[0]), 4 * width)
            wo, wup, wdown = rest
        o = part[5]
        y, mem, *more = call_feed_forward(s, segment_count, tokens, mem, o, wo, wup, wdown, vec, bup, y)
        saved.append((*part, *more))
    memory_final = mem[:, pad:].astype(BF16)
    dmem = jnp.pad(memory_cotangent.astype(F32), ((0, 0), (pad, 0), (0, 0)))
    tg = None
    pieces = [None] * segments
    vecs, vups, vats = [], [], []
    for s in reversed(range(segments)):
        x, q, k, v, e, o, li, xh1, sc1, h, a, gp, xh2, sc2 = saved[s]
        df, du, dr, db, vec_s, vup_s = call_feed_backward(
            s, segment_count, cotangent, dmem, xh2, sc2, gp, xh1, sc1, wup, wdown, vec
        )
        pieces[s] = (x, o, db, h, du, a, df)
        vecs.append(vec_s)
        vups.append(vup_s)
        into = {} if tg is None else {0: tg}
        back = functools.partial(call_attend_backward, s, segments, seg)
        tail = (q, k, v, e, o, li, wo, wq, wk, wv)
        if s == 0 and planned:
            o_all, db_all, h_all, du_all, a_all, df_all = list(zip(*pieces))[1:]
            down = call_weight_product(a_all, df_all, 768, 768, BF16)
            o_all = (after(o_all[0], down),) + tuple(o_all[1:])
            down = lax.psum_scatter(down, AXES, scatter_dimension=0, tiled=True).astype(F32)
            keep_up, send_up = call_product_up(me, o_all, db_all, h_all, du_all)
            up = reduce_core(keep_up, send_up)
            dr = after(dr, *up[0])
            up = reduce_far(*up)
        tg, dmem, dq, dk, dv, vat_s = back(segment_count, dmem, dr, db, *tail, into=into)
        pieces[s] += (dq, dk, dv)
        vats.append(vat_s)
    pieces = tuple(zip(*pieces))
    if planned:
        x, dq, dk, dv = pieces[0], *pieces[7:]
        x = (after(x[0], *up[0]),) + x[1:]
        keep, send = call_product_first(me, vats, vecs, vups, dmem, x, dq, dk, dv)
        up = reduce_near(*up)
        first = reduce_core(keep, send)
        y = shown(after(y, *first[0]))
        first = reduce_far(*first)
        up = reduce_z(*up, *first[0])
        tg = shown(after(tg, *first[0]))
        sends, held = reduce_near(*first)
        sends, y, tg = lax.optimization_barrier((sends, y, tg))
        first = reduce_z(sends, held)
        y, tg = y.transpose(0, 2, 1, 3), tg.transpose(0, 2, 1, 3)
        gq, gk, gv = [first[UNIT * w : UNIT * (w + 1)] for w in range(3)]
        tail = first[3 * UNIT :]
        per = jnp.concatenate([tail[:, 128 * c : 128 * c + UNIT] for c in range(3)], axis=0)
        bq, bv, bo, bdown, g1, s1 = [per[i] for i in range(6)]
        owned = (
            per[6:16].T, gq, gk, gv, up[0], up[1:].transpose(1, 0, 2).reshape(UNIT, -1), down, bq, bv, bo,
            tail[0, 384 : 384 + 4 * UNIT], bdown, g1, s1, per[16], per[17],
        )
    else:
        owned = reduce_plain(pieces, vats, vecs, vups, dmem)
    return (y, memory_final, tg) + tuple(owned)


def solution(mesh):
    rows = P(("dp", "shard"))
    return jax.shard_map(local, mesh=mesh, in_specs=(rows,) * 20, out_specs=(rows,) * 19, check_vma=False)
```

```python
import functools

import jax
import jax.numpy as jnp
from jax import lax
from jax.experimental import pallas as pl
from jax.experimental.layout import Layout, with_layout_constraint
from jax.experimental.pallas import tpu as pltpu
from jax.sharding import PartitionSpec as P

F32 = jnp.float32
BF16 = jnp.bfloat16
HEADS = 12
HEAD_DIM = 64
NORM_EPS = 1e-06
ROOT_HALF = 0.7071067811865476
ROOT_TWO_PI = 0.3989422804014327


def dot_nn(left, right):
    return jnp.dot(left, right, preferred_element_type=F32)


def dot_nt(left, right):
    return lax.dot_general(left, right, (((1,), (1,)), ((), ())), preferred_element_type=F32)


def dot_tn(left, right):
    return lax.dot_general(left, right, (((0,), (0,)), ((), ())), preferred_element_type=F32)


def lane_masks(rows):
    lane = lax.broadcasted_iota(jnp.int32, (rows, 128), 1)
    first = jnp.where(lane < HEAD_DIM, 1.0, 0.0)
    return first, 1.0 - first


def key_counts(rows, tokens):
    row = lax.broadcasted_iota(jnp.int32, (rows, 128), 0)
    return jnp.where(row < tokens, 1.0, 2.0)


def gelu_parts(u):
    bell = jnp.exp(u * u * -0.5)
    t = pl.reciprocal(1.0 + (0.3275911 * ROOT_HALF) * jnp.abs(u))
    poly = t * (
        0.5 * 0.254829592
        + t * (0.5 * -0.284496736 + t * (0.5 * 1.421413741 + t * (0.5 * -1.453152027 + t * (0.5 * 1.061405429))))
    )
    tail = poly * bell
    cdf = jnp.where(u < 0.0, tail, 1.0 - tail)
    return u * cdf, cdf + u * bell * ROOT_TWO_PI


def attend_forward(tok, mem, wq, wk, wv, vec, x_o, q_o, k_o, v_o, e_o, o_o, li_o):
    bq, bv = vec[0, 0:1, :], vec[0, 1:2, :]
    seg = tok.shape[2]
    rows = x_o.shape[1]
    x_o[0, rows - 16 :, :] = mem[0].astype(BF16)
    x_o[0, :seg, :] = tok[0, 0]
    x = x_o[0]
    q_o[0] = ((dot_nn(x, wq[...]) + bq).astype(BF16).astype(F32) * 0.125).astype(BF16)
    k_o[0] = dot_nn(x, wk[...]).astype(BF16)
    v_o[0] = (dot_nn(x, wv[...]) + bv).astype(BF16)
    masks = lane_masks(rows)
    count = key_counts(rows, seg)
    low_masks = tuple(m.astype(BF16) for m in masks)

    def pair(p, carry):
        at = pl.ds(pl.multiple_of(p * 128, 128), 128)
        q2 = q_o[0, :, at]
        k2 = k_o[0, :, at]
        v2 = v_o[0, :, at].astype(F32) * count
        total = None
        for h in range(2):
            s = dot_nt(q2 * low_masks[h], k2)
            e = jnp.exp(s - jnp.max(s, axis=-1, keepdims=True)).astype(BF16)
            e_o[0, 2 * p + h] = e
            right = jnp.concatenate(
                [(v2 * masks[h]).astype(BF16), (count * masks[h]).astype(BF16)], axis=1
            )
            part = dot_nn(e, right)
            total = part if total is None else total + part
        inv = 1.0 / total[:, 128:]
        li_o[0, :, at] = inv
        o_o[0, :, at] = (total[:, :128] * inv).astype(BF16)
        return carry

    lax.fori_loop(0, HEADS // 2, pair, 0, unroll=True)


def norm_rows(r):
    mean = jnp.mean(r, axis=-1, keepdims=True)
    center = r - mean
    var = jnp.mean(center * center, axis=-1, keepdims=True)
    scale = lax.rsqrt(var + NORM_EPS)
    return center * scale, scale


def feed_forward(
    segment, step,
    count, tok, mem, o, wo, wup, wdown, vec, bup,
    y_o, mem_o, xh1_o, sc1_o, h_o, a_o, gp_o, xh2_o, sc2_o, x_s,
):
    seg = tok.shape[2]
    rows = o.shape[1]
    ff = wup.shape[1]
    bo, bdown, g1, s1, g2, s2 = (vec[0, r : r + 1, :] for r in (2, 3, 4, 5, 16, 17))
    x_s[rows - 16 :, :] = mem[0]
    x_s[:seg, :] = tok[0, 0].astype(F32)
    xh, sc = norm_rows(x_s[...] + dot_nn(o[0], wo[...]) + bo)
    xh1_o[0] = xh.astype(BF16)
    sc1_o[0] = jnp.broadcast_to(sc, (rows, 128))
    h1 = xh * g1 + s1
    h_o[0] = h1.astype(BF16)
    x_s[...] = h1 + bdown

    def chunk(j, carry):
        at = pl.ds(pl.multiple_of(j * step, step), step)
        act, slope = gelu_parts(dot_nn(h_o[0], wup[:, at]) + bup[:, at])
        a_o[0, :, at] = act.astype(BF16)
        gp_o[0, :, at] = slope.astype(BF16)
        x_s[...] += dot_nn(a_o[0, :, at], wdown[at, :])
        return carry

    lax.fori_loop(0, ff // step, chunk, 0, unroll=True)
    xh, sc = norm_rows(x_s[...])
    xh2_o[0] = xh.astype(BF16)
    sc2_o[0] = jnp.broadcast_to(sc, (rows, 128))
    x_s[...] = xh * g2 + s2
    active = count[pl.program_id(0)] > segment
    y_o[0, 0] = jnp.where(active, x_s[:seg, :], 0.0).astype(BF16)
    mem_o[0] = jnp.where(active, x_s[rows - 16 :, :], mem[0])


def norm_back(dy, xh, sc, gain):
    dxh = dy * gain
    m1 = jnp.mean(dxh, axis=-1, keepdims=True)
    m2 = jnp.mean(dxh * xh, axis=-1, keepdims=True)
    return sc * (dxh - m1 - xh * m2)


def col_sum(x):
    return jnp.sum(x, axis=0, keepdims=True)


def feed_backward(
    segment, step,
    count, cot, dmem, xh2, sc2, gp, xh1, sc1, wup, wdown, vec,
    df_o, du_o, dr_o, db_o, vec_o, vup_o, x_s,
):
    seg = cot.shape[2]
    rows = xh2.shape[1]
    ff = wup.shape[1]
    g1, g2 = vec[0, 4:5, :], vec[0, 16:17, :]
    active = jnp.where(count[pl.program_id(0)] > segment, 1.0, 0.0)
    x_s[rows - 16 :, :] = dmem[0] * active
    x_s[:seg, :] = cot[0, 0].astype(F32) * active
    dy = x_s[...]
    xh = xh2[0].astype(F32)
    vec_o[0, 4:5, :] = col_sum(dy * xh)
    vec_o[0, 5:6, :] = col_sum(dy)
    dr = norm_back(dy, xh, sc2[0, :, :1], g2)
    df = dr.astype(BF16)
    df_o[0] = df
    vec_o[0, 1:2, :] = col_sum(df.astype(F32))
    x_s[...] = dr

    def chunk(j, carry):
        at = pl.ds(pl.multiple_of(j * step, step), step)
        du = dot_nt(df_o[0], wdown[at, :]) * gp[0, :, at].astype(F32)
        vup_o[0, :, at] = col_sum(du)
        du_o[0, :, at] = du.astype(BF16)
        x_s[...] += dot_nt(du_o[0, :, at], wup[:, at])
        return carry

    lax.fori_loop(0, ff // step, chunk, 0, unroll=True)
    dh = x_s[...]
    xh = xh1[0].astype(F32)
    vec_o[0, 2:3, :] = col_sum(dh * xh)
    vec_o[0, 3:4, :] = col_sum(dh)
    dr = norm_back(dh, xh, sc1[0, :, :1], g1)
    dr_o[0] = dr
    db_o[0] = dr.astype(BF16)
    vec_o[0, 0:1, :] = col_sum(dr)


def attend_backward(
    segment, first,
    count, dmem, dr, db, q, k, v, e, o, li, wo, wq, wk, wv,
    tg_o, dmem_o, dq_o, dk_o, dv_o, vec_o, do_s, x_s,
):
    seg = tg_o.shape[2]
    rows = q.shape[1]
    do_s[...] = dot_nt(db[0], wo[...]).astype(BF16)
    masks = lane_masks(rows)
    count2 = key_counts(rows, seg)
    low_masks = tuple(m.astype(BF16) for m in masks)
    ones = jnp.ones((rows, 128), BF16)

    def pair(p, carry):
        at = pl.ds(pl.multiple_of(p * 128, 128), 128)
        dop = do_s[:, at].astype(F32) * li[0, :, at]
        pr = (dop * o[0, :, at].astype(F32) * -1.0).astype(BF16)
        dop = dop.astype(BF16)
        q2 = q[0, :, at]
        k2 = (k[0, :, at].astype(F32) * (count2 * 0.125)).astype(BF16)
        right = jnp.concatenate([v[0, :, at], ones], axis=1)
        d_turned = dop.T
        q_turned = q2.T
        dq = None
        dk, dv = [], []
        for h in range(2):
            e_h = e[0, 2 * p + h]
            left = jnp.concatenate([dop * low_masks[h], pr * low_masks[h]], axis=1)
            ds = (e_h.astype(F32) * dot_nt(left, right)).astype(BF16)
            q_t = dot_nn(ds, k2 * low_masks[h])
            dq = q_t if dq is None else dq + q_t
            own = slice(HEAD_DIM * h, HEAD_DIM * (h + 1))
            dk.append(dot_nn(q_turned[own], ds))
            dv.append(dot_nn(d_turned[own], e_h))
        dq_o[0, :, at] = dq.astype(BF16)
        dk_o[0, :, at] = (jnp.concatenate(dk, axis=0).T * count2).astype(BF16)
        dv_o[0, :, at] = (jnp.concatenate(dv, axis=0).T * count2).astype(BF16)
        return carry

    lax.fori_loop(0, HEADS // 2, pair, 0, unroll=True)
    vec_o[0, 0:1, :] = col_sum(dq_o[0].astype(F32))
    vec_o[0, 1:2, :] = col_sum(dv_o[0].astype(F32))
    x_s[...] = (
        dr[0]
        + dot_nt(dq_o[0], wq[...])
        + dot_nt(dk_o[0], wk[...])
        + dot_nt(dv_o[0], wv[...])
    )
    tg_o[0, 0] = x_s[:seg, :].astype(BF16)
    kept = jnp.where(count[pl.program_id(0) + first] > segment, 0.0, 1.0)
    dmem_o[0] = dmem[0] * kept + x_s[rows - 16 :, :]


def weight_product(parts, *refs):
    lefts = refs[:parts]
    rights = refs[parts : 2 * parts]
    out = refs[2 * parts]
    total = None
    for left, right in zip(lefts, rights):
        for i in range(left.shape[0]):
            term = dot_tn(left[i], right[i])
            total = term if total is None else total + term
    out[...] = total.astype(out.dtype)


def whole(array):
    dims = array.shape
    return pl.BlockSpec(dims, lambda *g: (0,) * len(dims), pipeline_mode=pl.Buffered(1))


def per_item(dims, first=0):
    return pl.BlockSpec((1,) + dims, lambda i: (i + first,) + (0,) * len(dims))


def per_segment(dims, segment, first=0):
    return pl.BlockSpec((1, 1) + dims, lambda i: (i + first, segment) + (0,) * len(dims))


def memory_spec(array, first=0):
    shared = array.shape[0] == 1
    return pl.BlockSpec((1, 16, array.shape[2]), lambda i: (0 if shared else i + first, 0, 0))


def out_of(items, dims, dtype):
    return jax.ShapeDtypeStruct((items,) + dims, dtype)


SCALARS = pl.BlockSpec(memory_space=pltpu.SMEM)


def params(mib=60):
    return pltpu.CompilerParams(vmem_limit_bytes=mib << 20)


def launch(body, grid, args, in_specs, out_specs, out_shape, into=None, mib=60, **more):
    into = into or {}
    n_in = len(args)
    aliases = {n_in + k: o for k, o in enumerate(into)}

    def run(*refs):
        body(*refs[:n_in], *refs[n_in + len(into) :])

    return pl.pallas_call(
        run if into else body,
        grid=grid,
        in_specs=list(in_specs) + [pl.BlockSpec(memory_space=pl.ANY)] * len(into),
        out_specs=out_specs,
        out_shape=out_shape,
        input_output_aliases=aliases,
        compiler_params=params(mib),
        **more,
    )(*args, *into.values())


def call_attend_forward(segment, tokens, mem, wq, wk, wv, vec, first=0, many=None, into=None):
    items, _, seg, width = tokens.shape
    many = many or items
    rows = seg + 10
    outs = [((rows, width), BF16)] * 4 + [((HEADS, rows, rows), BF16), ((rows, width), BF16), ((rows, width), F32)]
    return launch(
        attend_forward,
        (many,),
        (tokens, mem, wq, wk, wv, vec),
        [per_segment((seg, width), segment, first), memory_spec(mem, first)] + [whole(w) for w in (wq, wk, wv, vec)],
        [per_item(d, first) for d, t in outs],
        [out_of(items, d, t) for d, t in outs],
        into=dict(enumerate(into)) if into else None,
        cost_estimate=pl.CostEstimate(flops=many * 2 * rows * (3 * width * width + 8 * rows * width), bytes_accessed=many * rows * (width * 14 + HEADS * rows * 2), transcendentals=0),
        name="attend_forward",
    )


def call_feed_forward(segment, count, tokens, mem, o, wo, wup, wdown, vec, bup, into=None):
    items, segments, seg, width = tokens.shape
    rows = o.shape[1]
    ff = wup.shape[1]
    outs = [
        ((16, width), F32), ((rows, width), BF16), ((rows, 128), F32), ((rows, width), BF16),
        ((rows, ff), BF16), ((rows, ff), BF16), ((rows, width), BF16), ((rows, 128), F32),
    ]
    fixed = (wo, wup, wdown, vec, bup)

    def body(*refs):
        feed_forward(segment, 768, *refs)

    return pl_scratch(
        body, (items,), (count, tokens, mem, o) + fixed,
        [SCALARS, per_segment((seg, width), segment), memory_spec(mem), per_item((rows, width))] + [whole(w) for w in fixed],
        [per_segment((seg, width), segment)] + [per_item(d) for d, t in outs],
        [out_of(items, (segments, seg, width), BF16)] + [out_of(items, d, t) for d, t in outs],
        [pltpu.VMEM((rows, width), F32)],
        into={0: into} if into is not None else None,
        cost_estimate=pl.CostEstimate(flops=items * 2 * rows * width * (width + 2 * ff), bytes_accessed=items * rows * (width * 14 + ff * 4), transcendentals=0),
        name="feed_forward",
    )


def pl_scratch(body, grid, args, in_specs, out_specs, out_shape, scratch, into=None, **more):
    return launch(body, grid, args, in_specs, out_specs, out_shape, into=into, scratch_shapes=scratch, **more)


def call_feed_backward(segment, count, cot, dmem, xh2, sc2, gp, xh1, sc1, wup, wdown, vec):
    items, _, seg, width = cot.shape
    rows = xh2.shape[1]
    ff = wup.shape[1]
    outs = [((rows, width), BF16), ((rows, ff), BF16), ((rows, width), F32), ((rows, width), BF16), ((8, width), F32), ((1, ff), F32)]
    fixed = (wup, wdown, vec)

    def body(*refs):
        feed_backward(segment, 768, *refs)

    return pl_scratch(
        body, (items,), (count, cot, dmem, xh2, sc2, gp, xh1, sc1) + fixed,
        [SCALARS, per_segment((seg, width), segment)] + [per_item(a.shape[1:]) for a in (dmem, xh2, sc2, gp, xh1, sc1)] + [whole(w) for w in fixed],
        [per_item(d) for d, t in outs],
        [out_of(items, d, t) for d, t in outs],
        [pltpu.VMEM((rows, width), F32)],
        cost_estimate=pl.CostEstimate(flops=items * 4 * rows * width * ff, bytes_accessed=items * rows * (width * 14 + ff * 4), transcendentals=0),
        name="feed_backward",
    )


def call_attend_backward(segment, segments, seg, count, dmem, dr, db, q, k, v, e, o, li, wo, wq, wk, wv, first=0, many=None, into=None):
    items, rows, width = q.shape
    many = many or items
    outs = [((16, width), F32)] + [((rows, width), BF16)] * 3 + [((8, width), F32)]
    fixed = (wo, wq, wk, wv)

    def body(*refs):
        attend_backward(segment, first, *refs)

    return pl_scratch(
        body, (many,), (count, dmem, dr, db, q, k, v, e, o, li) + fixed,
        [SCALARS] + [per_item(a.shape[1:], first) for a in (dmem, dr, db, q, k, v, e, o, li)] + [whole(w) for w in fixed],
        [per_segment((seg, width), segment, first)] + [per_item(d, first) for d, t in outs],
        [out_of(items, (segments, seg, width), BF16)] + [out_of(items, d, t) for d, t in outs],
        [pltpu.VMEM((rows, width), BF16), pltpu.VMEM((rows, width), F32)],
        into=into,
        cost_estimate=pl.CostEstimate(flops=many * 2 * rows * width * (4 * width + 16 * rows), bytes_accessed=many * rows * (width * 24 + HEADS * rows * 2), transcendentals=0),
        name="attend_backward",
    )


def call_weight_product(lefts, rights, step_left, step_right, dtype):
    parts = len(lefts)
    items, rows, n_left = lefts[0].shape
    n_right = rights[0].shape[2]
    left_spec = pl.BlockSpec((items, rows, step_left), lambda i, j: (0, 0, i))
    right_spec = pl.BlockSpec((items, rows, step_right), lambda i, j: (0, 0, j))
    return pl.pallas_call(
        functools.partial(weight_product, parts),
        grid=(n_left // step_left, n_right // step_right),
        in_specs=[left_spec] * parts + [right_spec] * parts,
        out_specs=pl.BlockSpec((step_left, step_right), lambda i, j: (i, j)),
        out_shape=jax.ShapeDtypeStruct((n_left, n_right), dtype),
        compiler_params=params(),
        cost_estimate=pl.CostEstimate(flops=2 * parts * items * rows * n_left * n_right, bytes_accessed=2 * parts * items * rows * (n_left + n_right), transcendentals=0),
        name="weight_product",
    )(*lefts, *rights)


AXES = ("dp", "shard")
UNIT = 24


def spot(z, y, c, x):
    return ((z * 2 + y) * 2 + c) * 2 + x


def swap(array, dz, dy, dc, dx):
    pairs = [
        (spot(z, y, c, x), spot(z ^ dz, y ^ dy, c ^ dc, x ^ dx))
        for z in range(4)
        for y in range(2)
        for c in range(2)
        for x in range(2)
    ]
    return lax.ppermute(array, AXES, pairs)


def coordinates():
    dp = lax.axis_index("dp")
    return jnp.stack([dp // 4, dp // 2 % 2, dp % 2, lax.axis_index("shard")]).astype(jnp.int32)


def join(*parts):
    return jnp.concatenate(parts, axis=0)


def after(array, *others):
    return lax.optimization_barrier((array,) + others)[0]


def gather_z(unit):
    one, two, three = swap(unit, 1, 0, 0, 0), swap(unit, 2, 0, 0, 0), swap(unit, 3, 0, 0, 0)
    return jnp.stack([unit, one]), jnp.stack([two, three])


def gather_near(a, b):
    return join(a, swap(a, 0, 1, 0, 0)), join(b, swap(b, 0, 0, 0, 1))


def gather_far(a, b):
    return (a, swap(a, 0, 0, 0, 1), b, swap(b, 0, 1, 0, 0))


def gather_core(mine):
    return mine + tuple(swap(m, 0, 0, 1, 0) for m in mine)


def add_low(left, right):
    return (left.astype(F32) + right.astype(F32)).astype(BF16)


def reduce_core(keep, send, *gate):
    got = after(swap(send, 0, 0, 1, 0), *gate)
    send_a = add_low(keep[:2, :, 1], got[:2, :, 1])
    send_b = add_low(keep[2:, 1], got[2:, 1])
    return (send_a, send_b), (keep, got)


def reduce_far(sends, held, *gate):
    keep, got = held
    got_a = after(swap(sends[0], 0, 0, 0, 1), *gate)
    got_b = after(swap(sends[1], 0, 1, 0, 0), *gate)
    a = keep[:2, :, 0].astype(F32) + got[:2, :, 0].astype(F32) + got_a.astype(F32)
    b = keep[2:, 0].astype(F32) + got[2:, 0].astype(F32) + got_b.astype(F32)
    return (a[:, 1].astype(BF16), b[:, 1].astype(BF16)), (a[:, 0], b[:, 0])


def reduce_near(sends, held):
    a = held[0] + swap(sends[0], 0, 1, 0, 0).astype(F32)
    b = held[1] + swap(sends[1], 0, 0, 0, 1).astype(F32)
    return (a[1].astype(BF16), b[0].astype(BF16), b[1].astype(BF16)), a[0]


def reduce_z(sends, held, *gate):
    for step, array in enumerate(sends):
        held = held + after(swap(array, step + 1, 0, 0, 0), *gate).astype(F32)
    return held


def unit_pairs(me, bufs, emit):
    mz, my, mc, mx = me[0], me[1], me[2], me[3]
    flip = jnp.broadcast_to(mx, (8, 128)) == 1

    def send(dz, dy, dc, near, far):
        dp = ((mz ^ dz) * 2 + (my ^ dy)) * 2 + (mc ^ dc)
        emit(dp, near, far)

    for dc in range(2):
        a, a_far, b, b_far = bufs[4 * dc : 4 * dc + 4]
        for i in range(2):
            for j in range(2):
                send(j, i, dc, (a, 2 * i + j), (a_far, 2 * i + j))
        for i, buf in enumerate((b, b_far)):
            for j in range(2):
                send(2 + j, i, dc, (buf, j), (buf, 2 + j))


def pack_first(wq, wk, wv, vec, bup, out):
    blocks = [vec[8 * c : 8 * c + 8, :] for c in range(3)] + [jnp.broadcast_to(bup[...], (8, 128))]
    width = out.shape[1]
    tail = jnp.concatenate(blocks + [jnp.zeros((8, width - 512), F32)], axis=1)
    out[...] = jnp.concatenate([w[...].astype(F32) for w in (wq, wk, wv)] + [tail], axis=0).astype(BF16)


def assemble_first(me, *refs):
    bufs, (wq, wk, wv, vec, bup, small) = refs[:8], refs[8:]
    mx = me[3]

    def emit(dp, near, far):
        n = near[0][near[1]].astype(F32)
        f = far[0][far[1]].astype(F32)
        low = jnp.where(mx == 0, n, f)
        high = jnp.where(mx == 0, f, n)
        at = pl.ds(pl.multiple_of(dp * 48, 16), 48)
        for w, ref in enumerate((wq, wk, wv)):
            ref[at, :] = jnp.concatenate(
                [low[UNIT * w : UNIT * (w + 1)], high[UNIT * w : UNIT * (w + 1)]], axis=0
            ).astype(BF16)
        for x, rows in enumerate((low, high)):
            for c in range(4):
                small[dp * 2 + x, 8 * c : 8 * c + 8, :] = rows[3 * UNIT :, 128 * c : 128 * c + 128]

    unit_pairs(me, bufs, emit)
    for idx in range(small.shape[0]):
        vec[0, :, UNIT * idx : UNIT * (idx + 1)] = small[idx, :24, :UNIT]
        bup[:, 4 * UNIT * idx : 4 * UNIT * (idx + 1)] = small[idx, 24:25, : 4 * UNIT]


def assemble_rest(units, wo, wup, wdown):
    count = units.shape[0]
    width = wo.shape[1]
    for w in range(5):
        rows = jnp.concatenate([units[i, w].astype(F32) for i in range(count)], axis=0).astype(BF16)
        if w == 0:
            wo[...] = rows
        else:
            wup[:, (w - 1) * width : w * width] = rows
    for i in range(0, count):
        rows = jnp.concatenate([units[i, w].astype(F32) for w in range(5, 9)], axis=0)
        wdown[4 * UNIT * i : 4 * UNIT * (i + 1), :] = rows.astype(BF16)


def call_assemble_rest(units, ff):
    devices, blocks, rows, width = units.shape
    step = 8
    return pl.pallas_call(
        assemble_rest,
        grid=(devices // step,),
        in_specs=[pl.BlockSpec((step, blocks, rows, width), lambda i: (i, 0, 0, 0))],
        out_specs=[
            pl.BlockSpec((step * rows, width), lambda i: (i, 0)),
            pl.BlockSpec((step * rows, ff), lambda i: (i, 0)),
            pl.BlockSpec((step * rows * 4, width), lambda i: (i, 0)),
        ],
        out_shape=[jax.ShapeDtypeStruct(d, BF16) for d in ((width, width), (width, ff), (ff, width))],
        compiler_params=params(),
        name="assemble_rest",
    )(units)


def call_pack_first(wq, wk, wv, vec, bup):
    return pl.pallas_call(
        pack_first, out_shape=jax.ShapeDtypeStruct((3 * UNIT + 8, wq.shape[1]), BF16), name="pack_first"
    )(wq, wk, wv, vec, bup)


def call_assemble(body, me, bufs, outs, name, scratch=()):
    vm = pl.BlockSpec(memory_space=pltpu.VMEM)
    return pl.pallas_call(
        body,
        in_specs=[SCALARS] + [vm] * 8,
        out_specs=[vm] * len(outs),
        out_shape=[jax.ShapeDtypeStruct(d, t) for d, t in outs],
        scratch_shapes=list(scratch),
        compiler_params=params(),
        name=name,
    )(me, *bufs)


def emit_units(me, keep, send, value_of):
    mz, my, mc, mx = me[0], me[1], me[2], me[3]
    for core in range(2):

        @pl.when(mc == core)
        def _():
            for z in range(4):
                for y in range(2):
                    for x in range(2):
                        to = (z ^ mz, y ^ my, x ^ mx)
                        keep[to] = value_of(z, y, core, x)
                        send[to] = value_of(z, y, 1 - core, x)


def product_sum(lefts, rights):
    total = None
    for left, right in zip(lefts, rights):
        for i in range(left.shape[0]):
            term = dot_tn(left[i], right[i])
            total = term if total is None else total + term
    return total


def product_up(segments, me, *refs):
    o, db, h, du = (refs[segments * i : segments * (i + 1)] for i in range(4))
    keep, send, acc = refs[4 * segments :]

    @pl.when(pl.program_id(0) == 0)
    def _():
        acc[...] = product_sum(o, db)

    @pl.when(pl.program_id(0) > 0)
    def _():
        acc[...] = product_sum(h, du)

    def value_of(*at):
        idx = spot(*at)
        return acc[UNIT * idx : UNIT * (idx + 1), :].astype(BF16)

    emit_units(me, keep.at[:, :, :, 0], send.at[:, :, :, 0], value_of)


def product_down(segments, me, *refs):
    a, df = refs[:segments], refs[segments : 2 * segments]
    keep, send, acc = refs[2 * segments :]
    tall = 4 * UNIT
    acc[...] = product_sum(a, df)
    my, mc, mx = me[1], me[2], me[3]
    for core in range(2):

        @pl.when(mc == core)
        def _():
            for y in range(2):
                for x in range(2):
                    for ref, c in ((keep, core), (send, 1 - core)):
                        row = ((y * 2 + c) * 2 + x) * tall
                        ref[0, y ^ my, x ^ mx] = acc[row : row + tall, :].astype(BF16)


def product_first(segments, me, *refs):
    vat, vec, vup = (refs[segments * i : segments * (i + 1)] for i in range(3))
    dmem = refs[3 * segments]
    refs = refs[3 * segments + 1 :]
    x, dq, dk, dv = (refs[segments * i : segments * (i + 1)] for i in range(4))
    keep, send, acc, vec_s, bup_s = refs[4 * segments :]
    step = pl.program_id(0)

    for w, right in enumerate((dq, dk, dv)):
        term = product_sum(x, right)

        @pl.when(step == 0)
        def _():
            acc[w] = term

        @pl.when(step > 0)
        def _():
            acc[w] += term

    @pl.when(step == pl.num_programs(0) - 1)
    def _():
        vat_sum = sum(v[...].sum(axis=0) for v in vat)
        vec_sum = sum(v[...].sum(axis=0) for v in vec)
        vec_s[...] = jnp.zeros_like(vec_s)
        vec_s[0:16, :] = dmem[...].sum(axis=0)
        vec_s[0:2, :] = vat_sum[0:2]
        vec_s[2:6, :] = vec_sum[0:4]
        vec_s[16:18, :] = vec_sum[4:6]
        bup_s[...] = jnp.broadcast_to(sum(v[...].sum(axis=0) for v in vup), bup_s.shape)
        width = acc.shape[2]
        blank = jnp.zeros((8, width - 512), F32)

        def window(ref, at):
            low = min(at // 128 * 128, ref.shape[1] - 256)
            two = ref[:, low : low + 256]
            return (two if at == low else pltpu.roll(two, 256 - (at - low), 1))[:, :128]

        def value_of(*at):
            idx = spot(*at)
            rows = [acc[w, UNIT * idx : UNIT * (idx + 1), :] for w in range(3)]
            vectors = window(vec_s, UNIT * idx)
            hidden = window(bup_s, 4 * UNIT * idx)
            tail = jnp.concatenate([vectors[0:8], vectors[8:16], vectors[16:24], hidden, blank], axis=1)
            return jnp.concatenate(rows + [tail], axis=0).astype(BF16)

        emit_units(me, keep, send, value_of)


def call_product_up(me, o, db, h, du):
    segments = len(o)
    items, rows, width = o[0].shape
    ff = du[0].shape[2]
    steps = ff // width
    fixed = [pl.BlockSpec((items, rows, width), lambda j, m: (0, 0, 0), pipeline_mode=pl.Buffered(1))] * (3 * segments)
    moving = [pl.BlockSpec((items, rows, width), lambda j, m: (0, 0, jnp.maximum(j - 1, 0)))] * segments
    dims = (4, 2, 2, steps + 1, UNIT, width)
    out = pl.BlockSpec((4, 2, 2, 1, UNIT, width), lambda j, m: (0, 0, 0, j, 0, 0))
    return pl.pallas_call(
        functools.partial(product_up, segments),
        grid_spec=pltpu.PrefetchScalarGridSpec(
            num_scalar_prefetch=1,
            grid=(steps + 1,),
            in_specs=fixed + moving,
            out_specs=[out, out],
            scratch_shapes=[pltpu.VMEM((width, width), F32)],
        ),
        out_shape=[jax.ShapeDtypeStruct(dims, BF16)] * 2,
        compiler_params=params(),
        cost_estimate=pl.CostEstimate(flops=2 * segments * items * rows * width * (ff + width), bytes_accessed=2 * segments * items * rows * (ff + 3 * width) + 2 * width * (ff + width), transcendentals=0),
        name="product_up",
    )(me, *o, *db, *h, *du)


def call_product_down(me, a, df):
    segments = len(a)
    items, rows, width = df[0].shape
    ff = a[0].shape[2]
    moving = [pl.BlockSpec((items, rows, ff // 4), lambda j, m: (0, 0, j ^ m[0]))] * segments
    fixed = [pl.BlockSpec((items, rows, width), lambda j, m: (0, 0, 0), pipeline_mode=pl.Buffered(1))] * segments
    dims = (4, 2, 2, 4 * UNIT, width)
    out = pl.BlockSpec((1, 2, 2, 4 * UNIT, width), lambda j, m: (j, 0, 0, 0, 0))
    return pl.pallas_call(
        functools.partial(product_down, segments),
        grid_spec=pltpu.PrefetchScalarGridSpec(
            num_scalar_prefetch=1,
            grid=(4,),
            in_specs=moving + fixed,
            out_specs=[out, out],
            scratch_shapes=[pltpu.VMEM((ff // 4, width), F32)],
        ),
        out_shape=[jax.ShapeDtypeStruct(dims, BF16)] * 2,
        compiler_params=params(),
        cost_estimate=pl.CostEstimate(flops=2 * segments * items * rows * width * ff, bytes_accessed=2 * segments * items * rows * (ff + width) + 2 * width * ff, transcendentals=0),
        name="product_down",
    )(me, *a, *df)


def call_product_first(me, vat, vec, vup, dmem, x, dq, dk, dv):
    segments = len(x)
    items, rows, width = x[0].shape
    fixed = (*vat, *vec, *vup, dmem)
    moving = [pl.BlockSpec((1, rows, width), lambda j, m: (j, 0, 0))] * (4 * segments)
    tall = 3 * UNIT + 8
    dims = (4, 2, 2, tall, width)
    out = pl.BlockSpec(dims, lambda j, m: (0,) * 5, pipeline_mode=pl.Buffered(1))
    return pl.pallas_call(
        functools.partial(product_first, segments),
        grid_spec=pltpu.PrefetchScalarGridSpec(
            num_scalar_prefetch=1,
            grid=(items,),
            in_specs=[whole(a) for a in fixed] + moving,
            out_specs=[out, out],
            scratch_shapes=[
                pltpu.VMEM((3, width, width), F32),
                pltpu.VMEM((24, width), F32),
                pltpu.VMEM((8, vup[0].shape[2]), F32),
            ],
        ),
        out_shape=[jax.ShapeDtypeStruct(dims, BF16)] * 2,
        compiler_params=params(),
        cost_estimate=pl.CostEstimate(flops=6 * segments * items * rows * width * width, bytes_accessed=8 * segments * items * rows * width + 6 * width * width, transcendentals=0),
        name="product_first",
    )(me, *fixed, *x, *dq, *dk, *dv)


def shown(array):
    turned = with_layout_constraint(array.transpose(0, 2, 1, 3), Layout(major_to_minor=(0, 1, 2, 3)))
    return lax.optimization_barrier(turned)


def gather_weights(me, shards, *rows):
    mem, wq, wk, wv, wo, wup, wdown, bq, bv, bo, bup, bdown, g1, s1, g2, s2 = shards
    width = wq.shape[1]
    ff = wup.shape[1]
    vec = jnp.concatenate([jnp.stack([bq, bv, bo, bdown, g1, s1]), mem.T, jnp.stack([g2, s2])], axis=0)
    vec = jnp.pad(vec, ((0, 6), (0, 128 - UNIT))).astype(F32)
    hidden = jnp.pad(bup[None], ((0, 0), (0, 128 - 4 * UNIT))).astype(F32)
    up_blocks = wup.reshape(UNIT, ff // width, width).transpose(1, 0, 2)
    units = jnp.concatenate([wo[None], up_blocks, wdown.reshape(4, UNIT, width)], axis=0)
    units = lax.all_gather(units, AXES, axis=0)
    a, b = gather_near(*gather_z(call_pack_first(wq, wk, wv, vec, hidden)))
    rows = tuple(lax.optimization_barrier(after(r.transpose(0, 2, 1, 3), b).transpose(0, 2, 1, 3)) for r in rows)
    far = gather_far(a, b)
    *far, tokens, cotangent = lax.optimization_barrier((*far, *rows))
    first = gather_core(tuple(far))
    square = ((width, width), BF16)
    wq, wk, wv, vec, bup = call_assemble(
        assemble_first, me, first, [square] * 3 + [((1, 24, width), F32), ((1, ff), F32)],
        "assemble_first", [pltpu.VMEM((width // UNIT, 32, 128), F32)],
    )
    return (wq, wk, wv, vec, bup), units, (tokens, cotangent)


def gather_plain(shards):
    mem, wq, wk, wv, wo, wup, wdown, bq, bv, bo, bup, bdown, g1, s1, g2, s2 = [
        lax.all_gather(a, AXES, axis=0, tiled=True) for a in shards
    ]
    rows = [bq, bv, bo, bdown, g1, s1, mem.T, g2, s2]
    vectors = jnp.concatenate([r.reshape(-1, wq.shape[1]) for r in rows], axis=0).astype(F32)
    vectors = jnp.pad(vectors, ((0, 6), (0, 0)))[None]
    return (wq, wk, wv, vectors, bup.astype(F32)[None, :]), (wo, wup, wdown)


def reduce_plain(pieces, vat, vec, vup, dmem):
    x, o, db, h, du, a, df, dq, dk, dv = pieces
    vat = sum(v.sum(axis=0) for v in vat)
    vec = sum(v.sum(axis=0) for v in vec)
    gq = call_weight_product(x, dq, 768, 256, F32)
    gk = call_weight_product(x, dk, 768, 256, F32)
    gv = call_weight_product(x, dv, 768, 256, F32)
    go = call_weight_product(o, db, 768, 256, F32)
    gup = call_weight_product(h, du, 768, 256, F32)
    gdown = call_weight_product(a, df, 256, 768, F32)
    terms = (dmem.sum(axis=0)[6:16].T, gq, gk, gv, go, gup, gdown, sum(v.sum(axis=(0, 1)) for v in vup))
    terms += (vat[0], vat[1]) + tuple(vec[i] for i in range(6))
    owned = lax.psum_scatter(terms, AXES, scatter_dimension=0, tiled=True)
    mem, gq, gk, gv, go, gup, gdown, bup, bq, bv, bo, bdown, g1, s1, g2, s2 = owned
    return mem, gq, gk, gv, go, gup, gdown, bq, bv, bo, bup, bdown, g1, s1, g2, s2


def local(*args):
    tokens, segment_count = args[:2]
    shards = args[2:18]
    cotangent, memory_cotangent = args[18:]
    items, segments, seg, width = tokens.shape
    pad = 16 - shards[0].shape[1]
    planned = lax.axis_size("dp") == 16 and lax.axis_size("shard") == 2
    me = coordinates()
    gathered = gather_weights(me, shards, tokens, cotangent) if planned else gather_plain(shards)
    (wq, wk, wv, vec, bup), rest = gathered[:2]
    if planned:
        tokens, cotangent = gathered[2]
    mem = vec
    saved = []
    y = None
    for s in range(segments):
        part = call_attend_forward(s, tokens, mem, wq, wk, wv, vec)
        if s == 0:
            if planned:
                rest = call_assemble_rest(after(rest, part[0]), 4 * width)
            wo, wup, wdown = rest
        o = part[5]
        y, mem, *more = call_feed_forward(s, segment_count, tokens, mem, o, wo, wup, wdown, vec, bup, y)
        saved.append((*part, *more))
    memory_final = mem[:, pad:].astype(BF16)
    dmem = jnp.pad(memory_cotangent.astype(F32), ((0, 0), (pad, 0), (0, 0)))
    tg = None
    pieces = [None] * segments
    vecs, vups, vats = [], [], []
    for s in reversed(range(segments)):
        x, q, k, v, e, o, li, xh1, sc1, h, a, gp, xh2, sc2 = saved[s]
        df, du, dr, db, vec_s, vup_s = call_feed_backward(
            s, segment_count, cotangent, dmem, xh2, sc2, gp, xh1, sc1, wup, wdown, vec
        )
        pieces[s] = (x, o, db, h, du, a, df)
        vecs.append(vec_s)
        vups.append(vup_s)
        into = {} if tg is None else {0: tg}
        back = functools.partial(call_attend_backward, s, segments, seg)
        tail = (q, k, v, e, o, li, wo, wq, wk, wv)
        if s == 0 and planned:
            o_all, db_all, h_all, du_all, a_all, df_all = list(zip(*pieces))[1:]
            down = call_weight_product(a_all, df_all, 768, 768, BF16)
            o_all = (after(o_all[0], down),) + tuple(o_all[1:])
            down = lax.psum_scatter(down, AXES, scatter_dimension=0, tiled=True).astype(F32)
            keep_up, send_up = call_product_up(me, o_all, db_all, h_all, du_all)
            up = reduce_core(keep_up, send_up)
            dr = after(dr, *up[0])
            up = reduce_far(*up)
        tg, dmem, dq, dk, dv, vat_s = back(segment_count, dmem, dr, db, *tail, into=into)
        pieces[s] += (dq, dk, dv)
        vats.append(vat_s)
    pieces = tuple(zip(*pieces))
    if planned:
        x, dq, dk, dv = pieces[0], *pieces[7:]
        x = (after(x[0], *up[0]),) + x[1:]
        keep, send = call_product_first(me, vats, vecs, vups, dmem, x, dq, dk, dv)
        up = reduce_near(*up)
        first = reduce_core(keep, send)
        y = shown(after(y, *first[0]))
        first = reduce_far(*first)
        up = reduce_z(*up, *first[0])
        tg = shown(after(tg, *first[0]))
        sends, held = reduce_near(*first)
        sends, y, tg = lax.optimization_barrier((sends, y, tg))
        first = reduce_z(sends, held)
        y, tg = y.transpose(0, 2, 1, 3), tg.transpose(0, 2, 1, 3)
        gq, gk, gv = [first[UNIT * w : UNIT * (w + 1)] for w in range(3)]
        tail = first[3 * UNIT :]
        per = jnp.concatenate([tail[:, 128 * c : 128 * c + UNIT] for c in range(3)], axis=0)
        bq, bv, bo, bdown, g1, s1 = [per[i] for i in range(6)]
        owned = (
            per[6:16].T, gq, gk, gv, up[0], up[1:].transpose(1, 0, 2).reshape(UNIT, -1), down, bq, bv, bo,
            tail[0, 384 : 384 + 4 * UNIT], bdown, g1, s1, per[16], per[17],
        )
    else:
        owned = reduce_plain(pieces, vats, vecs, vups, dmem)
    return (y, memory_final, tg) + tuple(owned)


def solution(mesh):
    rows = P(("dp", "shard"))
    return jax.shard_map(local, mesh=mesh, in_specs=(rows,) * 20, out_specs=(rows,) * 19, check_vma=False)
```

```python
import functools

import jax
import jax.numpy as jnp
from jax import lax
from jax.experimental import pallas as pl
from jax.experimental.layout import Layout, with_layout_constraint
from jax.experimental.pallas import tpu as pltpu
from jax.sharding import PartitionSpec as P

F32 = jnp.float32
BF16 = jnp.bfloat16
HEADS = 12
HEAD_DIM = 64
NORM_EPS = 1e-06
ROOT_HALF = 0.7071067811865476
ROOT_TWO_PI = 0.3989422804014327


def dot_nn(left, right):
    return jnp.dot(left, right, preferred_element_type=F32)


def dot_nt(left, right):
    return lax.dot_general(left, right, (((1,), (1,)), ((), ())), preferred_element_type=F32)


def dot_tn(left, right):
    return lax.dot_general(left, right, (((0,), (0,)), ((), ())), preferred_element_type=F32)


def lane_masks(rows):
    lane = lax.broadcasted_iota(jnp.int32, (rows, 128), 1)
    first = jnp.where(lane < HEAD_DIM, 1.0, 0.0)
    return first, 1.0 - first


def key_counts(rows, tokens):
    row = lax.broadcasted_iota(jnp.int32, (rows, 128), 0)
    return jnp.where(row < tokens, 1.0, 2.0)


def gelu_parts(u):
    bell = jnp.exp(u * u * -0.5)
    t = pl.reciprocal(1.0 + (0.3275911 * ROOT_HALF) * jnp.abs(u))
    poly = t * (
        0.5 * 0.254829592
        + t * (0.5 * -0.284496736 + t * (0.5 * 1.421413741 + t * (0.5 * -1.453152027 + t * (0.5 * 1.061405429))))
    )
    tail = poly * bell
    cdf = jnp.where(u < 0.0, tail, 1.0 - tail)
    return u * cdf, cdf + u * bell * ROOT_TWO_PI


def attend_forward(tok, mem, wq, wk, wv, vec, x_o, q_o, k_o, v_o, e_o, o_o, li_o):
    bq, bv = vec[0, 0:1, :], vec[0, 1:2, :]
    seg = tok.shape[2]
    rows = x_o.shape[1]
    x_o[0, rows - 16 :, :] = mem[0].astype(BF16)
    x_o[0, :seg, :] = tok[0, 0]
    x = x_o[0]
    q_o[0] = ((dot_nn(x, wq[...]) + bq).astype(BF16).astype(F32) * 0.125).astype(BF16)
    k_o[0] = dot_nn(x, wk[...]).astype(BF16)
    v_o[0] = (dot_nn(x, wv[...]) + bv).astype(BF16)
    masks = lane_masks(rows)
    count = key_counts(rows, seg)
    low_masks = tuple(m.astype(BF16) for m in masks)

    def pair(p, carry):
        at = pl.ds(pl.multiple_of(p * 128, 128), 128)
        q2 = q_o[0, :, at]
        k2 = k_o[0, :, at]
        v2 = v_o[0, :, at].astype(F32) * count
        total = None
        for h in range(2):
            s = dot_nt(q2 * low_masks[h], k2)
            e = jnp.exp(s - jnp.max(s, axis=-1, keepdims=True)).astype(BF16)
            e_o[0, 2 * p + h] = e
            right = jnp.concatenate(
                [(v2 * masks[h]).astype(BF16), (count * masks[h]).astype(BF16)], axis=1
            )
            part = dot_nn(e, right)
            total = part if total is None else total + part
        inv = 1.0 / total[:, 128:]
        li_o[0, :, at] = inv
        o_o[0, :, at] = (total[:, :128] * inv).astype(BF16)
        return carry

    lax.fori_loop(0, HEADS // 2, pair, 0, unroll=True)


def norm_rows(r):
    mean = jnp.mean(r, axis=-1, keepdims=True)
    center = r - mean
    var = jnp.mean(center * center, axis=-1, keepdims=True)
    scale = lax.rsqrt(var + NORM_EPS)
    return center * scale, scale


def feed_forward(
    segment, step,
    count, tok, mem, o, wo, wup, wdown, vec, bup,
    y_o, mem_o, xh1_o, sc1_o, h_o, a_o, gp_o, xh2_o, sc2_o, x_s,
):
    seg = tok.shape[2]
    rows = o.shape[1]
    ff = wup.shape[1]
    bo, bdown, g1, s1, g2, s2 = (vec[0, r : r + 1, :] for r in (2, 3, 4, 5, 16, 17))
    x_s[rows - 16 :, :] = mem[0]
    x_s[:seg, :] = tok[0, 0].astype(F32)
    xh, sc = norm_rows(x_s[...] + dot_nn(o[0], wo[...]) + bo)
    xh1_o[0] = xh.astype(BF16)
    sc1_o[0] = jnp.broadcast_to(sc, (rows, 128))
    h1 = xh * g1 + s1
    h_o[0] = h1.astype(BF16)
    x_s[...] = h1 + bdown

    def chunk(j, carry):
        at = pl.ds(pl.multiple_of(j * step, step), step)
        act, slope = gelu_parts(dot_nn(h_o[0], wup[:, at]) + bup[:, at])
        a_o[0, :, at] = act.astype(BF16)
        gp_o[0, :, at] = slope.astype(BF16)
        x_s[...] += dot_nn(a_o[0, :, at], wdown[at, :])
        return carry

    lax.fori_loop(0, ff // step, chunk, 0, unroll=True)
    xh, sc = norm_rows(x_s[...])
    xh2_o[0] = xh.astype(BF16)
    sc2_o[0] = jnp.broadcast_to(sc, (rows, 128))
    x_s[...] = xh * g2 + s2
    active = count[pl.program_id(0)] > segment
    y_o[0, 0] = jnp.where(active, x_s[:seg, :], 0.0).astype(BF16)
    mem_o[0] = jnp.where(active, x_s[rows - 16 :, :], mem[0])


def norm_back(dy, xh, sc, gain):
    dxh = dy * gain
    m1 = jnp.mean(dxh, axis=-1, keepdims=True)
    m2 = jnp.mean(dxh * xh, axis=-1, keepdims=True)
    return sc * (dxh - m1 - xh * m2)


def col_sum(x):
    return jnp.sum(x, axis=0, keepdims=True)


def feed_backward(
    segment, step,
    count, cot, dmem, xh2, sc2, gp, xh1, sc1, wup, wdown, vec,
    df_o, du_o, dr_o, db_o, vec_o, vup_o, x_s,
):
    seg = cot.shape[2]
    rows = xh2.shape[1]
    ff = wup.shape[1]
    g1, g2 = vec[0, 4:5, :], vec[0, 16:17, :]
    active = jnp.where(count[pl.program_id(0)] > segment, 1.0, 0.0)
    x_s[rows - 16 :, :] = dmem[0] * active
    x_s[:seg, :] = cot[0, 0].astype(F32) * active
    dy = x_s[...]
    xh = xh2[0].astype(F32)
    vec_o[0, 4:5, :] = col_sum(dy * xh)
    vec_o[0, 5:6, :] = col_sum(dy)
    dr = norm_back(dy, xh, sc2[0, :, :1], g2)
    df = dr.astype(BF16)
    df_o[0] = df
    vec_o[0, 1:2, :] = col_sum(df.astype(F32))
    x_s[...] = dr

    def chunk(j, carry):
        at = pl.ds(pl.multiple_of(j * step, step), step)
        du = dot_nt(df_o[0], wdown[at, :]) * gp[0, :, at].astype(F32)
        vup_o[0, :, at] = col_sum(du)
        du_o[0, :, at] = du.astype(BF16)
        x_s[...] += dot_nt(du_o[0, :, at], wup[:, at])
        return carry

    lax.fori_loop(0, ff // step, chunk, 0, unroll=True)
    dh = x_s[...]
    xh = xh1[0].astype(F32)
    vec_o[0, 2:3, :] = col_sum(dh * xh)
    vec_o[0, 3:4, :] = col_sum(dh)
    dr = norm_back(dh, xh, sc1[0, :, :1], g1)
    dr_o[0] = dr
    db_o[0] = dr.astype(BF16)
    vec_o[0, 0:1, :] = col_sum(dr)


def attend_backward(
    segment, first,
    count, dmem, dr, db, q, k, v, e, o, li, wo, wq, wk, wv,
    tg_o, dmem_o, dq_o, dk_o, dv_o, vec_o, do_s, x_s,
):
    seg = tg_o.shape[2]
    rows = q.shape[1]
    do_s[...] = dot_nt(db[0], wo[...]).astype(BF16)
    masks = lane_masks(rows)
    count2 = key_counts(rows, seg)
    low_masks = tuple(m.astype(BF16) for m in masks)
    ones = jnp.ones((rows, 128), BF16)

    def pair(p, carry):
        at = pl.ds(pl.multiple_of(p * 128, 128), 128)
        dop = do_s[:, at].astype(F32) * li[0, :, at]
        pr = (dop * o[0, :, at].astype(F32) * -1.0).astype(BF16)
        dop = dop.astype(BF16)
        q2 = q[0, :, at]
        k2 = (k[0, :, at].astype(F32) * (count2 * 0.125)).astype(BF16)
        right = jnp.concatenate([v[0, :, at], ones], axis=1)
        d_turned = dop.T
        q_turned = q2.T
        dq = None
        dk, dv = [], []
        for h in range(2):
            e_h = e[0, 2 * p + h]
            left = jnp.concatenate([dop * low_masks[h], pr * low_masks[h]], axis=1)
            ds = (e_h.astype(F32) * dot_nt(left, right)).astype(BF16)
            q_t = dot_nn(ds, k2 * low_masks[h])
            dq = q_t if dq is None else dq + q_t
            own = slice(HEAD_DIM * h, HEAD_DIM * (h + 1))
            dk.append(dot_nn(q_turned[own], ds))
            dv.append(dot_nn(d_turned[own], e_h))
        dq_o[0, :, at] = dq.astype(BF16)
        dk_o[0, :, at] = (jnp.concatenate(dk, axis=0).T * count2).astype(BF16)
        dv_o[0, :, at] = (jnp.concatenate(dv, axis=0).T * count2).astype(BF16)
        return carry

    lax.fori_loop(0, HEADS // 2, pair, 0, unroll=True)
    vec_o[0, 0:1, :] = col_sum(dq_o[0].astype(F32))
    vec_o[0, 1:2, :] = col_sum(dv_o[0].astype(F32))
    x_s[...] = (
        dr[0]
        + dot_nt(dq_o[0], wq[...])
        + dot_nt(dk_o[0], wk[...])
        + dot_nt(dv_o[0], wv[...])
    )
    tg_o[0, 0] = x_s[:seg, :].astype(BF16)
    kept = jnp.where(count[pl.program_id(0) + first] > segment, 0.0, 1.0)
    dmem_o[0] = dmem[0] * kept + x_s[rows - 16 :, :]


def weight_product(parts, *refs):
    lefts = refs[:parts]
    rights = refs[parts : 2 * parts]
    out = refs[2 * parts]
    total = None
    for left, right in zip(lefts, rights):
        for i in range(left.shape[0]):
            term = dot_tn(left[i], right[i])
            total = term if total is None else total + term
    out[...] = total.astype(out.dtype)


def whole(array):
    dims = array.shape
    return pl.BlockSpec(dims, lambda *g: (0,) * len(dims), pipeline_mode=pl.Buffered(1))


def per_item(dims, first=0):
    return pl.BlockSpec((1,) + dims, lambda i: (i + first,) + (0,) * len(dims))


def per_segment(dims, segment, first=0):
    return pl.BlockSpec((1, 1) + dims, lambda i: (i + first, segment) + (0,) * len(dims))


def memory_spec(array, first=0):
    shared = array.shape[0] == 1
    return pl.BlockSpec((1, 16, array.shape[2]), lambda i: (0 if shared else i + first, 0, 0))


def out_of(items, dims, dtype):
    return jax.ShapeDtypeStruct((items,) + dims, dtype)


SCALARS = pl.BlockSpec(memory_space=pltpu.SMEM)


def params(mib=60):
    return pltpu.CompilerParams(vmem_limit_bytes=mib << 20)


def launch(body, grid, args, in_specs, out_specs, out_shape, into=None, mib=60, **more):
    into = into or {}
    n_in = len(args)
    aliases = {n_in + k: o for k, o in enumerate(into)}

    def run(*refs):
        body(*refs[:n_in], *refs[n_in + len(into) :])

    return pl.pallas_call(
        run if into else body,
        grid=grid,
        in_specs=list(in_specs) + [pl.BlockSpec(memory_space=pl.ANY)] * len(into),
        out_specs=out_specs,
        out_shape=out_shape,
        input_output_aliases=aliases,
        compiler_params=params(mib),
        **more,
    )(*args, *into.values())


def call_attend_forward(segment, tokens, mem, wq, wk, wv, vec, first=0, many=None, into=None):
    items, _, seg, width = tokens.shape
    many = many or items
    rows = seg + 10
    outs = [((rows, width), BF16)] * 4 + [((HEADS, rows, rows), BF16), ((rows, width), BF16), ((rows, width), F32)]
    return launch(
        attend_forward,
        (many,),
        (tokens, mem, wq, wk, wv, vec),
        [per_segment((seg, width), segment, first), memory_spec(mem, first)] + [whole(w) for w in (wq, wk, wv, vec)],
        [per_item(d, first) for d, t in outs],
        [out_of(items, d, t) for d, t in outs],
        into=dict(enumerate(into)) if into else None,
        cost_estimate=pl.CostEstimate(flops=many * 2 * rows * (3 * width * width + 8 * rows * width), bytes_accessed=many * rows * (width * 14 + HEADS * rows * 2), transcendentals=0),
        name="attend_forward",
    )


def call_feed_forward(segment, count, tokens, mem, o, wo, wup, wdown, vec, bup, into=None):
    items, segments, seg, width = tokens.shape
    rows = o.shape[1]
    ff = wup.shape[1]
    outs = [
        ((16, width), F32), ((rows, width), BF16), ((rows, 128), F32), ((rows, width), BF16),
        ((rows, ff), BF16), ((rows, ff), BF16), ((rows, width), BF16), ((rows, 128), F32),
    ]
    fixed = (wo, wup, wdown, vec, bup)

    def body(*refs):
        feed_forward(segment, 768, *refs)

    return pl_scratch(
        body, (items,), (count, tokens, mem, o) + fixed,
        [SCALARS, per_segment((seg, width), segment), memory_spec(mem), per_item((rows, width))] + [whole(w) for w in fixed],
        [per_segment((seg, width), segment)] + [per_item(d) for d, t in outs],
        [out_of(items, (segments, seg, width), BF16)] + [out_of(items, d, t) for d, t in outs],
        [pltpu.VMEM((rows, width), F32)],
        into={0: into} if into is not None else None,
        cost_estimate=pl.CostEstimate(flops=items * 2 * rows * width * (width + 2 * ff), bytes_accessed=items * rows * (width * 14 + ff * 4), transcendentals=0),
        name="feed_forward",
    )


def pl_scratch(body, grid, args, in_specs, out_specs, out_shape, scratch, into=None, **more):
    return launch(body, grid, args, in_specs, out_specs, out_shape, into=into, scratch_shapes=scratch, **more)


def call_feed_backward(segment, count, cot, dmem, xh2, sc2, gp, xh1, sc1, wup, wdown, vec):
    items, _, seg, width = cot.shape
    rows = xh2.shape[1]
    ff = wup.shape[1]
    outs = [((rows, width), BF16), ((rows, ff), BF16), ((rows, width), F32), ((rows, width), BF16), ((8, width), F32), ((1, ff), F32)]
    fixed = (wup, wdown, vec)

    def body(*refs):
        feed_backward(segment, 768, *refs)

    return pl_scratch(
        body, (items,), (count, cot, dmem, xh2, sc2, gp, xh1, sc1) + fixed,
        [SCALARS, per_segment((seg, width), segment)] + [per_item(a.shape[1:]) for a in (dmem, xh2, sc2, gp, xh1, sc1)] + [whole(w) for w in fixed],
        [per_item(d) for d, t in outs],
        [out_of(items, d, t) for d, t in outs],
        [pltpu.VMEM((rows, width), F32)],
        cost_estimate=pl.CostEstimate(flops=items * 4 * rows * width * ff, bytes_accessed=items * rows * (width * 14 + ff * 4), transcendentals=0),
        name="feed_backward",
    )


def call_attend_backward(segment, segments, seg, count, dmem, dr, db, q, k, v, e, o, li, wo, wq, wk, wv, first=0, many=None, into=None):
    items, rows, width = q.shape
    many = many or items
    outs = [((16, width), F32)] + [((rows, width), BF16)] * 3 + [((8, width), F32)]
    fixed = (wo, wq, wk, wv)

    def body(*refs):
        attend_backward(segment, first, *refs)

    return pl_scratch(
        body, (many,), (count, dmem, dr, db, q, k, v, e, o, li) + fixed,
        [SCALARS] + [per_item(a.shape[1:], first) for a in (dmem, dr, db, q, k, v, e, o, li)] + [whole(w) for w in fixed],
        [per_segment((seg, width), segment, first)] + [per_item(d, first) for d, t in outs],
        [out_of(items, (segments, seg, width), BF16)] + [out_of(items, d, t) for d, t in outs],
        [pltpu.VMEM((rows, width), BF16), pltpu.VMEM((rows, width), F32)],
        into=into,
        cost_estimate=pl.CostEstimate(flops=many * 2 * rows * width * (4 * width + 16 * rows), bytes_accessed=many * rows * (width * 24 + HEADS * rows * 2), transcendentals=0),
        name="attend_backward",
    )


def call_weight_product(lefts, rights, step_left, step_right, dtype):
    parts = len(lefts)
    items, rows, n_left = lefts[0].shape
    n_right = rights[0].shape[2]
    left_spec = pl.BlockSpec((items, rows, step_left), lambda i, j: (0, 0, i))
    right_spec = pl.BlockSpec((items, rows, step_right), lambda i, j: (0, 0, j))
    return pl.pallas_call(
        functools.partial(weight_product, parts),
        grid=(n_left // step_left, n_right // step_right),
        in_specs=[left_spec] * parts + [right_spec] * parts,
        out_specs=pl.BlockSpec((step_left, step_right), lambda i, j: (i, j)),
        out_shape=jax.ShapeDtypeStruct((n_left, n_right), dtype),
        compiler_params=params(),
        cost_estimate=pl.CostEstimate(flops=2 * parts * items * rows * n_left * n_right, bytes_accessed=2 * parts * items * rows * (n_left + n_right), transcendentals=0),
        name="weight_product",
    )(*lefts, *rights)


AXES = ("dp", "shard")
UNIT = 24


def spot(z, y, c, x):
    return ((z * 2 + y) * 2 + c) * 2 + x


def swap(array, dz, dy, dc, dx):
    pairs = [
        (spot(z, y, c, x), spot(z ^ dz, y ^ dy, c ^ dc, x ^ dx))
        for z in range(4)
        for y in range(2)
        for c in range(2)
        for x in range(2)
    ]
    return lax.ppermute(array, AXES, pairs)


def coordinates():
    dp = lax.axis_index("dp")
    return jnp.stack([dp // 4, dp // 2 % 2, dp % 2, lax.axis_index("shard")]).astype(jnp.int32)


def join(*parts):
    return jnp.concatenate(parts, axis=0)


def after(array, *others):
    return lax.optimization_barrier((array,) + others)[0]


def gather_z(unit):
    one, two, three = swap(unit, 1, 0, 0, 0), swap(unit, 2, 0, 0, 0), swap(unit, 3, 0, 0, 0)
    return jnp.stack([unit, one]), jnp.stack([two, three])


def gather_near(a, b):
    return join(a, swap(a, 0, 1, 0, 0)), join(b, swap(b, 0, 0, 0, 1))


def gather_far(a, b):
    return (a, swap(a, 0, 0, 0, 1), b, swap(b, 0, 1, 0, 0))


def gather_core(mine):
    return mine + tuple(swap(m, 0, 0, 1, 0) for m in mine)


def add_low(left, right):
    return (left.astype(F32) + right.astype(F32)).astype(BF16)


def reduce_core(keep, send, *gate):
    got = after(swap(send, 0, 0, 1, 0), *gate)
    send_a = add_low(keep[:2, :, 1], got[:2, :, 1])
    send_b = add_low(keep[2:, 1], got[2:, 1])
    return (send_a, send_b), (keep, got)


def reduce_far(sends, held, *gate):
    keep, got = held
    got_a = after(swap(sends[0], 0, 0, 0, 1), *gate)
    got_b = after(swap(sends[1], 0, 1, 0, 0), *gate)
    a = keep[:2, :, 0].astype(F32) + got[:2, :, 0].astype(F32) + got_a.astype(F32)
    b = keep[2:, 0].astype(F32) + got[2:, 0].astype(F32) + got_b.astype(F32)
    return (a[:, 1].astype(BF16), b[:, 1].astype(BF16)), (a[:, 0], b[:, 0])


def reduce_near(sends, held):
    a = held[0] + swap(sends[0], 0, 1, 0, 0).astype(F32)
    b = held[1] + swap(sends[1], 0, 0, 0, 1).astype(F32)
    return (a[1].astype(BF16), b[0].astype(BF16), b[1].astype(BF16)), a[0]


def reduce_z(sends, held, *gate):
    for step, array in enumerate(sends):
        held = held + after(swap(array, step + 1, 0, 0, 0), *gate).astype(F32)
    return held


def unit_pairs(me, bufs, emit):
    mz, my, mc, mx = me[0], me[1], me[2], me[3]
    flip = jnp.broadcast_to(mx, (8, 128)) == 1

    def send(dz, dy, dc, near, far):
        dp = ((mz ^ dz) * 2 + (my ^ dy)) * 2 + (mc ^ dc)
        emit(dp, near, far)

    for dc in range(2):
        a, a_far, b, b_far = bufs[4 * dc : 4 * dc + 4]
        for i in range(2):
            for j in range(2):
                send(j, i, dc, (a, 2 * i + j), (a_far, 2 * i + j))
        for i, buf in enumerate((b, b_far)):
            for j in range(2):
                send(2 + j, i, dc, (buf, j), (buf, 2 + j))


def pack_first(wq, wk, wv, wo, vec, bup, out):
    blocks = [vec[8 * c : 8 * c + 8, :] for c in range(3)] + [jnp.broadcast_to(bup[...], (8, 128))]
    width = out.shape[1]
    tail = jnp.concatenate(blocks + [jnp.zeros((8, width - 512), F32)], axis=1)
    out[...] = jnp.concatenate([w[...].astype(F32) for w in (wq, wk, wv, wo)] + [tail], axis=0).astype(BF16)


def assemble_first(me, *refs):
    bufs, (wq, wk, wv, wo, vec, bup, small) = refs[:8], refs[8:]
    mx = me[3]

    def emit(dp, near, far):
        n = near[0][near[1]].astype(F32)
        f = far[0][far[1]].astype(F32)
        low = jnp.where(mx == 0, n, f)
        high = jnp.where(mx == 0, f, n)
        at = pl.ds(pl.multiple_of(dp * 48, 16), 48)
        for w, ref in enumerate((wq, wk, wv, wo)):
            ref[at, :] = jnp.concatenate(
                [low[UNIT * w : UNIT * (w + 1)], high[UNIT * w : UNIT * (w + 1)]], axis=0
            ).astype(BF16)
        for x, rows in enumerate((low, high)):
            for c in range(4):
                small[dp * 2 + x, 8 * c : 8 * c + 8, :] = rows[4 * UNIT :, 128 * c : 128 * c + 128]

    unit_pairs(me, bufs, emit)
    for idx in range(small.shape[0]):
        vec[0, :, UNIT * idx : UNIT * (idx + 1)] = small[idx, :24, :UNIT]
        bup[:, 4 * UNIT * idx : 4 * UNIT * (idx + 1)] = small[idx, 24:25, : 4 * UNIT]


def assemble_rest(units, wup, wdown):
    count = units.shape[0]
    width = units.shape[3]
    for w in range(4):
        rows = jnp.concatenate([units[i, w].astype(F32) for i in range(count)], axis=0).astype(BF16)
        wup[:, w * width : (w + 1) * width] = rows
    for i in range(0, count):
        rows = jnp.concatenate([units[i, w].astype(F32) for w in range(4, 8)], axis=0)
        wdown[4 * UNIT * i : 4 * UNIT * (i + 1), :] = rows.astype(BF16)


def call_assemble_rest(units, ff):
    devices, blocks, rows, width = units.shape
    step = 8
    return pl.pallas_call(
        assemble_rest,
        grid=(devices // step,),
        in_specs=[pl.BlockSpec((step, blocks, rows, width), lambda i: (i, 0, 0, 0))],
        out_specs=[
            pl.BlockSpec((step * rows, ff), lambda i: (i, 0)),
            pl.BlockSpec((step * rows * 4, width), lambda i: (i, 0)),
        ],
        out_shape=[jax.ShapeDtypeStruct(d, BF16) for d in ((width, ff), (ff, width))],
        compiler_params=params(),
        name="assemble_rest",
    )(units)


def call_pack_first(wq, wk, wv, wo, vec, bup):
    return pl.pallas_call(
        pack_first, out_shape=jax.ShapeDtypeStruct((4 * UNIT + 8, wq.shape[1]), BF16), name="pack_first"
    )(wq, wk, wv, wo, vec, bup)


def call_assemble(body, me, bufs, outs, name, scratch=()):
    vm = pl.BlockSpec(memory_space=pltpu.VMEM)
    return pl.pallas_call(
        body,
        in_specs=[SCALARS] + [vm] * 8,
        out_specs=[vm] * len(outs),
        out_shape=[jax.ShapeDtypeStruct(d, t) for d, t in outs],
        scratch_shapes=list(scratch),
        compiler_params=params(),
        name=name,
    )(me, *bufs)


def emit_units(me, keep, send, value_of):
    mz, my, mc, mx = me[0], me[1], me[2], me[3]
    for core in range(2):

        @pl.when(mc == core)
        def _():
            for z in range(4):
                for y in range(2):
                    for x in range(2):
                        to = (z ^ mz, y ^ my, x ^ mx)
                        keep[to] = value_of(z, y, core, x)
                        send[to] = value_of(z, y, 1 - core, x)


def product_sum(lefts, rights):
    total = None
    for left, right in zip(lefts, rights):
        for i in range(left.shape[0]):
            term = dot_tn(left[i], right[i])
            total = term if total is None else total + term
    return total


def product_up(segments, me, *refs):
    o, db, h, du = (refs[segments * i : segments * (i + 1)] for i in range(4))
    keep, send, acc = refs[4 * segments :]

    @pl.when(pl.program_id(0) == 0)
    def _():
        acc[...] = product_sum(o, db)

    @pl.when(pl.program_id(0) > 0)
    def _():
        acc[...] = product_sum(h, du)

    def value_of(*at):
        idx = spot(*at)
        return acc[UNIT * idx : UNIT * (idx + 1), :].astype(BF16)

    emit_units(me, keep.at[:, :, :, 0], send.at[:, :, :, 0], value_of)


def product_down(segments, me, *refs):
    a, df = refs[:segments], refs[segments : 2 * segments]
    keep, send, acc = refs[2 * segments :]
    tall = 4 * UNIT
    acc[...] = product_sum(a, df)
    my, mc, mx = me[1], me[2], me[3]
    for core in range(2):

        @pl.when(mc == core)
        def _():
            for y in range(2):
                for x in range(2):
                    for ref, c in ((keep, core), (send, 1 - core)):
                        row = ((y * 2 + c) * 2 + x) * tall
                        ref[0, y ^ my, x ^ mx] = acc[row : row + tall, :].astype(BF16)


def product_first(segments, me, *refs):
    vat, vec, vup = (refs[segments * i : segments * (i + 1)] for i in range(3))
    dmem = refs[3 * segments]
    refs = refs[3 * segments + 1 :]
    x, dq, dk, dv = (refs[segments * i : segments * (i + 1)] for i in range(4))
    keep, send, acc, vec_s, bup_s = refs[4 * segments :]
    step = pl.program_id(0)

    for w, right in enumerate((dq, dk, dv)):
        term = product_sum(x, right)

        @pl.when(step == 0)
        def _():
            acc[w] = term

        @pl.when(step > 0)
        def _():
            acc[w] += term

    @pl.when(step == pl.num_programs(0) - 1)
    def _():
        vat_sum = sum(v[...].sum(axis=0) for v in vat)
        vec_sum = sum(v[...].sum(axis=0) for v in vec)
        vec_s[...] = jnp.zeros_like(vec_s)
        vec_s[0:16, :] = dmem[...].sum(axis=0)
        vec_s[0:2, :] = vat_sum[0:2]
        vec_s[2:6, :] = vec_sum[0:4]
        vec_s[16:18, :] = vec_sum[4:6]
        bup_s[...] = jnp.broadcast_to(sum(v[...].sum(axis=0) for v in vup), bup_s.shape)
        width = acc.shape[2]
        blank = jnp.zeros((8, width - 512), F32)

        def window(ref, at):
            low = min(at // 128 * 128, ref.shape[1] - 256)
            two = ref[:, low : low + 256]
            return (two if at == low else pltpu.roll(two, 256 - (at - low), 1))[:, :128]

        def value_of(*at):
            idx = spot(*at)
            rows = [acc[w, UNIT * idx : UNIT * (idx + 1), :] for w in range(3)]
            vectors = window(vec_s, UNIT * idx)
            hidden = window(bup_s, 4 * UNIT * idx)
            tail = jnp.concatenate([vectors[0:8], vectors[8:16], vectors[16:24], hidden, blank], axis=1)
            return jnp.concatenate(rows + [tail], axis=0).astype(BF16)

        emit_units(me, keep, send, value_of)


def call_product_up(me, o, db, h, du):
    segments = len(o)
    items, rows, width = o[0].shape
    ff = du[0].shape[2]
    steps = ff // width
    fixed = [pl.BlockSpec((items, rows, width), lambda j, m: (0, 0, 0), pipeline_mode=pl.Buffered(1))] * (3 * segments)
    moving = [pl.BlockSpec((items, rows, width), lambda j, m: (0, 0, jnp.maximum(j - 1, 0)))] * segments
    dims = (4, 2, 2, steps + 1, UNIT, width)
    out = pl.BlockSpec((4, 2, 2, 1, UNIT, width), lambda j, m: (0, 0, 0, j, 0, 0))
    return pl.pallas_call(
        functools.partial(product_up, segments),
        grid_spec=pltpu.PrefetchScalarGridSpec(
            num_scalar_prefetch=1,
            grid=(steps + 1,),
            in_specs=fixed + moving,
            out_specs=[out, out],
            scratch_shapes=[pltpu.VMEM((width, width), F32)],
        ),
        out_shape=[jax.ShapeDtypeStruct(dims, BF16)] * 2,
        compiler_params=params(),
        cost_estimate=pl.CostEstimate(flops=2 * segments * items * rows * width * (ff + width), bytes_accessed=2 * segments * items * rows * (ff + 3 * width) + 2 * width * (ff + width), transcendentals=0),
        name="product_up",
    )(me, *o, *db, *h, *du)


def call_product_down(me, a, df):
    segments = len(a)
    items, rows, width = df[0].shape
    ff = a[0].shape[2]
    moving = [pl.BlockSpec((items, rows, ff // 4), lambda j, m: (0, 0, j ^ m[0]))] * segments
    fixed = [pl.BlockSpec((items, rows, width), lambda j, m: (0, 0, 0), pipeline_mode=pl.Buffered(1))] * segments
    dims = (4, 2, 2, 4 * UNIT, width)
    out = pl.BlockSpec((1, 2, 2, 4 * UNIT, width), lambda j, m: (j, 0, 0, 0, 0))
    return pl.pallas_call(
        functools.partial(product_down, segments),
        grid_spec=pltpu.PrefetchScalarGridSpec(
            num_scalar_prefetch=1,
            grid=(4,),
            in_specs=moving + fixed,
            out_specs=[out, out],
            scratch_shapes=[pltpu.VMEM((ff // 4, width), F32)],
        ),
        out_shape=[jax.ShapeDtypeStruct(dims, BF16)] * 2,
        compiler_params=params(),
        cost_estimate=pl.CostEstimate(flops=2 * segments * items * rows * width * ff, bytes_accessed=2 * segments * items * rows * (ff + width) + 2 * width * ff, transcendentals=0),
        name="product_down",
    )(me, *a, *df)


def call_product_first(me, vat, vec, vup, dmem, x, dq, dk, dv):
    segments = len(x)
    items, rows, width = x[0].shape
    fixed = (*vat, *vec, *vup, dmem)
    moving = [pl.BlockSpec((1, rows, width), lambda j, m: (j, 0, 0))] * (4 * segments)
    tall = 3 * UNIT + 8
    dims = (4, 2, 2, tall, width)
    out = pl.BlockSpec(dims, lambda j, m: (0,) * 5, pipeline_mode=pl.Buffered(1))
    return pl.pallas_call(
        functools.partial(product_first, segments),
        grid_spec=pltpu.PrefetchScalarGridSpec(
            num_scalar_prefetch=1,
            grid=(items,),
            in_specs=[whole(a) for a in fixed] + moving,
            out_specs=[out, out],
            scratch_shapes=[
                pltpu.VMEM((3, width, width), F32),
                pltpu.VMEM((24, width), F32),
                pltpu.VMEM((8, vup[0].shape[2]), F32),
            ],
        ),
        out_shape=[jax.ShapeDtypeStruct(dims, BF16)] * 2,
        compiler_params=params(),
        cost_estimate=pl.CostEstimate(flops=6 * segments * items * rows * width * width, bytes_accessed=8 * segments * items * rows * width + 6 * width * width, transcendentals=0),
        name="product_first",
    )(me, *fixed, *x, *dq, *dk, *dv)


def shown(array):
    turned = with_layout_constraint(array.transpose(0, 2, 1, 3), Layout(major_to_minor=(0, 1, 2, 3)))
    return lax.optimization_barrier(turned)


def gather_weights(me, shards, *rows):
    mem, wq, wk, wv, wo, wup, wdown, bq, bv, bo, bup, bdown, g1, s1, g2, s2 = shards
    width = wq.shape[1]
    ff = wup.shape[1]
    vec = jnp.concatenate([jnp.stack([bq, bv, bo, bdown, g1, s1]), mem.T, jnp.stack([g2, s2])], axis=0)
    vec = jnp.pad(vec, ((0, 6), (0, 128 - UNIT))).astype(F32)
    hidden = jnp.pad(bup[None], ((0, 0), (0, 128 - 4 * UNIT))).astype(F32)
    up_blocks = wup.reshape(UNIT, ff // width, width).transpose(1, 0, 2)
    units = jnp.concatenate([up_blocks, wdown.reshape(4, UNIT, width)], axis=0)
    units = lax.all_gather(units, AXES, axis=0)
    a, b = gather_near(*gather_z(call_pack_first(wq, wk, wv, wo, vec, hidden)))
    rows = tuple(lax.optimization_barrier(after(r.transpose(0, 2, 1, 3), b).transpose(0, 2, 1, 3)) for r in rows)
    far = gather_far(a, b)
    *far, tokens, cotangent = lax.optimization_barrier((*far, *rows))
    first = gather_core(tuple(far))
    square = ((width, width), BF16)
    wq, wk, wv, wo, vec, bup = call_assemble(
        assemble_first, me, first, [square] * 4 + [((1, 24, width), F32), ((1, ff), F32)],
        "assemble_first", [pltpu.VMEM((width // UNIT, 32, 128), F32)],
    )
    return (wq, wk, wv, vec, bup), (wo, units), (tokens, cotangent)


def gather_plain(shards):
    mem, wq, wk, wv, wo, wup, wdown, bq, bv, bo, bup, bdown, g1, s1, g2, s2 = [
        lax.all_gather(a, AXES, axis=0, tiled=True) for a in shards
    ]
    rows = [bq, bv, bo, bdown, g1, s1, mem.T, g2, s2]
    vectors = jnp.concatenate([r.reshape(-1, wq.shape[1]) for r in rows], axis=0).astype(F32)
    vectors = jnp.pad(vectors, ((0, 6), (0, 0)))[None]
    return (wq, wk, wv, vectors, bup.astype(F32)[None, :]), (wo, wup, wdown)


def reduce_plain(pieces, vat, vec, vup, dmem):
    x, o, db, h, du, a, df, dq, dk, dv = pieces
    vat = sum(v.sum(axis=0) for v in vat)
    vec = sum(v.sum(axis=0) for v in vec)
    gq = call_weight_product(x, dq, 768, 256, F32)
    gk = call_weight_product(x, dk, 768, 256, F32)
    gv = call_weight_product(x, dv, 768, 256, F32)
    go = call_weight_product(o, db, 768, 256, F32)
    gup = call_weight_product(h, du, 768, 256, F32)
    gdown = call_weight_product(a, df, 256, 768, F32)
    terms = (dmem.sum(axis=0)[6:16].T, gq, gk, gv, go, gup, gdown, sum(v.sum(axis=(0, 1)) for v in vup))
    terms += (vat[0], vat[1]) + tuple(vec[i] for i in range(6))
    owned = lax.psum_scatter(terms, AXES, scatter_dimension=0, tiled=True)
    mem, gq, gk, gv, go, gup, gdown, bup, bq, bv, bo, bdown, g1, s1, g2, s2 = owned
    return mem, gq, gk, gv, go, gup, gdown, bq, bv, bo, bup, bdown, g1, s1, g2, s2


def local(*args):
    tokens, segment_count = args[:2]
    shards = args[2:18]
    cotangent, memory_cotangent = args[18:]
    items, segments, seg, width = tokens.shape
    pad = 16 - shards[0].shape[1]
    planned = lax.axis_size("dp") == 16 and lax.axis_size("shard") == 2
    me = coordinates()
    gathered = gather_weights(me, shards, tokens, cotangent) if planned else gather_plain(shards)
    (wq, wk, wv, vec, bup), rest = gathered[:2]
    if planned:
        tokens, cotangent = gathered[2]
    mem = vec
    saved = []
    y = None
    for s in range(segments):
        part = call_attend_forward(s, tokens, mem, wq, wk, wv, vec)
        if s == 0:
            if planned:
                rest = (rest[0], *call_assemble_rest(after(rest[1], part[0]), 4 * width))
            wo, wup, wdown = rest
        o = part[5]
        y, mem, *more = call_feed_forward(s, segment_count, tokens, mem, o, wo, wup, wdown, vec, bup, y)
        saved.append((*part, *more))
    memory_final = mem[:, pad:].astype(BF16)
    dmem = jnp.pad(memory_cotangent.astype(F32), ((0, 0), (pad, 0), (0, 0)))
    tg = None
    pieces = [None] * segments
    vecs, vups, vats = [], [], []
    for s in reversed(range(segments)):
        x, q, k, v, e, o, li, xh1, sc1, h, a, gp, xh2, sc2 = saved[s]
        df, du, dr, db, vec_s, vup_s = call_feed_backward(
            s, segment_count, cotangent, dmem, xh2, sc2, gp, xh1, sc1, wup, wdown, vec
        )
        pieces[s] = (x, o, db, h, du, a, df)
        vecs.append(vec_s)
        vups.append(vup_s)
        into = {} if tg is None else {0: tg}
        back = functools.partial(call_attend_backward, s, segments, seg)
        tail = (q, k, v, e, o, li, wo, wq, wk, wv)
        if s == 0 and planned:
            o_all, db_all, h_all, du_all, a_all, df_all = list(zip(*pieces))[1:]
            down = call_weight_product(a_all, df_all, 768, 768, BF16)
            o_all = (after(o_all[0], down),) + tuple(o_all[1:])
            down = lax.psum_scatter(down, AXES, scatter_dimension=0, tiled=True).astype(F32)
            keep_up, send_up = call_product_up(me, o_all, db_all, h_all, du_all)
            up = reduce_core(keep_up, send_up)
            dr = after(dr, *up[0])
            up = reduce_far(*up)
        tg, dmem, dq, dk, dv, vat_s = back(segment_count, dmem, dr, db, *tail, into=into)
        pieces[s] += (dq, dk, dv)
        vats.append(vat_s)
    pieces = tuple(zip(*pieces))
    if planned:
        x, dq, dk, dv = pieces[0], *pieces[7:]
        x = (after(x[0], *up[0]),) + x[1:]
        keep, send = call_product_first(me, vats, vecs, vups, dmem, x, dq, dk, dv)
        up = reduce_near(*up)
        first = reduce_core(keep, send)
        y = shown(after(y, *first[0]))
        first = reduce_far(*first)
        up = reduce_z(*up, *first[0])
        tg = shown(after(tg, *first[0]))
        sends, held = reduce_near(*first)
        sends, y, tg = lax.optimization_barrier((sends, y, tg))
        first = reduce_z(sends, held)
        y, tg = y.transpose(0, 2, 1, 3), tg.transpose(0, 2, 1, 3)
        gq, gk, gv = [first[UNIT * w : UNIT * (w + 1)] for w in range(3)]
        tail = first[3 * UNIT :]
        per = jnp.concatenate([tail[:, 128 * c : 128 * c + UNIT] for c in range(3)], axis=0)
        bq, bv, bo, bdown, g1, s1 = [per[i] for i in range(6)]
        owned = (
            per[6:16].T, gq, gk, gv, up[0], up[1:].transpose(1, 0, 2).reshape(UNIT, -1), down, bq, bv, bo,
            tail[0, 384 : 384 + 4 * UNIT], bdown, g1, s1, per[16], per[17],
        )
    else:
        owned = reduce_plain(pieces, vats, vecs, vups, dmem)
    return (y, memory_final, tg) + tuple(owned)


def solution(mesh):
    rows = P(("dp", "shard"))
    return jax.shard_map(local, mesh=mesh, in_specs=(rows,) * 20, out_specs=(rows,) * 19, check_vma=False)
```
